128 devices in a mesh: grp: 4 (over z), dev: 32 (over x, y, core).
Axes of the slice: x: 4, y: 4, z: 4, core: 2. Of those that a mesh axis runs over, the one named last changes fastest.
Arguments:
- queries: float32 [16384, 4096], P(('grp', 'dev'))
- passages: float32 [16384, 4096], P(('grp', 'dev'))
- pairs: int32 [128, 8], P('grp'), may hold values from 0 to 127, as said below
- counts: int32 [4, 32], P('grp'), may hold values from 1 to 8, 128 in all within a row
- positives: int32 [16384], P(('grp', 'dev')), may hold values from 0 to 127
Outputs:
- loss: float32 [16384], P(('grp', 'dev'))
- grad_queries: float32 [16384, 4096], P(('grp', 'dev'))
- grad_passages: float32 [16384, 4096], P(('grp', 'dev'))
The draws below stay inside these ranges and needn't reach their ends.
Inputs may be any that keep to these rules, and one draw needn't show every extreme that they name: `pairs`: entries k < c_b of row b name passage blocks anywhere in the whole set; later entries are ignored. A list may name a block twice. The counts of one group sum to exactly 128.
All inputs are finite; a program needn't handle non-finite values.
Results may differ from the reference program's by a relative error of at most 0.0059.
Values may be sent and summed in bfloat16 or wider, within the bound.
No kernel may reach another device: no remote copies, remote signals or barrier semaphores. Data moves between devices by JAX's collectives and lax.ppermute only.
A program may use at most 128 MiB of HBM per device.

```python
import math
import jax
import jax.numpy as jnp
import numpy as np
from jax import lax

D = 4096
BLK = 128
MAXP = 8
MEANP = 4
GROUPS = 4
GROUP_BLOCKS = 32
NQB = 128
NQ = 16384
NP = 16384


def shared_ids(key):
    first = jax.random.randint(jax.random.fold_in(key, 101), (NQB,), 0, NQB)
    rows = jax.random.randint(jax.random.fold_in(key, 102), (NQ,), 0, BLK)
    return (first, rows)


def passage_values(key, amount):
    base = jnp.clip(jax.random.normal(jax.random.fold_in(key, 103), (NP, D), jnp.float32), -6.0, 6.0)
    return amount * base


def draw_passages(key, part):
    values = passage_values(key, 1.5)
    return values


def draw_queries(key, part):
    key = jax.random.fold_in(key, 3)
    noise = jnp.clip(jax.random.normal(key, (NQ, D), jnp.float32), -6.0, 6.0)
    values = 2.0 * noise
    return values


def draw_pairs(key, part):
    first, rows = shared_ids(key)
    key = jax.random.fold_in(key, 1)
    others = jax.random.randint(key, (NQB, MAXP - 1), 0, NQB)
    return jnp.concatenate([first[:, None], others], axis=1)


def draw_positives(key, part):
    first, rows = shared_ids(key)
    return rows


def profile(number_of, total, most, lean):
    portions = [(1 << 20) // math.isqrt(grade ** lean) + 1 for grade in range(2, number_of + 1)]
    spare, holding = total - most - (number_of - 1), [1] * (number_of - 1)
    while spare > 0:
        candidates = [i for i in range(number_of - 1) if holding[i] < most]
        whole, remaining = sum([portions[i] for i in candidates]), spare
        for i in candidates:
            more = min(most - holding[i], max(1, remaining * portions[i] // whole), spare)
            holding[i] = holding[i] + more
            spare = spare - more
    return np.array([most] + holding)


def uneven_parts(stream_key, number_of, total, reach, slope):
    if number_of == 2:
        one = jax.random.randint(stream_key, (), max(1, total - reach), min(reach, total - 1) + 1)
        return jnp.stack([one, total - one])
    tallies = jnp.asarray(profile(number_of, total, reach, slope), jnp.int32)
    pairs = (number_of - 1) // 2
    source_of, receiver = tallies[1:1 + 2 * pairs:2], tallies[2:2 + 2 * pairs:2]
    margin = jnp.minimum(source_of - 1, reach - receiver)
    moved = jax.random.randint(jax.random.fold_in(stream_key, 1), (pairs,), 0, 1 << 20) % (margin + 1)
    tallies = tallies.at[1:1 + 2 * pairs:2].set(source_of - moved).at[2:2 + 2 * pairs:2].set(receiver + moved)
    return tallies[jax.random.permutation(jax.random.fold_in(stream_key, 2), number_of)]


def setup_inputs(seed: int = 0) -> dict:
    splits = jax.random.split(jax.random.key(seed), 6)
    queries = draw_queries(jax.random.fold_in(splits[5], 71), 0)
    passages = draw_passages(jax.random.fold_in(splits[5], 71), 0)
    pairs = draw_pairs(jax.random.fold_in(splits[5], 71), 0)
    counts = jax.vmap(lambda own: uneven_parts(own, GROUP_BLOCKS, GROUP_BLOCKS * MEANP, MAXP, 2))(jax.random.split(splits[3], GROUPS)).reshape((GROUPS, GROUP_BLOCKS)).astype(jnp.int32)
    positives = draw_positives(jax.random.fold_in(splits[5], 71), 0)
    return dict(queries=queries, passages=passages, pairs=pairs, counts=counts, positives=positives)


def reference(queries, passages, pairs, counts, positives):
    nblk = NQB
    qh = lax.optimization_barrier(queries.astype(jnp.bfloat16)).astype(jnp.float32)
    ph = lax.optimization_barrier(passages.astype(jnp.bfloat16)).astype(jnp.float32)
    qb = qh.reshape(nblk, BLK, D)
    pb = ph.reshape(nblk, BLK, D)
    lists = pairs.reshape(nblk, MAXP).astype(jnp.int32)
    lengths = counts.reshape(nblk).astype(jnp.int32)
    posb = positives.reshape(nblk, BLK).astype(jnp.int32)
    scale = D ** -0.5

    def step(grad_p, inputs):
        qblk, ids, count, rows = inputs
        psel = pb[ids]
        scores = jnp.einsum('if,kjf->kij', qblk, psel, precision=lax.Precision.HIGHEST) * scale
        valid = (jnp.arange(MAXP, dtype=jnp.int32) < count)[:, None, None]
        masked = jnp.where(valid, scores, -1e30)
        top = jnp.max(masked, axis=(0, 2))
        total = jnp.sum(jnp.where(valid, jnp.exp(masked - top[None, :, None]), 0.0), axis=(0, 2))
        lse = top + jnp.log(total)
        hit = jnp.arange(BLK, dtype=jnp.int32)[None, :] == rows[:, None]
        positive = jnp.sum(jnp.where(hit, scores[0], 0.0), axis=1)
        first = (jnp.arange(MAXP, dtype=jnp.int32) == 0)[:, None, None] & hit[None]
        prob = jnp.where(valid, jnp.exp(masked - lse[None, :, None]), 0.0)
        weights = lax.optimization_barrier((prob - first.astype(prob.dtype)).astype(jnp.bfloat16)).astype(jnp.float32)
        grad_q = jnp.einsum('kij,kjf->if', weights, psel, precision=lax.Precision.HIGHEST)
        terms = jnp.einsum('kij,if->kjf', weights, qblk, precision=lax.Precision.HIGHEST)
        grad_p = grad_p.at[ids].add(terms)
        return grad_p, (lse - positive, grad_q)

    start = jnp.zeros((nblk, BLK, D), jnp.float32)
    grad_p, (loss, grad_q) = lax.scan(step, start, (qb, lists, lengths, posb))
    return loss.reshape(NQ), grad_q.reshape(NQ, D), grad_p.reshape(NP, D)
```

```python
import functools

import jax
import jax.numpy as jnp
from jax import lax
from jax.experimental import pallas as pl
from jax.experimental.pallas import tpu as pltpu
from jax.sharding import PartitionSpec as P

BLK = 128
PAIRS = 128
PART = PAIRS // 2
ROWS = 8 * PART
TAIL = 16
STEP = 8
PARTS = 8
MIB = 1024 * 1024
SMEM = pl.BlockSpec(memory_space=pltpu.SMEM)
ANY = pl.BlockSpec(memory_space=pl.ANY)
VMEM = pl.BlockSpec(memory_space=pltpu.VMEM)


def params(limit, moved, flops=0):
    cost = pl.CostEstimate(flops=flops, bytes_accessed=moved, transcendentals=0)
    limit = pltpu.CompilerParams(vmem_limit_bytes=limit * MIB)
    return dict(compiler_params=limit, cost_estimate=cost)


def run_copies(copies):
    for copy in copies:
        copy.start()
    for copy in copies:
        copy.wait()


def pack_kernel(x, *refs):
    *given, out, xv, outv, marks, sems = refs
    width = x.shape[1]
    number = outv.shape[0] // PARTS
    loads, stores = [], []
    for n in range(PARTS):
        cols = slice(n * width // PARTS, (n + 1) * width // PARTS)
        loads.append(pltpu.make_async_copy(x.at[:, cols], xv.at[:, cols], sems.at[n]))
        part = slice(n * number, (n + 1) * number)
        stores.append(pltpu.make_async_copy(outv.at[part], out.at[part], sems.at[PARTS + n]))
    for copy in loads:
        copy.start()
    if given:
        run_copies([pltpu.make_async_copy(given[0], marks, sems.at[2 * PARTS])])
        tile = jnp.broadcast_to(marks[...].astype(jnp.float32), (16, 128)).astype(jnp.bfloat16)
    for n in range(PARTS):
        loads[n].wait()
        for m in range(n * number, (n + 1) * number):
            outv[m, 0:BLK, :] = xv[:, 128 * m : 128 * m + 128].astype(jnp.bfloat16)
            if given:
                outv[m, BLK:, :] = tile
        stores[n].start()
    for copy in stores:
        copy.wait()


def by_features(x, pos=None):
    width = x.shape[1]
    shape = (width // 128, BLK + (0 if pos is None else 16), 128)
    given = (x,) if pos is None else (x, pos)
    return pl.pallas_call(
        pack_kernel,
        in_specs=[ANY] * len(given),
        out_specs=ANY,
        out_shape=jax.ShapeDtypeStruct(shape, jnp.bfloat16),
        scratch_shapes=[
            pltpu.VMEM(x.shape, x.dtype),
            pltpu.VMEM(shape, jnp.bfloat16),
            pltpu.VMEM((1, BLK), jnp.int32),
            pltpu.SemaphoreType.DMA((2 * PARTS + 1,)),
        ],
        **params(56 if pos is None else 5, 5 * MIB),
        name="pack",
    )(*given)


def unpack_kernel(x, out, xv, outv, sems):
    number = x.shape[0] // PARTS
    loads, stores = [], []
    for n in range(PARTS):
        part = slice(n * number, (n + 1) * number)
        loads.append(pltpu.make_async_copy(x.at[part], xv.at[part], sems.at[n]))
        cols = slice(n * number * 128, (n + 1) * number * 128)
        stores.append(pltpu.make_async_copy(outv.at[:, cols], out.at[:, cols], sems.at[PARTS + n]))
    for copy in loads:
        copy.start()
    for n in range(PARTS):
        loads[n].wait()
        for m in range(n * number, (n + 1) * number):
            outv[:, 128 * m : 128 * m + 128] = xv[m].astype(jnp.float32)
        stores[n].start()
    for copy in stores:
        copy.wait()


def by_rows(x):
    number = x.shape[0]
    return pl.pallas_call(
        unpack_kernel,
        in_specs=[ANY],
        out_specs=ANY,
        out_shape=jax.ShapeDtypeStruct((BLK, number * 128), jnp.float32),
        scratch_shapes=[
            pltpu.VMEM(x.shape, x.dtype),
            pltpu.VMEM((BLK, number * 128), jnp.float32),
            pltpu.SemaphoreType.DMA((2 * PARTS,)),
        ],
        **params(5, 8 * MIB),
        name="unpack",
    )(x)


PIECES = ((0, 32), (32, 16), (48, 16), (64, 16), (80, 16), (96, 16), (112, 16))
GIVEN = ((0, 0, 0, 32), (1, 0, 32, 16), (1, 16, 112, 16), (1, 32, 64, 32), (2, 0, 48, 16), (3, 0, 96, 16))


def chip_at(at, core, lead, other):
    rx = jnp.where(core == 0, lead, other)
    ry = jnp.where(core == 0, other, lead)
    return ((at[1] + rx) % 4) * 4 + (at[2] + ry) % 4


def score_kernel(ids, own, at, *refs):
    q, pieces, given, outs = refs[:2], refs[2:9], refs[9:13], refs[13:20]
    qv, pv, sv, sems = refs[20:]
    core = at[0]
    moves = [(q[n].at[:, 0:BLK, :], qv.at[n]) for n in range(2)]
    moves += [(pieces[n], pv.at[0, first : first + size]) for n, (first, size) in enumerate(PIECES)]
    for n, begin, first, size in GIVEN:
        moves.append((given[n].at[begin : begin + size], pv.at[1, first : first + size]))
    run_copies([pltpu.make_async_copy(*move, sems.at[n]) for n, move in enumerate(moves)])

    stores = []
    for half in range(2):

        @pl.loop(0, PART // 2 // STEP)
        def _(step):
            for u in range(STEP):
                n = half * PART // 2 + step * STEP + u
                t = PART * core + n
                left = jnp.concatenate([qv[0, own[t]], qv[1, own[t]]], axis=1)
                right = jnp.concatenate([pv[0, ids[t]], pv[1, ids[t]]], axis=1)
                tile = lax.dot_general(
                    left, right, (((1,), (1,)), ((), ())), preferred_element_type=jnp.float32
                )
                where = pl.ds(pl.multiple_of(8 * n, 8), 8)
                sv[:, where, :] = tile.reshape(BLK // 8, 8, 128)

        rows = slice(half * ROWS // 2, (half + 1) * ROWS // 2)
        for lead in (2, 1, 3, 0):
            for other in range(4):
                if lead == 0:
                    target = outs[6].at[other, rows, :]
                else:
                    target = outs[2 * lead - 2 + other // 2].at[other % 2, rows, :]
                source = sv.at[chip_at(at, core, lead, other), rows, :]
                sem = sems.at[15 + 16 * half + 4 * lead + other]
                stores.append(pltpu.make_async_copy(source, target, sem))
                stores[-1].start()
    for copy in stores:
        copy.wait()


def partial_scores(ids, own, at, q, pieces, given):
    nblk = q[0].shape[0]
    shapes = [(2, ROWS, 128)] * 6 + [(4, ROWS, 128)]
    return pl.pallas_call(
        score_kernel,
        in_specs=[SMEM] * 3 + [ANY] * 13,
        out_specs=[ANY] * 7,
        out_shape=[jax.ShapeDtypeStruct(s, jnp.float32) for s in shapes],
        scratch_shapes=[
            pltpu.VMEM((2, nblk, BLK, 128), jnp.bfloat16),
            pltpu.VMEM((2, 4 * nblk, BLK, 128), jnp.bfloat16),
            pltpu.VMEM((BLK // 8, ROWS, 128), jnp.float32),
            pltpu.SemaphoreType.DMA((47,)),
        ],
        **params(17, 32 * MIB),
        name="partial_scores",
    )(ids, own, at, *q, *pieces, *given)


def softmax_kernel(at, *refs, scale):
    terms, lists, q, out, xv, listv, markv, sems = refs[:2], *refs[2:]
    loads = [
        pltpu.make_async_copy(terms[n], xv.at[ROWS * n : ROWS * n + ROWS, :], sems.at[n])
        for n in range(2)
    ]
    loads.append(pltpu.make_async_copy(lists, listv, sems.at[2]))
    loads.append(pltpu.make_async_copy(q.at[:, BLK:, :], markv, sems.at[3]))
    run_copies(loads)

    core = at[0]
    row = lax.broadcasted_iota(jnp.int32, (2 * ROWS, 1), 0)
    side = row // ROWS
    t = PART * (core + side - 2 * core * side) + (row & (ROWS - 1)) // 8
    r = row & 7
    lane = lax.broadcasted_iota(jnp.int32, (2 * ROWS, 128), 1)
    own = jnp.sum((listv[0:1, :] <= t).astype(jnp.int32), axis=1, keepdims=True)
    key = own * 8 + r

    x = xv[...] * scale
    high = jnp.max(x, axis=1, keepdims=True)
    part = jnp.sum(jnp.exp(x - high), axis=1, keepdims=True)
    lines = jnp.where(lane == 0, high, jnp.where(lane == 1, part, key.astype(jnp.float32))).T
    high, part, keys = lines[0:1], lines[1:2], lines[2:3]

    x, t, r, lane, own, key = [v[:ROWS] for v in (x, t, r, lane, own, key)]
    same = key.astype(jnp.float32) == keys
    top = jnp.max(jnp.where(same, high, -jnp.inf), axis=1, keepdims=True)
    total = jnp.where(same, part * jnp.exp(high - top), 0.0)
    lse = top + jnp.log(jnp.sum(total, axis=1, keepdims=True))

    block = lane == own
    first = t == jnp.sum(jnp.where(block, listv[1:2, :], 0), axis=1, keepdims=True)
    marks = jnp.max(markv[...].astype(jnp.float32), axis=1)
    marks = jnp.concatenate([marks, jnp.zeros((128 - marks.shape[0], 128), jnp.float32)], axis=0)
    listed = jnp.dot(
        block.astype(jnp.bfloat16), marks.astype(jnp.bfloat16), preferred_element_type=jnp.float32
    )
    target = jnp.sum(jnp.where(lane == at[4] * 8 + r, listed, 0.0), axis=1, keepdims=True)
    hit = first & (lane == target.astype(jnp.int32))
    weights = jnp.exp(x - lse) - hit.astype(jnp.float32)
    out[0:ROWS, :] = weights.astype(jnp.bfloat16)

    loss = lse - jnp.sum(jnp.where(hit, x, 0.0), axis=1, keepdims=True)
    line = lax.broadcasted_iota(jnp.int32, (TAIL, 128), 0)
    tail = jnp.zeros((TAIL, 128), jnp.float32)
    for h in range(2):
        here = first & (lane + 128 * h == key)
        rest = jnp.sum(jnp.where(here, loss, 0.0), axis=0, keepdims=True)
        for n in range(3):
            term = rest.astype(jnp.bfloat16).astype(jnp.float32)
            tail = jnp.where(line == 3 * h + n, term, tail)
            rest = rest - term
    out[ROWS:, :] = tail.astype(jnp.bfloat16)


def softmax_weights(at, terms, lists, q, scale):
    return pl.pallas_call(
        functools.partial(softmax_kernel, scale=scale),
        in_specs=[SMEM] + [ANY] * 4,
        out_specs=VMEM,
        out_shape=jax.ShapeDtypeStruct((ROWS + TAIL, 128), jnp.bfloat16),
        scratch_shapes=[
            pltpu.VMEM((2 * ROWS, 128), jnp.float32),
            pltpu.VMEM(lists.shape, jnp.int32),
            pltpu.VMEM((q.shape[0], TAIL, 128), jnp.bfloat16),
            pltpu.SemaphoreType.DMA((4,)),
        ],
        **params(16, 8 * MIB),
        name="softmax_weights",
    )(at, *terms, lists, q)


def grad_kernel(ids, own, at, q, *refs):
    pieces, parts, outs, gq, loss = refs[:7], refs[7:15], refs[15:22], *refs[22:24]
    wv, qv, pv, gq_sum, gp_sum, sems = refs[24:]
    core = at[0]
    moves = [(q.at[:, 0:BLK, :], qv)]
    moves += [(pieces[n], pv.at[first : first + size]) for n, (first, size) in enumerate(PIECES)]
    for n, piece in enumerate(parts):
        side = jnp.where(core == n // 4, 0, 1)
        for lead in range(4):
            chip = chip_at(at, side, lead, (0, 3, 1, 2)[n % 4])
            moves.append((piece.at[lead], wv.at[side, chip]))
    loads = [pltpu.make_async_copy(*move, sems.at[n]) for n, move in enumerate(moves)]
    for copy in loads:
        copy.start()

    @pl.loop(0, gq_sum.shape[0])
    def _(n):
        gq_sum[n] = jnp.zeros((BLK, 128), jnp.float32)
        for m in range(4):
            gp_sum[4 * n + m] = jnp.zeros((BLK, 128), jnp.float32)

    for copy in loads:
        copy.wait()

    for side in range(2):

        @pl.loop(0, PART // STEP)
        def _(step):
            for v in range(STEP // 2):
                where = pl.ds(pl.multiple_of(8 * STEP * step + 16 * v, 16), 16)
                two = wv[side, :, where, :].astype(jnp.float32)
                for o in range(2):
                    t = side * PART + step * STEP + 2 * v + o
                    here, there = own[t], ids[t]
                    tile = two[:, 8 * o : 8 * o + 8, :].reshape(BLK, 128).astype(jnp.bfloat16)
                    gq_sum[here] += jnp.dot(tile, pv[there], preferred_element_type=jnp.float32)
                    gp_sum[there] += lax.dot_general(
                        tile, qv[here], (((0,), (0,)), ((), ())), preferred_element_type=jnp.float32
                    )

    stores = []

    def send(source, target):
        stores.append(pltpu.make_async_copy(source, target, sems.at[len(stores)]))
        stores[-1].start()

    for m in (3, 4, 1, 2, 5, 6, 0):
        first, size = PIECES[m]

        @pl.loop(0, size // 4)
        def _(n):
            for e in range(4):
                pv[first + 4 * n + e] = gp_sum[first + 4 * n + e].astype(jnp.bfloat16)

        send(pv.at[first : first + size], outs[m])

    @pl.loop(0, gq_sum.shape[0] // 4)
    def _(n):
        for e in range(4):
            qv[4 * n + e] = gq_sum[4 * n + e].astype(jnp.bfloat16)

    send(qv, gq)
    tails = wv[0, :, ROWS:, :].astype(jnp.float32) + wv[1, :, ROWS:, :].astype(jnp.float32)
    line = lax.broadcasted_iota(jnp.int32, tails.shape, 1) // 3
    mine = jnp.sum(jnp.where(line == at[3] // 16, tails, 0.0), axis=1)
    loss[...] = pltpu.roll(mine, (128 - 8 * (at[3] % 16)) % 128, 1)
    for copy in stores:
        copy.wait()


def gradients(ids, own, at, q, pieces, parts):
    nblk = q.shape[0]
    shapes = [(size, BLK, 128) for _, size in PIECES] + [(nblk, BLK, 128)]
    return pl.pallas_call(
        grad_kernel,
        in_specs=[SMEM] * 3 + [ANY] * 16,
        out_specs=[ANY] * 8 + [VMEM],
        out_shape=[jax.ShapeDtypeStruct(s, jnp.bfloat16) for s in shapes]
        + [jax.ShapeDtypeStruct((BLK // 8, 128), jnp.float32)],
        scratch_shapes=[
            pltpu.VMEM((2, BLK // 8, ROWS + TAIL, 128), jnp.bfloat16),
            pltpu.VMEM((nblk, BLK, 128), jnp.bfloat16),
            pltpu.VMEM((4 * nblk, BLK, 128), jnp.bfloat16),
            pltpu.VMEM((nblk, BLK, 128), jnp.float32),
            pltpu.VMEM((4 * nblk, BLK, 128), jnp.float32),
            pltpu.SemaphoreType.DMA((40,)),
        ],
        **params(23, 32 * MIB),
        name="gradients",
    )(ids, own, at, q, *pieces, *parts)


def join_kernel(*refs):
    kept, terms, out, keptv, termv, outv, sems = refs[0], refs[1:5], refs[5], *refs[6:]
    half = kept.shape[0] // 2
    loads = [pltpu.make_async_copy(terms[n], termv.at[n], sems.at[n]) for n in range(4)]
    stores = []
    for h in range(2):
        part = slice(half * h, half * h + half)
        loads.append(pltpu.make_async_copy(kept.at[part], keptv.at[part], sems.at[4 + h]))
        stores.append(pltpu.make_async_copy(outv.at[part], out.at[part], sems.at[6 + h]))
    for copy in loads:
        copy.start()
    for h in range(2):
        for n in (4 + h, 2 * h, 2 * h + 1):
            loads[n].wait()

        @pl.loop(0, half)
        def _(n):
            value = keptv[half * h + n].astype(jnp.float32)
            for m in (2 * h, 2 * h + 1):
                value = value + termv[m, n].astype(jnp.float32)
            outv[half * h + n] = value.astype(out.dtype)

        stores[h].start()
    for copy in stores:
        copy.wait()


def join(kept, low, high):
    term = low[0].shape
    return pl.pallas_call(
        join_kernel,
        in_specs=[ANY] * 5,
        out_specs=ANY,
        out_shape=jax.ShapeDtypeStruct(kept.shape, kept.dtype),
        scratch_shapes=[
            pltpu.VMEM(kept.shape, kept.dtype),
            pltpu.VMEM((4,) + term, kept.dtype),
            pltpu.VMEM(kept.shape, kept.dtype),
            pltpu.SemaphoreType.DMA((8,)),
        ],
        **params(5, 8 * MIB),
        name="join",
    )(kept, *low, *high)


def along(axis, delta):
    if axis == "z":
        number = lax.axis_size("grp")
        perm = [(i, (i + delta) % number) for i in range(number)]
        return lambda v: lax.ppermute(v, "grp", perm)

    def target(d):
        x, y, core = d // 8, d // 2 % 4, d % 2
        if axis == "core":
            core = 1 - core
        elif (axis == "first") == (core == 0):
            x = (x + delta) % 4
        else:
            y = (y + delta) % 4
        return x * 8 + y * 2 + core

    perm = [(d, target(d)) for d in range(32)]
    return lambda v: lax.ppermute(v, "dev", perm)


def add(*terms):
    total = terms[0].astype(jnp.float32)
    for term in terms[1:]:
        total = total + term.astype(jnp.float32)
    return total.astype(terms[0].dtype)


def ring_terms(axis, rel1, rel2, rel3):
    up, down = along(axis, 1), along(axis, -1)
    from_below = up(rel2[0])
    from_above = down(rel2[1])
    below1 = up(rel1[1])
    above0 = down(rel3[0])
    below0 = up(add(rel1[0], from_below))
    above1 = down(add(rel3[1], from_above))
    return (below0, above0), (below1, above1)


def scatter_scores(outs):
    halves = ring_terms("first", outs[0:2], outs[2:4], outs[4:6])
    sums = [outs[6][n] + halves[n // 2][0][n % 2] + halves[n // 2][1][n % 2] for n in range(4)]
    got = [along("second", n)(sums[n]) for n in (1, 2, 3)]
    return sums[0] + got[0] + got[1] + got[2]


def gather_weights(v):
    got = {3: along("first", 1)(v), 1: along("first", -1)(v), 2: along("first", 2)(v)}
    near = jnp.stack([v, got[1], got[2], got[3]])
    up, down, flip = along("second", 1), along("second", -1), along("core", 1)
    below, above = up(near), down(near)
    side = [near, below, above, down(above)]
    return side + [flip(w) for w in side]


def per_device(queries, passages, pairs, counts, positives):
    ndev = lax.axis_size("dev")
    ngrp = lax.axis_size("grp")
    width = queries.shape[1]
    maxp = pairs.shape[1]
    me = lax.axis_index("dev")
    z = lax.axis_index("grp")
    chip, core = me // 2, me % 2
    at = jnp.stack([core, chip // 4, chip % 4, me, chip]).astype(jnp.int32)

    def exchange(v):
        return lax.all_to_all(v, "dev", 0, 0, tiled=True)

    up, down, flip = along("z", 1), along("z", -1), along("core", 1)
    p_own = exchange(by_features(passages))
    low, high = p_own[: ndev // 2], p_own[ndev // 2 :]
    above0, below1 = down(low), up(high)
    low, _ = lax.optimization_barrier((low, below1))
    high, _ = lax.optimization_barrier((high, above0))
    far0, far1 = down(above0), up(below1)
    above1, below0 = down(high), up(low)
    pieces = [p_own, above0, above1, far0, far1, below0, below1]
    q_own = exchange(by_features(queries, positives.reshape(1, BLK)))
    early = jnp.concatenate([above0, below1, far0, far1])
    given = [flip(v) for v in (p_own, early, above1, below0)]
    q = [q_own, flip(q_own)]

    group = counts[0]
    block = jnp.arange(ndev, dtype=jnp.int32)
    ends = jnp.sum(jnp.where(block[None, :] <= block[:, None], group[None, :], 0), axis=1)
    starts = ends - group
    t = jnp.arange(PAIRS, dtype=jnp.int32)
    own = jnp.sum((ends[None, :] <= t[:, None]).astype(jnp.int32), axis=1)
    start = jnp.sum(jnp.where(block[None, :] == own[:, None], starts[None, :], 0), axis=1)
    entry = own * maxp + t - start
    slot = jnp.arange(ndev * maxp, dtype=jnp.int32)
    ids = jnp.sum(jnp.where(slot[None, :] == entry[:, None], pairs.reshape(1, -1), 0), axis=1)
    ids = (ids + (ngrp - z) * ndev) % (ngrp * ndev)
    spare = jnp.full((128 - ndev,), 2 * PAIRS, jnp.int32)
    lists = jnp.stack([jnp.concatenate([v, spare]) for v in (ends, starts)] * 4)

    scores = scatter_scores(partial_scores(ids, own, at, q, pieces, given))
    weights = softmax_weights(at, (scores, flip(scores)), lists, q_own, width ** (-0.5))
    *g, gq, lines = gradients(ids, own, at, q_own, pieces, gather_weights(weights))

    low, high = ring_terms("z", g[1:3], g[3:5], g[5:7])
    q_rows = by_rows(exchange(gq))
    p_rows = by_rows(exchange(join(g[0], low, high)))
    return lines[:, 0:8].reshape(BLK), q_rows, p_rows


def solution(mesh):
    placed = (
        P(("grp", "dev"), None),
        P(("grp", "dev"), None),
        P("grp", None),
        P("grp", None),
        P(("grp", "dev")),
    )
    return jax.shard_map(
        per_device,
        mesh=mesh,
        in_specs=placed,
        out_specs=(P(("grp", "dev")), P(("grp", "dev"), None), P(("grp", "dev"), None)),
        check_vma=False,
    )
```

```python
import functools

import jax
import jax.numpy as jnp
from jax import lax
from jax.experimental import pallas as pl
from jax.experimental.pallas import tpu as pltpu
from jax.sharding import PartitionSpec as P

BLK = 128
PAIRS = 128
PART = PAIRS // 2
ROWS = 8 * PART
TAIL = 16
STEP = 8
PARTS = 8
MIB = 1024 * 1024
SMEM = pl.BlockSpec(memory_space=pltpu.SMEM)
ANY = pl.BlockSpec(memory_space=pl.ANY)
VMEM = pl.BlockSpec(memory_space=pltpu.VMEM)


def params(limit, moved, flops=0):
    cost = pl.CostEstimate(flops=flops, bytes_accessed=moved, transcendentals=0)
    limit = pltpu.CompilerParams(vmem_limit_bytes=limit * MIB)
    return dict(compiler_params=limit, cost_estimate=cost)


def run_copies(copies):
    for copy in copies:
        copy.start()
    for copy in copies:
        copy.wait()


def pack_kernel(x, *refs):
    *given, out, xv, outv, marks, sems = refs
    width = x.shape[1]
    number = outv.shape[0] // PARTS
    loads, stores = [], []
    for n in range(PARTS):
        cols = slice(n * width // PARTS, (n + 1) * width // PARTS)
        loads.append(pltpu.make_async_copy(x.at[:, cols], xv.at[:, cols], sems.at[n]))
        part = slice(n * number, (n + 1) * number)
        stores.append(pltpu.make_async_copy(outv.at[part], out.at[part], sems.at[PARTS + n]))
    for copy in loads:
        copy.start()
    if given:
        run_copies([pltpu.make_async_copy(given[0], marks, sems.at[2 * PARTS])])
        tile = jnp.broadcast_to(marks[...].astype(jnp.float32), (16, 128)).astype(jnp.bfloat16)
    for n in range(PARTS):
        loads[n].wait()
        for m in range(n * number, (n + 1) * number):
            outv[m, 0:BLK, :] = xv[:, 128 * m : 128 * m + 128].astype(jnp.bfloat16)
            if given:
                outv[m, BLK:, :] = tile
        stores[n].start()
    for copy in stores:
        copy.wait()


def by_features(x, pos=None):
    width = x.shape[1]
    shape = (width // 128, BLK + (0 if pos is None else 16), 128)
    given = (x,) if pos is None else (x, pos)
    return pl.pallas_call(
        pack_kernel,
        in_specs=[ANY] * len(given),
        out_specs=ANY,
        out_shape=jax.ShapeDtypeStruct(shape, jnp.bfloat16),
        scratch_shapes=[
            pltpu.VMEM(x.shape, x.dtype),
            pltpu.VMEM(shape, jnp.bfloat16),
            pltpu.VMEM((1, BLK), jnp.int32),
            pltpu.SemaphoreType.DMA((2 * PARTS + 1,)),
        ],
        **params(56 if pos is None else 5, 5 * MIB),
        name="pack",
    )(*given)


def unpack_kernel(x, out, xv, outv, sems):
    number = x.shape[0] // PARTS
    loads, stores = [], []
    for n in range(PARTS):
        part = slice(n * number, (n + 1) * number)
        loads.append(pltpu.make_async_copy(x.at[part], xv.at[part], sems.at[n]))
        cols = slice(n * number * 128, (n + 1) * number * 128)
        stores.append(pltpu.make_async_copy(outv.at[:, cols], out.at[:, cols], sems.at[PARTS + n]))
    for copy in loads:
        copy.start()
    for n in range(PARTS):
        loads[n].wait()
        for m in range(n * number, (n + 1) * number):
            outv[:, 128 * m : 128 * m + 128] = xv[m].astype(jnp.float32)
        stores[n].start()
    for copy in stores:
        copy.wait()


def by_rows(x):
    number = x.shape[0]
    return pl.pallas_call(
        unpack_kernel,
        in_specs=[ANY],
        out_specs=ANY,
        out_shape=jax.ShapeDtypeStruct((BLK, number * 128), jnp.float32),
        scratch_shapes=[
            pltpu.VMEM(x.shape, x.dtype),
            pltpu.VMEM((BLK, number * 128), jnp.float32),
            pltpu.SemaphoreType.DMA((2 * PARTS,)),
        ],
        **params(5, 8 * MIB),
        name="unpack",
    )(x)


PIECES = ((0, 32), (32, 16), (48, 16), (64, 16), (80, 16), (96, 16), (112, 16))


def chip_at(at, core, lead, other):
    rx = jnp.where(core == 0, lead, other)
    ry = jnp.where(core == 0, other, lead)
    return ((at[1] + rx) % 4) * 4 + (at[2] + ry) % 4


def score_kernel(ids, own, at, *refs):
    q, pieces, outs = refs[:2], refs[2:16], refs[16:23]
    qv, pv, sv, sems = refs[23:]
    core = at[0]
    moves = [(q[n].at[:, 0:BLK, :], qv.at[n]) for n in range(2)]
    for n, piece in enumerate(pieces):
        first, size = PIECES[n % 7]
        moves.append((piece, pv.at[n // 7, first : first + size]))
    run_copies([pltpu.make_async_copy(*move, sems.at[n]) for n, move in enumerate(moves)])

    stores = []
    for half in range(2):

        @pl.loop(0, PART // 2 // STEP)
        def _(step):
            for u in range(STEP):
                n = half * PART // 2 + step * STEP + u
                t = PART * core + n
                left = jnp.concatenate([qv[0, own[t]], qv[1, own[t]]], axis=1)
                right = jnp.concatenate([pv[0, ids[t]], pv[1, ids[t]]], axis=1)
                tile = lax.dot_general(
                    left, right, (((1,), (1,)), ((), ())), preferred_element_type=jnp.float32
                )
                where = pl.ds(pl.multiple_of(8 * n, 8), 8)
                sv[:, where, :] = tile.reshape(BLK // 8, 8, 128)

        rows = slice(half * ROWS // 2, (half + 1) * ROWS // 2)
        for lead in (2, 1, 3, 0):
            for other in range(4):
                if lead == 0:
                    target = outs[6].at[other, rows, :]
                else:
                    target = outs[2 * lead - 2 + other // 2].at[other % 2, rows, :]
                source = sv.at[chip_at(at, core, lead, other), rows, :]
                sem = sems.at[16 + 16 * half + 4 * lead + other]
                stores.append(pltpu.make_async_copy(source, target, sem))
                stores[-1].start()
    for copy in stores:
        copy.wait()


def partial_scores(ids, own, at, q, pieces, given):
    nblk = q[0].shape[0]
    shapes = [(2, ROWS, 128)] * 6 + [(4, ROWS, 128)]
    return pl.pallas_call(
        score_kernel,
        in_specs=[SMEM] * 3 + [ANY] * 16,
        out_specs=[ANY] * 7,
        out_shape=[jax.ShapeDtypeStruct(s, jnp.float32) for s in shapes],
        scratch_shapes=[
            pltpu.VMEM((2, nblk, BLK, 128), jnp.bfloat16),
            pltpu.VMEM((2, 4 * nblk, BLK, 128), jnp.bfloat16),
            pltpu.VMEM((BLK // 8, ROWS, 128), jnp.float32),
            pltpu.SemaphoreType.DMA((48,)),
        ],
        **params(17, 32 * MIB),
        name="partial_scores",
    )(ids, own, at, *q, *pieces, *given)


def softmax_kernel(at, *refs, scale):
    terms, lists, q, out, xv, listv, markv, sems = refs[:2], *refs[2:]
    loads = [
        pltpu.make_async_copy(terms[n], xv.at[ROWS * n : ROWS * n + ROWS, :], sems.at[n])
        for n in range(2)
    ]
    loads.append(pltpu.make_async_copy(lists, listv, sems.at[2]))
    loads.append(pltpu.make_async_copy(q.at[:, BLK:, :], markv, sems.at[3]))
    run_copies(loads)

    core = at[0]
    row = lax.broadcasted_iota(jnp.int32, (2 * ROWS, 1), 0)
    side = row // ROWS
    t = PART * (core + side - 2 * core * side) + (row & (ROWS - 1)) // 8
    r = row & 7
    lane = lax.broadcasted_iota(jnp.int32, (2 * ROWS, 128), 1)
    own = jnp.sum((listv[0:1, :] <= t).astype(jnp.int32), axis=1, keepdims=True)
    key = own * 8 + r

    x = xv[...] * scale
    high = jnp.max(x, axis=1, keepdims=True)
    part = jnp.sum(jnp.exp(x - high), axis=1, keepdims=True)
    lines = jnp.where(lane == 0, high, jnp.where(lane == 1, part, key.astype(jnp.float32))).T
    high, part, keys = lines[0:1], lines[1:2], lines[2:3]

    x, t, r, lane, own, key = [v[:ROWS] for v in (x, t, r, lane, own, key)]
    same = key.astype(jnp.float32) == keys
    top = jnp.max(jnp.where(same, high, -jnp.inf), axis=1, keepdims=True)
    total = jnp.where(same, part * jnp.exp(high - top), 0.0)
    lse = top + jnp.log(jnp.sum(total, axis=1, keepdims=True))

    block = lane == own
    first = t == jnp.sum(jnp.where(block, listv[1:2, :], 0), axis=1, keepdims=True)
    marks = jnp.max(markv[...].astype(jnp.float32), axis=1)
    marks = jnp.concatenate([marks, jnp.zeros((128 - marks.shape[0], 128), jnp.float32)], axis=0)
    listed = jnp.dot(
        block.astype(jnp.bfloat16), marks.astype(jnp.bfloat16), preferred_element_type=jnp.float32
    )
    target = jnp.sum(jnp.where(lane == at[4] * 8 + r, listed, 0.0), axis=1, keepdims=True)
    hit = first & (lane == target.astype(jnp.int32))
    weights = jnp.exp(x - lse) - hit.astype(jnp.float32)
    out[0:ROWS, :] = weights.astype(jnp.bfloat16)

    loss = lse - jnp.sum(jnp.where(hit, x, 0.0), axis=1, keepdims=True)
    line = lax.broadcasted_iota(jnp.int32, (TAIL, 128), 0)
    tail = jnp.zeros((TAIL, 128), jnp.float32)
    for h in range(2):
        here = first & (lane + 128 * h == key)
        rest = jnp.sum(jnp.where(here, loss, 0.0), axis=0, keepdims=True)
        for n in range(3):
            term = rest.astype(jnp.bfloat16).astype(jnp.float32)
            tail = jnp.where(line == 3 * h + n, term, tail)
            rest = rest - term
    out[ROWS:, :] = tail.astype(jnp.bfloat16)


def softmax_weights(at, terms, lists, q, scale):
    return pl.pallas_call(
        functools.partial(softmax_kernel, scale=scale),
        in_specs=[SMEM] + [ANY] * 4,
        out_specs=VMEM,
        out_shape=jax.ShapeDtypeStruct((ROWS + TAIL, 128), jnp.bfloat16),
        scratch_shapes=[
            pltpu.VMEM((2 * ROWS, 128), jnp.float32),
            pltpu.VMEM(lists.shape, jnp.int32),
            pltpu.VMEM((q.shape[0], TAIL, 128), jnp.bfloat16),
            pltpu.SemaphoreType.DMA((4,)),
        ],
        **params(16, 8 * MIB),
        name="softmax_weights",
    )(at, *terms, lists, q)


def grad_kernel(ids, own, at, q, *refs):
    pieces, parts, outs, gq, loss = refs[:7], refs[7:15], refs[15:22], *refs[22:24]
    wv, qv, pv, gq_sum, gp_sum, sems = refs[24:]
    core = at[0]
    moves = [(q.at[:, 0:BLK, :], qv)]
    moves += [(pieces[n], pv.at[first : first + size]) for n, (first, size) in enumerate(PIECES)]
    for n, piece in enumerate(parts):
        side = jnp.where(core == n // 4, 0, 1)
        for lead in range(4):
            chip = chip_at(at, side, lead, (0, 3, 1, 2)[n % 4])
            moves.append((piece.at[lead], wv.at[side, chip]))
    loads = [pltpu.make_async_copy(*move, sems.at[n]) for n, move in enumerate(moves)]
    for copy in loads:
        copy.start()

    @pl.loop(0, gq_sum.shape[0])
    def _(n):
        gq_sum[n] = jnp.zeros((BLK, 128), jnp.float32)
        for m in range(4):
            gp_sum[4 * n + m] = jnp.zeros((BLK, 128), jnp.float32)

    for n in range(2):
        for copy in loads[24 * n : 24 + 16 * n]:
            copy.wait()
        side = jnp.where(core == n, 0, 1)

        @pl.loop(0, PART // STEP)
        def _(step):
            for v in range(STEP // 2):
                where = pl.ds(pl.multiple_of(8 * STEP * step + 16 * v, 16), 16)
                two = wv[side, :, where, :].astype(jnp.float32)
                for o in range(2):
                    t = side * PART + step * STEP + 2 * v + o
                    here, there = own[t], ids[t]
                    tile = two[:, 8 * o : 8 * o + 8, :].reshape(BLK, 128).astype(jnp.bfloat16)
                    gq_sum[here] += jnp.dot(tile, pv[there], preferred_element_type=jnp.float32)
                    gp_sum[there] += lax.dot_general(
                        tile, qv[here], (((0,), (0,)), ((), ())), preferred_element_type=jnp.float32
                    )

    stores = []

    def send(source, target):
        stores.append(pltpu.make_async_copy(source, target, sems.at[len(stores)]))
        stores[-1].start()

    for m in (3, 4, 1, 2, 5, 6, 0):
        first, size = PIECES[m]

        @pl.loop(0, size // 4)
        def _(n):
            for e in range(4):
                pv[first + 4 * n + e] = gp_sum[first + 4 * n + e].astype(jnp.bfloat16)

        send(pv.at[first : first + size], outs[m])

    @pl.loop(0, gq_sum.shape[0] // 4)
    def _(n):
        for e in range(4):
            qv[4 * n + e] = gq_sum[4 * n + e].astype(jnp.bfloat16)

    send(qv, gq)
    tails = wv[0, :, ROWS:, :].astype(jnp.float32) + wv[1, :, ROWS:, :].astype(jnp.float32)
    line = lax.broadcasted_iota(jnp.int32, tails.shape, 1) // 3
    mine = jnp.sum(jnp.where(line == at[3] // 16, tails, 0.0), axis=1)
    loss[...] = pltpu.roll(mine, (128 - 8 * (at[3] % 16)) % 128, 1)
    for copy in stores:
        copy.wait()


def gradients(ids, own, at, q, pieces, parts):
    nblk = q.shape[0]
    shapes = [(size, BLK, 128) for _, size in PIECES] + [(nblk, BLK, 128)]
    return pl.pallas_call(
        grad_kernel,
        in_specs=[SMEM] * 3 + [ANY] * 16,
        out_specs=[ANY] * 8 + [VMEM],
        out_shape=[jax.ShapeDtypeStruct(s, jnp.bfloat16) for s in shapes]
        + [jax.ShapeDtypeStruct((BLK // 8, 128), jnp.float32)],
        scratch_shapes=[
            pltpu.VMEM((2, BLK // 8, ROWS + TAIL, 128), jnp.bfloat16),
            pltpu.VMEM((nblk, BLK, 128), jnp.bfloat16),
            pltpu.VMEM((4 * nblk, BLK, 128), jnp.bfloat16),
            pltpu.VMEM((nblk, BLK, 128), jnp.float32),
            pltpu.VMEM((4 * nblk, BLK, 128), jnp.float32),
            pltpu.SemaphoreType.DMA((40,)),
        ],
        **params(23, 32 * MIB),
        name="gradients",
    )(ids, own, at, q, *pieces, *parts)


def join_kernel(*refs):
    kept, terms, out, keptv, termv, outv, sems = refs[0], refs[1:5], refs[5], *refs[6:]
    half = kept.shape[0] // 2
    loads = [pltpu.make_async_copy(terms[n], termv.at[n], sems.at[n]) for n in range(4)]
    stores = []
    for h in range(2):
        part = slice(half * h, half * h + half)
        loads.append(pltpu.make_async_copy(kept.at[part], keptv.at[part], sems.at[4 + h]))
        stores.append(pltpu.make_async_copy(outv.at[part], out.at[part], sems.at[6 + h]))
    for copy in loads:
        copy.start()
    for h in range(2):
        for n in (4 + h, 2 * h, 2 * h + 1):
            loads[n].wait()

        @pl.loop(0, half)
        def _(n):
            value = keptv[half * h + n].astype(jnp.float32)
            for m in (2 * h, 2 * h + 1):
                value = value + termv[m, n].astype(jnp.float32)
            outv[half * h + n] = value.astype(out.dtype)

        stores[h].start()
    for copy in stores:
        copy.wait()


def join(kept, low, high):
    term = low[0].shape
    return pl.pallas_call(
        join_kernel,
        in_specs=[ANY] * 5,
        out_specs=ANY,
        out_shape=jax.ShapeDtypeStruct(kept.shape, kept.dtype),
        scratch_shapes=[
            pltpu.VMEM(kept.shape, kept.dtype),
            pltpu.VMEM((4,) + term, kept.dtype),
            pltpu.VMEM(kept.shape, kept.dtype),
            pltpu.SemaphoreType.DMA((8,)),
        ],
        **params(5, 8 * MIB),
        name="join",
    )(kept, *low, *high)


def along(axis, delta):
    if axis == "z":
        number = lax.axis_size("grp")
        perm = [(i, (i + delta) % number) for i in range(number)]
        return lambda v: lax.ppermute(v, "grp", perm)

    def target(d):
        x, y, core = d // 8, d // 2 % 4, d % 2
        if axis == "core":
            core = 1 - core
        elif (axis == "first") == (core == 0):
            x = (x + delta) % 4
        else:
            y = (y + delta) % 4
        return x * 8 + y * 2 + core

    perm = [(d, target(d)) for d in range(32)]
    return lambda v: lax.ppermute(v, "dev", perm)


def add(*terms):
    total = terms[0].astype(jnp.float32)
    for term in terms[1:]:
        total = total + term.astype(jnp.float32)
    return total.astype(terms[0].dtype)


def ring_terms(axis, rel1, rel2, rel3):
    up, down = along(axis, 1), along(axis, -1)
    from_below = up(rel2[0])
    from_above = down(rel2[1])
    below1 = up(rel1[1])
    above0 = down(rel3[0])
    below0 = up(add(rel1[0], from_below))
    above1 = down(add(rel3[1], from_above))
    return (below0, above0), (below1, above1)


def scatter_scores(outs):
    halves = ring_terms("first", outs[0:2], outs[2:4], outs[4:6])
    sums = [outs[6][n] + halves[n // 2][0][n % 2] + halves[n // 2][1][n % 2] for n in range(4)]
    got = [along("second", n)(sums[n]) for n in (1, 2, 3)]
    return sums[0] + got[0] + got[1] + got[2]


def gather_weights(v):
    got = {3: along("first", 1)(v), 1: along("first", -1)(v), 2: along("first", 2)(v)}
    near = jnp.stack([v, got[1], got[2], got[3]])
    up, down, flip = along("second", 1), along("second", -1), along("core", 1)
    below, above = up(near), down(near)
    side = [near, below, above, down(above)]
    return side + [flip(w) for w in side]


def per_device(queries, passages, pairs, counts, positives):
    ndev = lax.axis_size("dev")
    ngrp = lax.axis_size("grp")
    width = queries.shape[1]
    maxp = pairs.shape[1]
    me = lax.axis_index("dev")
    z = lax.axis_index("grp")
    chip, core = me // 2, me % 2
    at = jnp.stack([core, chip // 4, chip % 4, me, chip]).astype(jnp.int32)

    def exchange(v):
        return lax.all_to_all(v, "dev", 0, 0, tiled=True)

    up, down, flip = along("z", 1), along("z", -1), along("core", 1)
    p_own = exchange(by_features(passages))
    low, high = p_own[: ndev // 2], p_own[ndev // 2 :]
    above0, below1, given0 = down(low), up(high), flip(p_own)
    low, high, *_ = lax.optimization_barrier((low, high, above0, below1, given0))
    above1, below0, given1, given2 = down(high), up(low), flip(above0), flip(below1)
    last0, last1, *_ = lax.optimization_barrier((above0, below1, above1, below0, given1, given2))
    far0, far1 = down(last0), up(last1)
    pieces = [p_own, above0, above1, far0, far1, below0, below1]
    given = [given0, given1, flip(above1), flip(far0), flip(far1), flip(below0), given2]
    q_own = exchange(by_features(queries, positives.reshape(1, BLK)))
    q = [q_own, flip(q_own)]

    group = counts[0]
    block = jnp.arange(ndev, dtype=jnp.int32)
    ends = jnp.sum(jnp.where(block[None, :] <= block[:, None], group[None, :], 0), axis=1)
    starts = ends - group
    t = jnp.arange(PAIRS, dtype=jnp.int32)
    own = jnp.sum((ends[None, :] <= t[:, None]).astype(jnp.int32), axis=1)
    start = jnp.sum(jnp.where(block[None, :] == own[:, None], starts[None, :], 0), axis=1)
    entry = own * maxp + t - start
    slot = jnp.arange(ndev * maxp, dtype=jnp.int32)
    ids = jnp.sum(jnp.where(slot[None, :] == entry[:, None], pairs.reshape(1, -1), 0), axis=1)
    ids = (ids + (ngrp - z) * ndev) % (ngrp * ndev)
    spare = jnp.full((128 - ndev,), 2 * PAIRS, jnp.int32)
    lists = jnp.stack([jnp.concatenate([v, spare]) for v in (ends, starts)] * 4)

    scores = scatter_scores(partial_scores(ids, own, at, q, pieces, given))
    weights = softmax_weights(at, (scores, flip(scores)), lists, q_own, width ** (-0.5))
    *g, gq, lines = gradients(ids, own, at, q_own, pieces, gather_weights(weights))

    low, high = ring_terms("z", g[1:3], g[3:5], g[5:7])
    q_rows = by_rows(exchange(gq))
    p_rows = by_rows(exchange(join(g[0], low, high)))
    return lines[:, 0:8].reshape(BLK), q_rows, p_rows


def solution(mesh):
    placed = (
        P(("grp", "dev"), None),
        P(("grp", "dev"), None),
        P("grp", None),
        P("grp", None),
        P(("grp", "dev")),
    )
    return jax.shard_map(
        per_device,
        mesh=mesh,
        in_specs=placed,
        out_specs=(P(("grp", "dev")), P(("grp", "dev"), None), P(("grp", "dev"), None)),
        check_vma=False,
    )
```

```python
import functools

import jax
import jax.numpy as jnp
from jax import lax
from jax.experimental import pallas as pl
from jax.experimental.pallas import tpu as pltpu
from jax.sharding import PartitionSpec as P

BLK = 128
PAIRS = 128
PART = PAIRS // 2
ROWS = 8 * PART
TAIL = 16
STEP = 8
PARTS = 8
MIB = 1024 * 1024
SMEM = pl.BlockSpec(memory_space=pltpu.SMEM)
ANY = pl.BlockSpec(memory_space=pl.ANY)
VMEM = pl.BlockSpec(memory_space=pltpu.VMEM)


def params(limit, moved, flops=0):
    cost = pl.CostEstimate(flops=flops, bytes_accessed=moved, transcendentals=0)
    limit = pltpu.CompilerParams(vmem_limit_bytes=limit * MIB)
    return dict(compiler_params=limit, cost_estimate=cost)


def run_copies(copies):
    for copy in copies:
        copy.start()
    for copy in copies:
        copy.wait()


def pack_kernel(x, *refs):
    *given, out, xv, outv, marks, sems = refs
    width = x.shape[1]
    number = outv.shape[0] // PARTS
    loads, stores = [], []
    for n in range(PARTS):
        cols = slice(n * width // PARTS, (n + 1) * width // PARTS)
        loads.append(pltpu.make_async_copy(x.at[:, cols], xv.at[:, cols], sems.at[n]))
        part = slice(n * number, (n + 1) * number)
        stores.append(pltpu.make_async_copy(outv.at[part], out.at[part], sems.at[PARTS + n]))
    for copy in loads:
        copy.start()
    if given:
        run_copies([pltpu.make_async_copy(given[0], marks, sems.at[2 * PARTS])])
        tile = jnp.broadcast_to(marks[...].astype(jnp.float32), (16, 128)).astype(jnp.bfloat16)
    for n in range(PARTS):
        loads[n].wait()
        for m in range(n * number, (n + 1) * number):
            outv[m, 0:BLK, :] = xv[:, 128 * m : 128 * m + 128].astype(jnp.bfloat16)
            if given:
                outv[m, BLK:, :] = tile
        stores[n].start()
    for copy in stores:
        copy.wait()


def by_features(x, pos=None):
    width = x.shape[1]
    shape = (width // 128, BLK + (0 if pos is None else 16), 128)
    given = (x,) if pos is None else (x, pos)
    return pl.pallas_call(
        pack_kernel,
        in_specs=[ANY] * len(given),
        out_specs=ANY,
        out_shape=jax.ShapeDtypeStruct(shape, jnp.bfloat16),
        scratch_shapes=[
            pltpu.VMEM(x.shape, x.dtype),
            pltpu.VMEM(shape, jnp.bfloat16),
            pltpu.VMEM((1, BLK), jnp.int32),
            pltpu.SemaphoreType.DMA((2 * PARTS + 1,)),
        ],
        **params(56 if pos is None else 5, 5 * MIB),
        name="pack",
    )(*given)


def unpack_kernel(x, out, xv, outv, sems):
    number = x.shape[0] // PARTS
    loads, stores = [], []
    for n in range(PARTS):
        part = slice(n * number, (n + 1) * number)
        loads.append(pltpu.make_async_copy(x.at[part], xv.at[part], sems.at[n]))
        cols = slice(n * number * 128, (n + 1) * number * 128)
        stores.append(pltpu.make_async_copy(outv.at[:, cols], out.at[:, cols], sems.at[PARTS + n]))
    for copy in loads:
        copy.start()
    for n in range(PARTS):
        loads[n].wait()
        for m in range(n * number, (n + 1) * number):
            outv[:, 128 * m : 128 * m + 128] = xv[m].astype(jnp.float32)
        stores[n].start()
    for copy in stores:
        copy.wait()


def by_rows(x):
    number = x.shape[0]
    return pl.pallas_call(
        unpack_kernel,
        in_specs=[ANY],
        out_specs=ANY,
        out_shape=jax.ShapeDtypeStruct((BLK, number * 128), jnp.float32),
        scratch_shapes=[
            pltpu.VMEM(x.shape, x.dtype),
            pltpu.VMEM((BLK, number * 128), jnp.float32),
            pltpu.SemaphoreType.DMA((2 * PARTS,)),
        ],
        **params(5, 8 * MIB),
        name="unpack",
    )(x)


PIECES = ((0, 32), (32, 16), (48, 16), (64, 16), (80, 16), (96, 16), (112, 16))


def place_kernel(*refs, spots):
    *pieces, out, sems = refs
    pieces = pieces[len(pieces) - len(spots) :]
    run_copies(
        [
            pltpu.make_async_copy(piece, out.at[first : first + piece.shape[0]], sems.at[n])
            for n, (piece, first) in enumerate(zip(pieces, spots))
        ]
    )


def place(whole, pieces, spots):
    given = tuple(pieces) if whole is None else (whole, *pieces)
    shape = (4 * 32,) + pieces[0].shape[1:]
    return pl.pallas_call(
        functools.partial(place_kernel, spots=spots),
        in_specs=[ANY] * len(given),
        out_specs=ANY,
        out_shape=jax.ShapeDtypeStruct(shape, pieces[0].dtype),
        scratch_shapes=[pltpu.SemaphoreType.DMA((len(pieces),))],
        input_output_aliases={} if whole is None else {0: 0},
        **params(1, 4 * MIB),
        name="place",
    )(*given)


def chip_at(at, core, lead, other):
    rx = jnp.where(core == 0, lead, other)
    ry = jnp.where(core == 0, other, lead)
    return ((at[1] + rx) % 4) * 4 + (at[2] + ry) % 4


def score_kernel(ids, own, at, q_own, q_sib, p_own, p_sib, *refs):
    outs, sv = refs[:7], refs[7]
    core = at[0]
    spots = [
        (lead, other, chip_at(at, core, lead, other)) for lead in range(4) for other in range(4)
    ]

    @pl.loop(0, PART // STEP)
    def _(step):
        for u in range(STEP):
            n = step * STEP + u
            here, there = own[PART * core + n], ids[PART * core + n]
            left = jnp.concatenate([q_own[here, 0:BLK, :], q_sib[here, 0:BLK, :]], axis=1)
            right = jnp.concatenate([p_own[there], p_sib[there]], axis=1)
            tile = lax.dot_general(
                left, right, (((1,), (1,)), ((), ())), preferred_element_type=jnp.float32
            )
            sv[u] = tile.reshape(BLK // 8, 8, 128)
        for u in range(STEP):
            where = pl.ds(pl.multiple_of(8 * (step * STEP + u), 8), 8)
            for lead, other, chip in spots:
                if lead == 0:
                    outs[6][other, where, :] = sv[u, chip]
                else:
                    outs[2 * lead - 2 + other // 2][other % 2, where, :] = sv[u, chip]


def partial_scores(ids, own, at, q, p):
    shapes = [(2, ROWS, 128)] * 6 + [(4, ROWS, 128)]
    return pl.pallas_call(
        score_kernel,
        in_specs=[SMEM] * 3 + [VMEM] * 4,
        out_specs=[VMEM] * 7,
        out_shape=[jax.ShapeDtypeStruct(s, jnp.float32) for s in shapes],
        scratch_shapes=[pltpu.VMEM((STEP, BLK // 8, 8, 128), jnp.float32)],
        **params(17, 20 * MIB),
        name="partial_scores",
    )(ids, own, at, *q, *p)


def softmax_kernel(at, *refs, scale):
    terms, lists, q, out, xv, listv, markv, sems = refs[:2], *refs[2:]
    loads = [
        pltpu.make_async_copy(terms[n], xv.at[ROWS * n : ROWS * n + ROWS, :], sems.at[n])
        for n in range(2)
    ]
    loads.append(pltpu.make_async_copy(lists, listv, sems.at[2]))
    loads.append(pltpu.make_async_copy(q.at[:, BLK:, :], markv, sems.at[3]))
    run_copies(loads)

    core = at[0]
    row = lax.broadcasted_iota(jnp.int32, (2 * ROWS, 1), 0)
    side = row // ROWS
    t = PART * (core + side - 2 * core * side) + (row & (ROWS - 1)) // 8
    r = row & 7
    lane = lax.broadcasted_iota(jnp.int32, (2 * ROWS, 128), 1)
    own = jnp.sum((listv[0:1, :] <= t).astype(jnp.int32), axis=1, keepdims=True)
    key = own * 8 + r

    x = xv[...] * scale
    high = jnp.max(x, axis=1, keepdims=True)
    part = jnp.sum(jnp.exp(x - high), axis=1, keepdims=True)
    lines = jnp.where(lane == 0, high, jnp.where(lane == 1, part, key.astype(jnp.float32))).T
    high, part, keys = lines[0:1], lines[1:2], lines[2:3]

    x, t, r, lane, own, key = [v[:ROWS] for v in (x, t, r, lane, own, key)]
    same = key.astype(jnp.float32) == keys
    top = jnp.max(jnp.where(same, high, -jnp.inf), axis=1, keepdims=True)
    total = jnp.where(same, part * jnp.exp(high - top), 0.0)
    lse = top + jnp.log(jnp.sum(total, axis=1, keepdims=True))

    block = lane == own
    first = t == jnp.sum(jnp.where(block, listv[1:2, :], 0), axis=1, keepdims=True)
    marks = jnp.max(markv[...].astype(jnp.float32), axis=1)
    marks = jnp.concatenate([marks, jnp.zeros((128 - marks.shape[0], 128), jnp.float32)], axis=0)
    listed = jnp.dot(
        block.astype(jnp.bfloat16), marks.astype(jnp.bfloat16), preferred_element_type=jnp.float32
    )
    target = jnp.sum(jnp.where(lane == at[4] * 8 + r, listed, 0.0), axis=1, keepdims=True)
    hit = first & (lane == target.astype(jnp.int32))
    weights = jnp.exp(x - lse) - hit.astype(jnp.float32)
    out[0:ROWS, :] = weights.astype(jnp.bfloat16)

    loss = lse - jnp.sum(jnp.where(hit, x, 0.0), axis=1, keepdims=True)
    line = lax.broadcasted_iota(jnp.int32, (TAIL, 128), 0)
    tail = jnp.zeros((TAIL, 128), jnp.float32)
    for h in range(2):
        here = first & (lane + 128 * h == key)
        rest = jnp.sum(jnp.where(here, loss, 0.0), axis=0, keepdims=True)
        for n in range(3):
            term = rest.astype(jnp.bfloat16).astype(jnp.float32)
            tail = jnp.where(line == 3 * h + n, term, tail)
            rest = rest - term
    out[ROWS:, :] = tail.astype(jnp.bfloat16)


def softmax_weights(at, terms, lists, q, scale):
    return pl.pallas_call(
        functools.partial(softmax_kernel, scale=scale),
        in_specs=[SMEM] + [ANY] * 4,
        out_specs=VMEM,
        out_shape=jax.ShapeDtypeStruct((ROWS + TAIL, 128), jnp.bfloat16),
        scratch_shapes=[
            pltpu.VMEM((2 * ROWS, 128), jnp.float32),
            pltpu.VMEM(lists.shape, jnp.int32),
            pltpu.VMEM((q.shape[0], TAIL, 128), jnp.bfloat16),
            pltpu.SemaphoreType.DMA((4,)),
        ],
        **params(16, 8 * MIB),
        name="softmax_weights",
    )(at, *terms, lists, q)


def grad_kernel(ids, own, at, q, p, *refs):
    parts, outs, gq, loss = refs[:8], refs[8:15], *refs[15:17]
    wv, gq_sum, gp_sum = refs[17:]
    core = at[0]

    @pl.loop(0, gq_sum.shape[0])
    def _(n):
        gq_sum[n] = jnp.zeros((BLK, 128), jnp.float32)
        for m in range(4):
            gp_sum[4 * n + m] = jnp.zeros((BLK, 128), jnp.float32)

    loss[...] = jnp.zeros(loss.shape, jnp.float32)
    line = lax.broadcasted_iota(jnp.int32, (TAIL, 128), 0) // 3
    mine = line == at[3] // 16
    for n in range(2):
        side = jnp.where(core == n, 0, 1)
        spots = []
        for m in range(4):
            for lead in range(4):
                chip = chip_at(at, side, lead, (0, 3, 1, 2)[m])
                spots.append((4 * n + m, lead, chip))
                tail = parts[4 * n + m][lead, ROWS:, :].astype(jnp.float32)
                loss[pl.ds(chip, 1), :] += jnp.sum(
                    jnp.where(mine, tail, 0.0), axis=0, keepdims=True
                )

        @pl.loop(0, PART // STEP)
        def _(step):
            for v in range(STEP // 2):
                where = pl.ds(pl.multiple_of(8 * STEP * step + 16 * v, 16), 16)
                for m, lead, chip in spots:
                    wv[v, chip] = parts[m][lead, where, :]
                two = wv[v].astype(jnp.float32)
                for o in range(2):
                    t = side * PART + step * STEP + 2 * v + o
                    here, there = own[t], ids[t]
                    tile = two[:, 8 * o : 8 * o + 8, :].reshape(BLK, 128).astype(jnp.bfloat16)
                    gq_sum[here] += jnp.dot(tile, p[there], preferred_element_type=jnp.float32)
                    gp_sum[there] += lax.dot_general(
                        tile,
                        q[here, 0:BLK, :],
                        (((0,), (0,)), ((), ())),
                        preferred_element_type=jnp.float32,
                    )

    @pl.loop(0, 16)
    def _(n):
        for m, (first, size) in enumerate(PIECES):
            for e in range(size // 16):
                outs[m][16 * e + n] = gp_sum[first + 16 * e + n].astype(jnp.bfloat16)
        for e in range(2):
            gq[16 * e + n] = gq_sum[16 * e + n].astype(jnp.bfloat16)

    loss[...] = pltpu.roll(loss[...], (128 - 8 * (at[3] % 16)) % 128, 1)


def gradients(ids, own, at, q, p, parts):
    nblk = q.shape[0]
    shapes = [(size, BLK, 128) for _, size in PIECES] + [(nblk, BLK, 128)]
    return pl.pallas_call(
        grad_kernel,
        in_specs=[SMEM] * 3 + [VMEM] * 10,
        out_specs=[VMEM] * 9,
        out_shape=[jax.ShapeDtypeStruct(s, jnp.bfloat16) for s in shapes]
        + [jax.ShapeDtypeStruct((BLK // 8, 128), jnp.float32)],
        scratch_shapes=[
            pltpu.VMEM((STEP // 2, BLK // 8, 16, 128), jnp.bfloat16),
            pltpu.VMEM((nblk, BLK, 128), jnp.float32),
            pltpu.VMEM((4 * nblk, BLK, 128), jnp.float32),
        ],
        **params(27, 32 * MIB),
        name="gradients",
    )(ids, own, at, q, p, *parts)


def join_kernel(*refs):
    kept, terms, out, keptv, termv, outv, sems = refs[0], refs[1:5], refs[5], *refs[6:]
    half = kept.shape[0] // 2
    loads = [pltpu.make_async_copy(terms[n], termv.at[n], sems.at[n]) for n in range(4)]
    stores = []
    for h in range(2):
        part = slice(half * h, half * h + half)
        loads.append(pltpu.make_async_copy(kept.at[part], keptv.at[part], sems.at[4 + h]))
        stores.append(pltpu.make_async_copy(outv.at[part], out.at[part], sems.at[6 + h]))
    for copy in loads:
        copy.start()
    for h in range(2):
        for n in (4 + h, 2 * h, 2 * h + 1):
            loads[n].wait()

        @pl.loop(0, half)
        def _(n):
            value = keptv[half * h + n].astype(jnp.float32)
            for m in (2 * h, 2 * h + 1):
                value = value + termv[m, n].astype(jnp.float32)
            outv[half * h + n] = value.astype(out.dtype)

        stores[h].start()
    for copy in stores:
        copy.wait()


def join(kept, low, high):
    term = low[0].shape
    return pl.pallas_call(
        join_kernel,
        in_specs=[ANY] * 5,
        out_specs=ANY,
        out_shape=jax.ShapeDtypeStruct(kept.shape, kept.dtype),
        scratch_shapes=[
            pltpu.VMEM(kept.shape, kept.dtype),
            pltpu.VMEM((4,) + term, kept.dtype),
            pltpu.VMEM(kept.shape, kept.dtype),
            pltpu.SemaphoreType.DMA((8,)),
        ],
        **params(5, 8 * MIB),
        name="join",
    )(kept, *low, *high)


def along(axis, delta):
    if axis == "z":
        number = lax.axis_size("grp")
        perm = [(i, (i + delta) % number) for i in range(number)]
        return lambda v: lax.ppermute(v, "grp", perm)

    def target(d):
        x, y, core = d // 8, d // 2 % 4, d % 2
        if axis == "core":
            core = 1 - core
        elif (axis == "first") == (core == 0):
            x = (x + delta) % 4
        else:
            y = (y + delta) % 4
        return x * 8 + y * 2 + core

    perm = [(d, target(d)) for d in range(32)]
    return lambda v: lax.ppermute(v, "dev", perm)


def add(*terms):
    total = terms[0].astype(jnp.float32)
    for term in terms[1:]:
        total = total + term.astype(jnp.float32)
    return total.astype(terms[0].dtype)


def ring_terms(axis, rel1, rel2, rel3):
    up, down = along(axis, 1), along(axis, -1)
    from_below = up(rel2[0])
    from_above = down(rel2[1])
    below1 = up(rel1[1])
    above0 = down(rel3[0])
    below0 = up(add(rel1[0], from_below))
    above1 = down(add(rel3[1], from_above))
    return (below0, above0), (below1, above1)


def scatter_scores(outs):
    halves = ring_terms("first", outs[0:2], outs[2:4], outs[4:6])
    sums = [outs[6][n] + halves[n // 2][0][n % 2] + halves[n // 2][1][n % 2] for n in range(4)]
    got = [along("second", n)(sums[n]) for n in (1, 2, 3)]
    return sums[0] + got[0] + got[1] + got[2]


def gather_weights(v):
    got = {3: along("first", 1)(v), 1: along("first", -1)(v), 2: along("first", 2)(v)}
    near = jnp.stack([v, got[1], got[2], got[3]])
    up, down, flip = along("second", 1), along("second", -1), along("core", 1)
    below, above = up(near), down(near)
    side = [near, below, above, down(above)]
    return side + [flip(w) for w in side]


def per_device(queries, passages, pairs, counts, positives):
    ndev = lax.axis_size("dev")
    ngrp = lax.axis_size("grp")
    width = queries.shape[1]
    maxp = pairs.shape[1]
    me = lax.axis_index("dev")
    z = lax.axis_index("grp")
    chip, core = me // 2, me % 2
    at = jnp.stack([core, chip // 4, chip % 4, me, chip]).astype(jnp.int32)

    def exchange(v):
        return lax.all_to_all(v, "dev", 0, 0, tiled=True)

    up, down, flip = along("z", 1), along("z", -1), along("core", 1)
    p_own = exchange(by_features(passages))
    above, below, given = down(p_own), up(p_own), flip(p_own)
    mine, theirs = place(None, [p_own], [0]), place(None, [given], [0])
    low, high = above[: ndev // 2], below[ndev // 2 :]
    low, high, theirs = lax.optimization_barrier((low, high, theirs))
    far = [down(low), up(high)]
    near = [above, below]
    mine = place(mine, near, [32, 96])
    theirs = place(theirs, [flip(v) for v in near], [32, 96])
    mine = place(mine, far, [64, 80])
    theirs = place(theirs, [flip(v) for v in far], [64, 80])
    q_own = exchange(by_features(queries, positives.reshape(1, BLK)))
    q = [q_own, flip(q_own)]

    group = counts[0]
    block = jnp.arange(ndev, dtype=jnp.int32)
    ends = jnp.sum(jnp.where(block[None, :] <= block[:, None], group[None, :], 0), axis=1)
    starts = ends - group
    t = jnp.arange(PAIRS, dtype=jnp.int32)
    own = jnp.sum((ends[None, :] <= t[:, None]).astype(jnp.int32), axis=1)
    start = jnp.sum(jnp.where(block[None, :] == own[:, None], starts[None, :], 0), axis=1)
    entry = own * maxp + t - start
    slot = jnp.arange(ndev * maxp, dtype=jnp.int32)
    ids = jnp.sum(jnp.where(slot[None, :] == entry[:, None], pairs.reshape(1, -1), 0), axis=1)
    ids = (ids + (ngrp - z) * ndev) % (ngrp * ndev)
    spare = jnp.full((128 - ndev,), 2 * PAIRS, jnp.int32)
    lists = jnp.stack([jnp.concatenate([v, spare]) for v in (ends, starts)] * 4)

    scores = scatter_scores(partial_scores(ids, own, at, q, (mine, theirs)))
    weights = softmax_weights(at, (scores, flip(scores)), lists, q_own, width ** (-0.5))
    *g, gq, lines = gradients(ids, own, at, q_own, mine, gather_weights(weights))

    low, high = ring_terms("z", g[1:3], g[3:5], g[5:7])
    q_rows = by_rows(exchange(gq))
    p_rows = by_rows(exchange(join(g[0], low, high)))
    return lines[:, 0:8].reshape(BLK), q_rows, p_rows


def solution(mesh):
    placed = (
        P(("grp", "dev"), None),
        P(("grp", "dev"), None),
        P("grp", None),
        P("grp", None),
        P(("grp", "dev")),
    )
    return jax.shard_map(
        per_device,
        mesh=mesh,
        in_specs=placed,
        out_specs=(P(("grp", "dev")), P(("grp", "dev"), None), P(("grp", "dev"), None)),
        check_vma=False,
    )
```

```python
import functools

import jax
import jax.numpy as jnp
from jax import lax
from jax.experimental import pallas as pl
from jax.experimental.pallas import tpu as pltpu
from jax.sharding import PartitionSpec as P

BLK = 128
HALF = BLK // 2
PAIRS = 128
PART = PAIRS // 2
ROWS = 8 * PART
TAIL = 16
STEP = 8
PARTS = 8
MIB = 1024 * 1024
SMEM = pl.BlockSpec(memory_space=pltpu.SMEM)
ANY = pl.BlockSpec(memory_space=pl.ANY)
VMEM = pl.BlockSpec(memory_space=pltpu.VMEM)


def params(limit, moved, flops=0):
    cost = pl.CostEstimate(flops=flops, bytes_accessed=moved, transcendentals=0)
    limit = pltpu.CompilerParams(vmem_limit_bytes=limit * MIB)
    return dict(compiler_params=limit, cost_estimate=cost)


def run_copies(copies):
    for copy in copies:
        copy.start()
    for copy in copies:
        copy.wait()


def pack_kernel(x, *refs):
    *outs, xv, outv, marks, sems = refs
    extra = outv.shape[1] - BLK
    if extra:
        run_copies([pltpu.make_async_copy(outs[0], marks, sems.at[0])])
        outs = outs[1:]
        tile = jnp.broadcast_to(marks[...].astype(jnp.float32), (extra, 128)).astype(jnp.bfloat16)
    width = x.shape[1]
    number = outv.shape[0] // PARTS
    tall = outv.shape[1] // len(outs)
    loads, stores = [], []
    for n in range(PARTS):
        cols = slice(n * width // PARTS, (n + 1) * width // PARTS)
        loads.append(pltpu.make_async_copy(x.at[:, cols], xv.at[:, cols], sems.at[n]))
        part = slice(n * number, (n + 1) * number)
        for m, out in enumerate(outs):
            source = outv.at[part, m * tall : (m + 1) * tall, :]
            sem = sems.at[PARTS * (1 + m) + n]
            stores.append(pltpu.make_async_copy(source, out.at[part], sem))
    for copy in loads:
        copy.start()
    for n in range(PARTS):
        loads[n].wait()
        for m in range(n * number, (n + 1) * number):
            outv[m, 0:BLK, :] = xv[:, 128 * m : 128 * m + 128].astype(jnp.bfloat16)
            if extra:
                outv[m, BLK:, :] = tile
        for copy in stores[n * len(outs) : (n + 1) * len(outs)]:
            copy.start()
    for copy in stores:
        copy.wait()


def by_features(x, pos=None):
    number = x.shape[1] // 128
    tall = BLK + (0 if pos is None else 16)
    shapes = [(number, HALF, 128)] * 2 if pos is None else [(number, tall, 128)]
    given = (x,) if pos is None else (x, pos)
    return pl.pallas_call(
        pack_kernel,
        in_specs=[ANY] * len(given),
        out_specs=[ANY] * len(shapes),
        out_shape=[jax.ShapeDtypeStruct(s, jnp.bfloat16) for s in shapes],
        scratch_shapes=[
            pltpu.VMEM(x.shape, x.dtype),
            pltpu.VMEM((number, tall, 128), jnp.bfloat16),
            pltpu.VMEM((1, BLK), jnp.int32),
            pltpu.SemaphoreType.DMA((3 * PARTS,)),
        ],
        **params(56 if pos is None else 5, 5 * MIB),
        name="pack",
    )(*given)


def unpack_kernel(x, out, xv, outv, sems):
    number = x.shape[0] // PARTS
    loads, stores = [], []
    for n in range(PARTS):
        part = slice(n * number, (n + 1) * number)
        loads.append(pltpu.make_async_copy(x.at[part], xv.at[part], sems.at[n]))
        cols = slice(n * number * 128, (n + 1) * number * 128)
        stores.append(pltpu.make_async_copy(outv.at[:, cols], out.at[:, cols], sems.at[PARTS + n]))
    for copy in loads:
        copy.start()
    for n in range(PARTS):
        loads[n].wait()
        for m in range(n * number, (n + 1) * number):
            outv[:, 128 * m : 128 * m + 128] = xv[m].astype(jnp.float32)
        stores[n].start()
    for copy in stores:
        copy.wait()


def by_rows(x):
    number = x.shape[0]
    return pl.pallas_call(
        unpack_kernel,
        in_specs=[ANY],
        out_specs=ANY,
        out_shape=jax.ShapeDtypeStruct((BLK, number * 128), jnp.float32),
        scratch_shapes=[
            pltpu.VMEM(x.shape, x.dtype),
            pltpu.VMEM((BLK, number * 128), jnp.float32),
            pltpu.SemaphoreType.DMA((2 * PARTS,)),
        ],
        **params(5, 8 * MIB),
        name="unpack",
    )(x)


PIECES = ((0, 32), (32, 16), (48, 16), (64, 16), (80, 16), (96, 16), (112, 16))


def place_kernel(*refs):
    *pieces, out, sems = refs
    copies = []
    for n, piece in enumerate(pieces):
        target = out.at[32 * (n // 2) : 32 * (n // 2) + 32, HALF * (n % 2) : HALF * (n % 2) + HALF, :]
        copies.append(pltpu.make_async_copy(piece, target, sems.at[n]))
    run_copies(copies)


def place(pieces):
    return pl.pallas_call(
        place_kernel,
        in_specs=[ANY] * 8,
        out_specs=ANY,
        out_shape=jax.ShapeDtypeStruct((4 * 32, BLK, 128), pieces[0].dtype),
        scratch_shapes=[pltpu.SemaphoreType.DMA((8,))],
        **params(1, 12 * MIB),
        name="place",
    )(*pieces)


def chip_at(at, core, lead, other):
    rx = jnp.where(core == 0, lead, other)
    ry = jnp.where(core == 0, other, lead)
    return ((at[1] + rx) % 4) * 4 + (at[2] + ry) % 4


def score_kernel(ids, own, at, q_own, q_sib, *refs):
    pieces, outs, (pv, sv) = (refs[:8], refs[8:16]), refs[16:23], refs[23:]
    core = at[0]
    spots = [
        (lead, other, chip_at(at, core, lead, other)) for lead in range(4) for other in range(4)
    ]

    @pl.loop(0, PART // STEP)
    def _(step):
        for u in range(STEP):
            there = ids[PART * core + step * STEP + u]
            for rel in range(4):

                @pl.when(there // 32 == rel)
                def _():
                    for side in range(2):
                        for h in range(2):
                            rows = slice(HALF * h, HALF * h + HALF)
                            lanes = slice(128 * side, 128 * side + 128)
                            pv[u, rows, lanes] = pieces[side][2 * rel + h][there % 32]

        for u in range(STEP):
            here = own[PART * core + step * STEP + u]
            left = jnp.concatenate([q_own[here, 0:BLK, :], q_sib[here, 0:BLK, :]], axis=1)
            tile = lax.dot_general(
                left, pv[u], (((1,), (1,)), ((), ())), preferred_element_type=jnp.float32
            )
            sv[u] = tile.reshape(BLK // 8, 8, 128)
        for u in range(STEP):
            where = pl.ds(pl.multiple_of(8 * (step * STEP + u), 8), 8)
            for lead, other, chip in spots:
                if lead == 0:
                    outs[6][other, where, :] = sv[u, chip]
                else:
                    outs[2 * lead - 2 + other // 2][other % 2, where, :] = sv[u, chip]


def partial_scores(ids, own, at, q, pieces):
    shapes = [(2, ROWS, 128)] * 6 + [(4, ROWS, 128)]
    return pl.pallas_call(
        score_kernel,
        in_specs=[SMEM] * 3 + [VMEM] * 18,
        out_specs=[VMEM] * 7,
        out_shape=[jax.ShapeDtypeStruct(s, jnp.float32) for s in shapes],
        scratch_shapes=[
            pltpu.VMEM((STEP, BLK, 2 * 128), jnp.bfloat16),
            pltpu.VMEM((STEP, BLK // 8, 8, 128), jnp.float32),
        ],
        **params(18, 20 * MIB),
        name="partial_scores",
    )(ids, own, at, *q, *pieces)


def softmax_kernel(at, *refs, scale):
    terms, lists, q, out, xv, listv, markv, sems = refs[:2], *refs[2:]
    loads = [
        pltpu.make_async_copy(terms[n], xv.at[ROWS * n : ROWS * n + ROWS, :], sems.at[n])
        for n in range(2)
    ]
    loads.append(pltpu.make_async_copy(lists, listv, sems.at[2]))
    loads.append(pltpu.make_async_copy(q.at[:, BLK:, :], markv, sems.at[3]))
    run_copies(loads)

    core = at[0]
    row = lax.broadcasted_iota(jnp.int32, (2 * ROWS, 1), 0)
    side = row // ROWS
    t = PART * (core + side - 2 * core * side) + (row & (ROWS - 1)) // 8
    r = row & 7
    lane = lax.broadcasted_iota(jnp.int32, (2 * ROWS, 128), 1)
    own = jnp.sum((listv[0:1, :] <= t).astype(jnp.int32), axis=1, keepdims=True)
    key = own * 8 + r

    x = xv[...] * scale
    high = jnp.max(x, axis=1, keepdims=True)
    part = jnp.sum(jnp.exp(x - high), axis=1, keepdims=True)
    lines = jnp.where(lane == 0, high, jnp.where(lane == 1, part, key.astype(jnp.float32))).T
    high, part, keys = lines[0:1], lines[1:2], lines[2:3]

    x, t, r, lane, own, key = [v[:ROWS] for v in (x, t, r, lane, own, key)]
    same = key.astype(jnp.float32) == keys
    top = jnp.max(jnp.where(same, high, -jnp.inf), axis=1, keepdims=True)
    total = jnp.where(same, part * jnp.exp(high - top), 0.0)
    lse = top + jnp.log(jnp.sum(total, axis=1, keepdims=True))

    block = lane == own
    first = t == jnp.sum(jnp.where(block, listv[1:2, :], 0), axis=1, keepdims=True)
    marks = jnp.max(markv[...].astype(jnp.float32), axis=1)
    marks = jnp.concatenate([marks, jnp.zeros((128 - marks.shape[0], 128), jnp.float32)], axis=0)
    listed = jnp.dot(
        block.astype(jnp.bfloat16), marks.astype(jnp.bfloat16), preferred_element_type=jnp.float32
    )
    target = jnp.sum(jnp.where(lane == at[4] * 8 + r, listed, 0.0), axis=1, keepdims=True)
    hit = first & (lane == target.astype(jnp.int32))
    weights = jnp.exp(x - lse) - hit.astype(jnp.float32)
    out[0:ROWS, :] = weights.astype(jnp.bfloat16)

    loss = lse - jnp.sum(jnp.where(hit, x, 0.0), axis=1, keepdims=True)
    line = lax.broadcasted_iota(jnp.int32, (TAIL, 128), 0)
    tail = jnp.zeros((TAIL, 128), jnp.float32)
    for h in range(2):
        here = first & (lane + 128 * h == key)
        rest = jnp.sum(jnp.where(here, loss, 0.0), axis=0, keepdims=True)
        for n in range(3):
            term = rest.astype(jnp.bfloat16).astype(jnp.float32)
            tail = jnp.where(line == 3 * h + n, term, tail)
            rest = rest - term
    out[ROWS:, :] = tail.astype(jnp.bfloat16)


def softmax_weights(at, terms, lists, q, scale):
    return pl.pallas_call(
        functools.partial(softmax_kernel, scale=scale),
        in_specs=[SMEM] + [ANY] * 4,
        out_specs=VMEM,
        out_shape=jax.ShapeDtypeStruct((ROWS + TAIL, 128), jnp.bfloat16),
        scratch_shapes=[
            pltpu.VMEM((2 * ROWS, 128), jnp.float32),
            pltpu.VMEM(lists.shape, jnp.int32),
            pltpu.VMEM((q.shape[0], TAIL, 128), jnp.bfloat16),
            pltpu.SemaphoreType.DMA((4,)),
        ],
        **params(16, 8 * MIB),
        name="softmax_weights",
    )(at, *terms, lists, q)


def grad_kernel(ids, own, at, q, p, *refs):
    parts, outs, gq, loss = refs[:8], refs[8:15], *refs[15:17]
    wv, gq_sum, gp_sum = refs[17:]
    core = at[0]

    @pl.loop(0, gq_sum.shape[0])
    def _(n):
        gq_sum[n] = jnp.zeros((BLK, 128), jnp.float32)
        for m in range(4):
            gp_sum[4 * n + m] = jnp.zeros((BLK, 128), jnp.float32)

    loss[...] = jnp.zeros(loss.shape, jnp.float32)
    line = lax.broadcasted_iota(jnp.int32, (TAIL, 128), 0) // 3
    mine = line == at[3] // 16
    for n in range(2):
        side = jnp.where(core == n, 0, 1)
        spots = []
        for m in range(4):
            for lead in range(4):
                chip = chip_at(at, side, lead, (0, 3, 1, 2)[m])
                spots.append((4 * n + m, lead, chip))
                tail = parts[4 * n + m][lead, ROWS:, :].astype(jnp.float32)
                loss[pl.ds(chip, 1), :] += jnp.sum(
                    jnp.where(mine, tail, 0.0), axis=0, keepdims=True
                )

        @pl.loop(0, PART // STEP)
        def _(step):
            for v in range(STEP // 2):
                where = pl.ds(pl.multiple_of(8 * STEP * step + 16 * v, 16), 16)
                for m, lead, chip in spots:
                    wv[v, chip] = parts[m][lead, where, :]
                two = wv[v].astype(jnp.float32)
                for o in range(2):
                    t = side * PART + step * STEP + 2 * v + o
                    here, there = own[t], ids[t]
                    tile = two[:, 8 * o : 8 * o + 8, :].reshape(BLK, 128).astype(jnp.bfloat16)
                    gq_sum[here] += jnp.dot(tile, p[there], preferred_element_type=jnp.float32)
                    gp_sum[there] += lax.dot_general(
                        tile,
                        q[here, 0:BLK, :],
                        (((0,), (0,)), ((), ())),
                        preferred_element_type=jnp.float32,
                    )

    @pl.loop(0, 16)
    def _(n):
        for m, (first, size) in enumerate(PIECES):
            for e in range(size // 16):
                outs[m][16 * e + n] = gp_sum[first + 16 * e + n].astype(jnp.bfloat16)
        for e in range(2):
            gq[16 * e + n] = gq_sum[16 * e + n].astype(jnp.bfloat16)

    loss[...] = pltpu.roll(loss[...], (128 - 8 * (at[3] % 16)) % 128, 1)


def gradients(ids, own, at, q, p, parts):
    nblk = q.shape[0]
    shapes = [(size, BLK, 128) for _, size in PIECES] + [(nblk, BLK, 128)]
    return pl.pallas_call(
        grad_kernel,
        in_specs=[SMEM] * 3 + [VMEM] * 10,
        out_specs=[VMEM] * 9,
        out_shape=[jax.ShapeDtypeStruct(s, jnp.bfloat16) for s in shapes]
        + [jax.ShapeDtypeStruct((BLK // 8, 128), jnp.float32)],
        scratch_shapes=[
            pltpu.VMEM((STEP // 2, BLK // 8, 16, 128), jnp.bfloat16),
            pltpu.VMEM((nblk, BLK, 128), jnp.float32),
            pltpu.VMEM((4 * nblk, BLK, 128), jnp.float32),
        ],
        **params(27, 32 * MIB),
        name="gradients",
    )(ids, own, at, q, p, *parts)


def join_kernel(*refs):
    kept, terms, out, keptv, termv, outv, sems = refs[0], refs[1:5], refs[5], *refs[6:]
    half = kept.shape[0] // 2
    loads = [pltpu.make_async_copy(terms[n], termv.at[n], sems.at[n]) for n in range(4)]
    stores = []
    for h in range(2):
        part = slice(half * h, half * h + half)
        loads.append(pltpu.make_async_copy(kept.at[part], keptv.at[part], sems.at[4 + h]))
        stores.append(pltpu.make_async_copy(outv.at[part], out.at[part], sems.at[6 + h]))
    for copy in loads:
        copy.start()
    for h in range(2):
        for n in (4 + h, 2 * h, 2 * h + 1):
            loads[n].wait()

        @pl.loop(0, half)
        def _(n):
            value = keptv[half * h + n].astype(jnp.float32)
            for m in (2 * h, 2 * h + 1):
                value = value + termv[m, n].astype(jnp.float32)
            outv[half * h + n] = value.astype(out.dtype)

        stores[h].start()
    for copy in stores:
        copy.wait()


def join(kept, low, high):
    term = low[0].shape
    return pl.pallas_call(
        join_kernel,
        in_specs=[ANY] * 5,
        out_specs=ANY,
        out_shape=jax.ShapeDtypeStruct(kept.shape, kept.dtype),
        scratch_shapes=[
            pltpu.VMEM(kept.shape, kept.dtype),
            pltpu.VMEM((4,) + term, kept.dtype),
            pltpu.VMEM(kept.shape, kept.dtype),
            pltpu.SemaphoreType.DMA((8,)),
        ],
        **params(5, 8 * MIB),
        name="join",
    )(kept, *low, *high)


def along(axis, delta):
    if axis == "z":
        number = lax.axis_size("grp")
        perm = [(i, (i + delta) % number) for i in range(number)]
        return lambda v: lax.ppermute(v, "grp", perm)

    def target(d):
        x, y, core = d // 8, d // 2 % 4, d % 2
        if axis == "core":
            core = 1 - core
        elif (axis == "first") == (core == 0):
            x = (x + delta) % 4
        else:
            y = (y + delta) % 4
        return x * 8 + y * 2 + core

    perm = [(d, target(d)) for d in range(32)]
    return lambda v: lax.ppermute(v, "dev", perm)


def add(*terms):
    total = terms[0].astype(jnp.float32)
    for term in terms[1:]:
        total = total + term.astype(jnp.float32)
    return total.astype(terms[0].dtype)


def ring_terms(axis, rel1, rel2, rel3):
    up, down = along(axis, 1), along(axis, -1)
    from_below = up(rel2[0])
    from_above = down(rel2[1])
    below1 = up(rel1[1])
    above0 = down(rel3[0])
    below0 = up(add(rel1[0], from_below))
    above1 = down(add(rel3[1], from_above))
    return (below0, above0), (below1, above1)


def scatter_scores(outs):
    halves = ring_terms("first", outs[0:2], outs[2:4], outs[4:6])
    sums = [outs[6][n] + halves[n // 2][0][n % 2] + halves[n // 2][1][n % 2] for n in range(4)]
    got = [along("second", n)(sums[n]) for n in (1, 2, 3)]
    return sums[0] + got[0] + got[1] + got[2]


def gather_weights(v):
    got = {3: along("first", 1)(v), 1: along("first", -1)(v), 2: along("first", 2)(v)}
    near = jnp.stack([v, got[1], got[2], got[3]])
    up, down, flip = along("second", 1), along("second", -1), along("core", 1)
    below, above = up(near), down(near)
    side = [near, below, above, down(above)]
    return side + [flip(w) for w in side]


def per_device(queries, passages, pairs, counts, positives):
    ndev = lax.axis_size("dev")
    ngrp = lax.axis_size("grp")
    width = queries.shape[1]
    maxp = pairs.shape[1]
    me = lax.axis_index("dev")
    z = lax.axis_index("grp")
    chip, core = me // 2, me % 2
    at = jnp.stack([core, chip // 4, chip % 4, me, chip]).astype(jnp.int32)

    def exchange(v):
        return lax.all_to_all(v, "dev", 0, 0, tiled=True)

    up, down, flip = along("z", 1), along("z", -1), along("core", 1)
    low, high = [exchange(v) for v in by_features(passages)]
    above0, below0 = down(low), up(low)
    q_tiles = by_features(queries, positives.reshape(1, BLK))[0]
    q_tiles, late, *_ = lax.optimization_barrier((q_tiles, high, above0, below0))
    above1, below1 = down(late), up(late)
    last0, last1, *_ = lax.optimization_barrier((above0, below1, above1))
    far0, far1 = down(last0), up(last1)
    pieces = [low, high, above0, above1, far0, far1, below0, below1]
    others = [flip(v) for v in pieces]
    q_own = exchange(q_tiles)
    q = [q_own, flip(q_own)]

    group = counts[0]
    block = jnp.arange(ndev, dtype=jnp.int32)
    ends = jnp.sum(jnp.where(block[None, :] <= block[:, None], group[None, :], 0), axis=1)
    starts = ends - group
    t = jnp.arange(PAIRS, dtype=jnp.int32)
    own = jnp.sum((ends[None, :] <= t[:, None]).astype(jnp.int32), axis=1)
    start = jnp.sum(jnp.where(block[None, :] == own[:, None], starts[None, :], 0), axis=1)
    entry = own * maxp + t - start
    slot = jnp.arange(ndev * maxp, dtype=jnp.int32)
    ids = jnp.sum(jnp.where(slot[None, :] == entry[:, None], pairs.reshape(1, -1), 0), axis=1)
    ids = (ids + (ngrp - z) * ndev) % (ngrp * ndev)
    spare = jnp.full((128 - ndev,), 2 * PAIRS, jnp.int32)
    lists = jnp.stack([jnp.concatenate([v, spare]) for v in (ends, starts)] * 4)

    scores = scatter_scores(partial_scores(ids, own, at, q, pieces + others))
    weights = softmax_weights(at, (scores, flip(scores)), lists, q_own, width ** (-0.5))
    *g, gq, lines = gradients(ids, own, at, q_own, place(pieces), gather_weights(weights))

    low, high = ring_terms("z", g[1:3], g[3:5], g[5:7])
    q_rows = by_rows(exchange(gq))
    p_rows = by_rows(exchange(join(g[0], low, high)))
    return lines[:, 0:8].reshape(BLK), q_rows, p_rows


def solution(mesh):
    placed = (
        P(("grp", "dev"), None),
        P(("grp", "dev"), None),
        P("grp", None),
        P("grp", None),
        P(("grp", "dev")),
    )
    return jax.shard_map(
        per_device,
        mesh=mesh,
        in_specs=placed,
        out_specs=(P(("grp", "dev")), P(("grp", "dev"), None), P(("grp", "dev"), None)),
        check_vma=False,
    )
```

```python
import functools

import jax
import jax.numpy as jnp
from jax import lax
from jax.experimental import pallas as pl
from jax.experimental.pallas import tpu as pltpu
from jax.sharding import PartitionSpec as P

BLK = 128
HALF = BLK // 2
PAIRS = 128
PART = PAIRS // 2
ROWS = 8 * PART
TAIL = 16
STEP = 8
PARTS = 8
MIB = 1024 * 1024
SMEM = pl.BlockSpec(memory_space=pltpu.SMEM)
ANY = pl.BlockSpec(memory_space=pl.ANY)
VMEM = pl.BlockSpec(memory_space=pltpu.VMEM)


def params(limit, moved, flops=0):
    cost = pl.CostEstimate(flops=flops, bytes_accessed=moved, transcendentals=0)
    limit = pltpu.CompilerParams(vmem_limit_bytes=limit * MIB)
    return dict(compiler_params=limit, cost_estimate=cost)


def run_copies(copies):
    for copy in copies:
        copy.start()
    for copy in copies:
        copy.wait()


def pack_kernel(x, *refs):
    *outs, xv, outv, marks, sems = refs
    extra = outv.shape[1] - BLK
    if extra:
        run_copies([pltpu.make_async_copy(outs[0], marks, sems.at[0])])
        outs = outs[1:]
        tile = jnp.broadcast_to(marks[...].astype(jnp.float32), (extra, 128)).astype(jnp.bfloat16)
    width = x.shape[1]
    number = outv.shape[0] // PARTS
    tall = outv.shape[1] // len(outs)
    loads, stores = [], []
    for n in range(PARTS):
        cols = slice(n * width // PARTS, (n + 1) * width // PARTS)
        loads.append(pltpu.make_async_copy(x.at[:, cols], xv.at[:, cols], sems.at[n]))
        part = slice(n * number, (n + 1) * number)
        for m, out in enumerate(outs):
            source = outv.at[part, m * tall : (m + 1) * tall, :]
            sem = sems.at[PARTS * (1 + m) + n]
            stores.append(pltpu.make_async_copy(source, out.at[part], sem))
    for copy in loads:
        copy.start()
    for n in range(PARTS):
        loads[n].wait()
        for m in range(n * number, (n + 1) * number):
            outv[m, 0:BLK, :] = xv[:, 128 * m : 128 * m + 128].astype(jnp.bfloat16)
            if extra:
                outv[m, BLK:, :] = tile
        for copy in stores[n * len(outs) : (n + 1) * len(outs)]:
            copy.start()
    for copy in stores:
        copy.wait()


def by_features(x, pos=None):
    number = x.shape[1] // 128
    tall = BLK + (0 if pos is None else 16)
    shapes = [(number, HALF, 128)] * 2 if pos is None else [(number, tall, 128)]
    given = (x,) if pos is None else (x, pos)
    return pl.pallas_call(
        pack_kernel,
        in_specs=[ANY] * len(given),
        out_specs=[ANY] * len(shapes),
        out_shape=[jax.ShapeDtypeStruct(s, jnp.bfloat16) for s in shapes],
        scratch_shapes=[
            pltpu.VMEM(x.shape, x.dtype),
            pltpu.VMEM((number, tall, 128), jnp.bfloat16),
            pltpu.VMEM((1, BLK), jnp.int32),
            pltpu.SemaphoreType.DMA((3 * PARTS,)),
        ],
        **params(56 if pos is None else 5, 5 * MIB),
        name="pack",
    )(*given)


def unpack_kernel(x, out, outv, sems):
    copies = []
    for n in range(PARTS):
        rows = slice(n * BLK // PARTS, (n + 1) * BLK // PARTS)
        for m in range(x.shape[0]):
            outv[rows, 128 * m : 128 * m + 128] = x[m, rows, :].astype(jnp.float32)
        copies.append(pltpu.make_async_copy(outv.at[rows, :], out.at[rows, :], sems.at[n]))
        copies[n].start()
    for copy in copies:
        copy.wait()


def by_rows(x):
    number = x.shape[0]
    return pl.pallas_call(
        unpack_kernel,
        in_specs=[VMEM],
        out_specs=ANY,
        out_shape=jax.ShapeDtypeStruct((BLK, number * 128), jnp.float32),
        scratch_shapes=[
            pltpu.VMEM((BLK, number * 128), jnp.float32),
            pltpu.SemaphoreType.DMA((PARTS,)),
        ],
        **params(5, 8 * MIB),
        name="unpack",
    )(x)


PIECES = ((0, 32), (32, 16), (48, 16), (64, 16), (80, 16), (96, 16), (112, 16))


def place_kernel(*refs):
    *pieces, out, sems = refs
    copies = []
    for n, piece in enumerate(pieces):
        target = out.at[32 * (n // 2) : 32 * (n // 2) + 32, HALF * (n % 2) : HALF * (n % 2) + HALF, :]
        copies.append(pltpu.make_async_copy(piece, target, sems.at[n]))
    run_copies(copies)


def place(pieces):
    return pl.pallas_call(
        place_kernel,
        in_specs=[ANY] * 8,
        out_specs=ANY,
        out_shape=jax.ShapeDtypeStruct((4 * 32, BLK, 128), pieces[0].dtype),
        scratch_shapes=[pltpu.SemaphoreType.DMA((8,))],
        **params(1, 12 * MIB),
        name="place",
    )(*pieces)


def chip_at(at, core, lead, other):
    rx = jnp.where(core == 0, lead, other)
    ry = jnp.where(core == 0, other, lead)
    return ((at[1] + rx) % 4) * 4 + (at[2] + ry) % 4


def score_kernel(ids, own, at, q_own, q_sib, *refs):
    pieces, outs, (pv, sv) = (refs[:8], refs[8:16]), refs[16:23], refs[23:]
    core = at[0]
    spots = [
        (lead, other, chip_at(at, core, lead, other)) for lead in range(4) for other in range(4)
    ]

    @pl.loop(0, PART // STEP)
    def _(step):
        for u in range(STEP):
            there = ids[PART * core + step * STEP + u]
            for rel in range(4):

                @pl.when(there // 32 == rel)
                def _():
                    for side in range(2):
                        for h in range(2):
                            rows = slice(HALF * h, HALF * h + HALF)
                            lanes = slice(128 * side, 128 * side + 128)
                            pv[u, rows, lanes] = pieces[side][2 * rel + h][there % 32]

        for u in range(STEP):
            here = own[PART * core + step * STEP + u]
            left = jnp.concatenate([q_own[here, 0:BLK, :], q_sib[here, 0:BLK, :]], axis=1)
            tile = lax.dot_general(
                left, pv[u], (((1,), (1,)), ((), ())), preferred_element_type=jnp.float32
            )
            sv[u] = tile.reshape(BLK // 8, 8, 128)
        for u in range(STEP):
            where = pl.ds(pl.multiple_of(8 * (step * STEP + u), 8), 8)
            for lead, other, chip in spots:
                if lead == 0:
                    outs[6][other, where, :] = sv[u, chip]
                else:
                    outs[2 * lead - 2 + other // 2][other % 2, where, :] = sv[u, chip]


def partial_scores(ids, own, at, q, pieces):
    shapes = [(2, ROWS, 128)] * 6 + [(4, ROWS, 128)]
    return pl.pallas_call(
        score_kernel,
        in_specs=[SMEM] * 3 + [VMEM] * 18,
        out_specs=[VMEM] * 7,
        out_shape=[jax.ShapeDtypeStruct(s, jnp.float32) for s in shapes],
        scratch_shapes=[
            pltpu.VMEM((STEP, BLK, 2 * 128), jnp.bfloat16),
            pltpu.VMEM((STEP, BLK // 8, 8, 128), jnp.float32),
        ],
        **params(18, 20 * MIB),
        name="partial_scores",
    )(ids, own, at, *q, *pieces)


def softmax_kernel(at, *refs, scale):
    terms, lists, q, out, xv, listv, markv, sems = refs[:2], *refs[2:]
    loads = [
        pltpu.make_async_copy(terms[n], xv.at[ROWS * n : ROWS * n + ROWS, :], sems.at[n])
        for n in range(2)
    ]
    loads.append(pltpu.make_async_copy(lists, listv, sems.at[2]))
    loads.append(pltpu.make_async_copy(q.at[:, BLK:, :], markv, sems.at[3]))
    run_copies(loads)

    core = at[0]
    row = lax.broadcasted_iota(jnp.int32, (2 * ROWS, 1), 0)
    side = row // ROWS
    t = PART * (core + side - 2 * core * side) + (row & (ROWS - 1)) // 8
    r = row & 7
    lane = lax.broadcasted_iota(jnp.int32, (2 * ROWS, 128), 1)
    own = jnp.sum((listv[0:1, :] <= t).astype(jnp.int32), axis=1, keepdims=True)
    key = own * 8 + r

    x = xv[...] * scale
    high = jnp.max(x, axis=1, keepdims=True)
    part = jnp.sum(jnp.exp(x - high), axis=1, keepdims=True)
    lines = jnp.where(lane == 0, high, jnp.where(lane == 1, part, key.astype(jnp.float32))).T
    high, part, keys = lines[0:1], lines[1:2], lines[2:3]

    x, t, r, lane, own, key = [v[:ROWS] for v in (x, t, r, lane, own, key)]
    same = key.astype(jnp.float32) == keys
    top = jnp.max(jnp.where(same, high, -jnp.inf), axis=1, keepdims=True)
    total = jnp.where(same, part * jnp.exp(high - top), 0.0)
    lse = top + jnp.log(jnp.sum(total, axis=1, keepdims=True))

    block = lane == own
    first = t == jnp.sum(jnp.where(block, listv[1:2, :], 0), axis=1, keepdims=True)
    marks = jnp.max(markv[...].astype(jnp.float32), axis=1)
    marks = jnp.concatenate([marks, jnp.zeros((128 - marks.shape[0], 128), jnp.float32)], axis=0)
    listed = jnp.dot(
        block.astype(jnp.bfloat16), marks.astype(jnp.bfloat16), preferred_element_type=jnp.float32
    )
    target = jnp.sum(jnp.where(lane == at[4] * 8 + r, listed, 0.0), axis=1, keepdims=True)
    hit = first & (lane == target.astype(jnp.int32))
    weights = jnp.exp(x - lse) - hit.astype(jnp.float32)
    out[0:ROWS, :] = weights.astype(jnp.bfloat16)

    loss = lse - jnp.sum(jnp.where(hit, x, 0.0), axis=1, keepdims=True)
    line = lax.broadcasted_iota(jnp.int32, (TAIL, 128), 0)
    tail = jnp.zeros((TAIL, 128), jnp.float32)
    for h in range(2):
        here = first & (lane + 128 * h == key)
        rest = jnp.sum(jnp.where(here, loss, 0.0), axis=0, keepdims=True)
        for n in range(3):
            term = rest.astype(jnp.bfloat16).astype(jnp.float32)
            tail = jnp.where(line == 3 * h + n, term, tail)
            rest = rest - term
    out[ROWS:, :] = tail.astype(jnp.bfloat16)


def softmax_weights(at, terms, lists, q, scale):
    return pl.pallas_call(
        functools.partial(softmax_kernel, scale=scale),
        in_specs=[SMEM] + [ANY] * 4,
        out_specs=VMEM,
        out_shape=jax.ShapeDtypeStruct((ROWS + TAIL, 128), jnp.bfloat16),
        scratch_shapes=[
            pltpu.VMEM((2 * ROWS, 128), jnp.float32),
            pltpu.VMEM(lists.shape, jnp.int32),
            pltpu.VMEM((q.shape[0], TAIL, 128), jnp.bfloat16),
            pltpu.SemaphoreType.DMA((4,)),
        ],
        **params(16, 8 * MIB),
        name="softmax_weights",
    )(at, *terms, lists, q)


GATHERED = tuple((other, (0, 1, 2, 3)) for other in (0, 3, 1, 2))


def weight_spots(at, n, parts):
    side = jnp.where(at[0] == n, 0, 1)
    spots = []
    for m, (other, leads) in enumerate(GATHERED):
        for e, lead in enumerate(leads):
            spots.append((parts[len(GATHERED) * n + m], e, chip_at(at, side, lead, other)))
    return side * PART, spots


def for_pairs(spots, wv, use):
    @pl.loop(0, PART // STEP)
    def _(step):
        for v in range(STEP // 2):
            where = pl.ds(pl.multiple_of(8 * STEP * step + 16 * v, 16), 16)
            for piece, e, chip in spots:
                wv[v, chip] = piece[e, where, :]
            two = wv[v].astype(jnp.float32)
            for o in range(2):
                tile = two[:, 8 * o : 8 * o + 8, :].reshape(BLK, 128).astype(jnp.bfloat16)
                use(step * STEP + 2 * v + o, tile)


def clear(total):
    @pl.loop(0, total.shape[0] // 4)
    def _(n):
        for m in range(4):
            total[4 * n + m] = jnp.zeros((BLK, 128), jnp.float32)


def grad_p_kernel(ids, own, at, q, *refs):
    parts, outs, loss, wv, total = refs[:8], refs[8:15], *refs[15:]
    clear(total)
    mine = lax.broadcasted_iota(jnp.int32, (TAIL, 128), 0) // 3 == at[3] // 16
    for n in range(2):
        start, spots = weight_spots(at, n, parts)
        for piece, e, chip in spots:
            tail = jnp.where(mine, piece[e, ROWS:, :].astype(jnp.float32), 0.0)
            line = jnp.sum(tail, axis=0, keepdims=True)
            row = pl.ds(chip, 1)
            loss[row, :] = line if n == 0 else loss[row, :] + line

        def use(k, tile):
            total[ids[start + k]] += lax.dot_general(
                tile,
                q[own[start + k], 0:BLK, :],
                (((0,), (0,)), ((), ())),
                preferred_element_type=jnp.float32,
            )

        for_pairs(spots, wv, use)

    @pl.loop(0, 16)
    def _(n):
        for m, (first, size) in enumerate(PIECES):
            for e in range(size // 16):
                outs[m][16 * e + n] = total[first + 16 * e + n].astype(jnp.bfloat16)

    loss[...] = pltpu.roll(loss[...], (128 - 8 * (at[3] % 16)) % 128, 1)


def grad_passages(ids, own, at, q, parts):
    shapes = [jax.ShapeDtypeStruct((size, BLK, 128), jnp.bfloat16) for _, size in PIECES]
    return pl.pallas_call(
        grad_p_kernel,
        in_specs=[SMEM] * 3 + [VMEM] * 9,
        out_specs=[VMEM] * 8,
        out_shape=shapes + [jax.ShapeDtypeStruct((BLK // 8, 128), jnp.float32)],
        scratch_shapes=[
            pltpu.VMEM((STEP // 2, BLK // 8, 16, 128), jnp.bfloat16),
            pltpu.VMEM((PAIRS, BLK, 128), jnp.float32),
        ],
        **params(20, 20 * MIB),
        name="grad_passages",
    )(ids, own, at, q, *parts)


def grad_q_kernel(ids, own, at, p, *refs):
    parts, out, wv, total = refs[:8], *refs[8:]
    clear(total)
    for n in range(2):
        start, spots = weight_spots(at, n, parts)

        def use(k, tile):
            total[own[start + k]] += jnp.dot(
                tile, p[ids[start + k]], preferred_element_type=jnp.float32
            )

        for_pairs(spots, wv, use)

    @pl.loop(0, total.shape[0] // 4)
    def _(n):
        for m in range(4):
            out[4 * n + m] = total[4 * n + m].astype(jnp.bfloat16)


def grad_queries(ids, own, at, p, parts):
    nblk = p.shape[0] // 4
    return pl.pallas_call(
        grad_q_kernel,
        in_specs=[SMEM] * 3 + [VMEM] * 9,
        out_specs=VMEM,
        out_shape=jax.ShapeDtypeStruct((nblk, BLK, 128), jnp.bfloat16),
        scratch_shapes=[
            pltpu.VMEM((STEP // 2, BLK // 8, 16, 128), jnp.bfloat16),
            pltpu.VMEM((nblk, BLK, 128), jnp.float32),
        ],
        **params(14, 20 * MIB),
        name="grad_queries",
    )(ids, own, at, p, *parts)


def join_kernel(*refs):
    kept, terms, out, keptv, termv, outv, sems = refs[0], refs[1:5], refs[5], *refs[6:]
    half = kept.shape[0] // 2
    loads = [pltpu.make_async_copy(terms[n], termv.at[n], sems.at[n]) for n in range(4)]
    stores = []
    for h in range(2):
        part = slice(half * h, half * h + half)
        loads.append(pltpu.make_async_copy(kept.at[part], keptv.at[part], sems.at[4 + h]))
        stores.append(pltpu.make_async_copy(outv.at[part], out.at[part], sems.at[6 + h]))
    for copy in loads:
        copy.start()
    for h in range(2):
        for n in (4 + h, 2 * h, 2 * h + 1):
            loads[n].wait()

        @pl.loop(0, half)
        def _(n):
            value = keptv[half * h + n].astype(jnp.float32)
            for m in (2 * h, 2 * h + 1):
                value = value + termv[m, n].astype(jnp.float32)
            outv[half * h + n] = value.astype(out.dtype)

        stores[h].start()
    for copy in stores:
        copy.wait()


def join(kept, low, high):
    term = low[0].shape
    return pl.pallas_call(
        join_kernel,
        in_specs=[ANY] * 5,
        out_specs=ANY,
        out_shape=jax.ShapeDtypeStruct(kept.shape, kept.dtype),
        scratch_shapes=[
            pltpu.VMEM(kept.shape, kept.dtype),
            pltpu.VMEM((4,) + term, kept.dtype),
            pltpu.VMEM(kept.shape, kept.dtype),
            pltpu.SemaphoreType.DMA((8,)),
        ],
        **params(5, 8 * MIB),
        name="join",
    )(kept, *low, *high)


def along(axis, delta):
    if axis == "z":
        number = lax.axis_size("grp")
        perm = [(i, (i + delta) % number) for i in range(number)]
        return lambda v: lax.ppermute(v, "grp", perm)

    def target(d):
        x, y, core = d // 8, d // 2 % 4, d % 2
        if axis == "core":
            core = 1 - core
        elif (axis == "first") == (core == 0):
            x = (x + delta) % 4
        else:
            y = (y + delta) % 4
        return x * 8 + y * 2 + core

    perm = [(d, target(d)) for d in range(32)]
    return lambda v: lax.ppermute(v, "dev", perm)


def add(*terms):
    total = terms[0].astype(jnp.float32)
    for term in terms[1:]:
        total = total + term.astype(jnp.float32)
    return total.astype(terms[0].dtype)


def ring_terms(axis, rel1, rel2, rel3):
    up, down = along(axis, 1), along(axis, -1)
    from_below = up(rel2[0])
    from_above = down(rel2[1])
    below1 = up(rel1[1])
    above0 = down(rel3[0])
    below0 = up(add(rel1[0], from_below))
    above1 = down(add(rel3[1], from_above))
    return (below0, above0), (below1, above1)


def scatter_scores(outs):
    halves = ring_terms("first", outs[0:2], outs[2:4], outs[4:6])
    sums = [outs[6][n] + halves[n // 2][0][n % 2] + halves[n // 2][1][n % 2] for n in range(4)]
    got = [along("second", n)(sums[n]) for n in (1, 2, 3)]
    return sums[0] + got[0] + got[1] + got[2]


def gather_weights(v):
    got = {3: along("first", 1)(v), 1: along("first", -1)(v), 2: along("first", 2)(v)}
    near = jnp.stack([v, got[1], got[2], got[3]])
    up, down, flip = along("second", 1), along("second", -1), along("core", 1)
    below, above = up(near), down(near)
    side = [near, below, above, down(above)]
    return side + [flip(w) for w in side]


def per_device(queries, passages, pairs, counts, positives):
    ndev = lax.axis_size("dev")
    ngrp = lax.axis_size("grp")
    width = queries.shape[1]
    maxp = pairs.shape[1]
    me = lax.axis_index("dev")
    z = lax.axis_index("grp")
    chip, core = me // 2, me % 2
    at = jnp.stack([core, chip // 4, chip % 4, me, chip]).astype(jnp.int32)

    def exchange(v):
        return lax.all_to_all(v, "dev", 0, 0, tiled=True)

    up, down, flip = along("z", 1), along("z", -1), along("core", 1)
    low, high = [exchange(v) for v in by_features(passages)]
    above0, below0 = down(low), up(low)
    q_tiles = by_features(queries, positives.reshape(1, BLK))[0]
    q_tiles, late, *_ = lax.optimization_barrier((q_tiles, high, above0, below0))
    above1, below1 = down(late), up(late)
    last0, last1, *_ = lax.optimization_barrier((above0, below1, above1))
    far0, far1 = down(last0), up(last1)
    pieces = [low, high, above0, above1, far0, far1, below0, below1]
    others = [flip(v) for v in pieces]
    q_own = exchange(q_tiles)
    q = [q_own, flip(q_own)]

    group = counts[0]
    block = jnp.arange(ndev, dtype=jnp.int32)
    ends = jnp.sum(jnp.where(block[None, :] <= block[:, None], group[None, :], 0), axis=1)
    starts = ends - group
    t = jnp.arange(PAIRS, dtype=jnp.int32)
    own = jnp.sum((ends[None, :] <= t[:, None]).astype(jnp.int32), axis=1)
    start = jnp.sum(jnp.where(block[None, :] == own[:, None], starts[None, :], 0), axis=1)
    entry = own * maxp + t - start
    slot = jnp.arange(ndev * maxp, dtype=jnp.int32)
    ids = jnp.sum(jnp.where(slot[None, :] == entry[:, None], pairs.reshape(1, -1), 0), axis=1)
    ids = (ids + (ngrp - z) * ndev) % (ngrp * ndev)
    spare = jnp.full((128 - ndev,), 2 * PAIRS, jnp.int32)
    lists = jnp.stack([jnp.concatenate([v, spare]) for v in (ends, starts)] * 4)

    scores = scatter_scores(partial_scores(ids, own, at, q, pieces + others))
    weights = softmax_weights(at, (scores, flip(scores)), lists, q_own, width ** (-0.5))
    parts = gather_weights(weights)
    q_own, mine = lax.optimization_barrier((q_own, place(pieces)))
    *g, lines = grad_passages(ids, own, at, q_own, parts)

    low, high = ring_terms("z", g[1:3], g[3:5], g[5:7])
    q_rows = by_rows(exchange(grad_queries(ids, own, at, mine, parts)))
    p_rows = by_rows(exchange(join(g[0], low, high)))
    return lines[:, 0:8].reshape(BLK), q_rows, p_rows


def solution(mesh):
    placed = (
        P(("grp", "dev"), None),
        P(("grp", "dev"), None),
        P("grp", None),
        P("grp", None),
        P(("grp", "dev")),
    )
    return jax.shard_map(
        per_device,
        mesh=mesh,
        in_specs=placed,
        out_specs=(P(("grp", "dev")), P(("grp", "dev"), None), P(("grp", "dev"), None)),
        check_vma=False,
    )
```

```python
import functools

import jax
import jax.numpy as jnp
from jax import lax
from jax.experimental import pallas as pl
from jax.experimental.pallas import tpu as pltpu
from jax.sharding import PartitionSpec as P

BLK = 128
HALF = BLK // 2
PAIRS = 128
PART = PAIRS // 2
ROWS = 8 * PART
TAIL = 16
STEP = 8
PARTS = 8
MIB = 1024 * 1024
SMEM = pl.BlockSpec(memory_space=pltpu.SMEM)
ANY = pl.BlockSpec(memory_space=pl.ANY)
VMEM = pl.BlockSpec(memory_space=pltpu.VMEM)


def params(limit, moved, flops=0):
    cost = pl.CostEstimate(flops=flops, bytes_accessed=moved, transcendentals=0)
    limit = pltpu.CompilerParams(vmem_limit_bytes=limit * MIB)
    return dict(compiler_params=limit, cost_estimate=cost)


def run_copies(copies):
    for copy in copies:
        copy.start()
    for copy in copies:
        copy.wait()


def pack_kernel(x, *refs, rows):
    *given, out, xv, outv, marks, sems = refs
    tall = rows.stop - rows.start
    width = x.shape[1]
    number = outv.shape[0] // PARTS
    loads, stores = [], []
    for n in range(PARTS):
        cols = slice(n * width // PARTS, (n + 1) * width // PARTS)
        loads.append(pltpu.make_async_copy(x.at[rows, cols], xv.at[:, cols], sems.at[n]))
        part = slice(n * number, (n + 1) * number)
        stores.append(pltpu.make_async_copy(outv.at[part], out.at[part], sems.at[PARTS + n]))
    for copy in loads:
        copy.start()
    if given:
        run_copies([pltpu.make_async_copy(given[0], marks, sems.at[2 * PARTS])])
        tile = jnp.broadcast_to(marks[...].astype(jnp.float32), (16, 128)).astype(jnp.bfloat16)
    for n in range(PARTS):
        loads[n].wait()
        for m in range(n * number, (n + 1) * number):
            outv[m, 0:tall, :] = xv[:, 128 * m : 128 * m + 128].astype(jnp.bfloat16)
            if given:
                outv[m, tall:, :] = tile
        stores[n].start()
    for copy in stores:
        copy.wait()


def by_features(x, rows, *pos):
    tall = rows.stop - rows.start
    shape = (x.shape[1] // 128, tall + 16 * len(pos), 128)
    return pl.pallas_call(
        functools.partial(pack_kernel, rows=rows),
        in_specs=[ANY] * (1 + len(pos)),
        out_specs=ANY,
        out_shape=jax.ShapeDtypeStruct(shape, jnp.bfloat16),
        scratch_shapes=[
            pltpu.VMEM((tall, x.shape[1]), x.dtype),
            pltpu.VMEM(shape, jnp.bfloat16),
            pltpu.VMEM((1, BLK), jnp.int32),
            pltpu.SemaphoreType.DMA((2 * PARTS + 1,)),
        ],
        **params(56 if rows.stop == HALF else 5, 4 * MIB),
        name="pack",
    )(x, *pos)


def unpack_kernel(x, out, outv, sems):
    copies = []
    for n in range(PARTS):
        rows = slice(n * BLK // PARTS, (n + 1) * BLK // PARTS)
        for m in range(x.shape[0]):
            outv[rows, 128 * m : 128 * m + 128] = x[m, rows, :].astype(jnp.float32)
        copies.append(pltpu.make_async_copy(outv.at[rows, :], out.at[rows, :], sems.at[n]))
        copies[n].start()
    for copy in copies:
        copy.wait()


def by_rows(x):
    number = x.shape[0]
    return pl.pallas_call(
        unpack_kernel,
        in_specs=[VMEM],
        out_specs=ANY,
        out_shape=jax.ShapeDtypeStruct((BLK, number * 128), jnp.float32),
        scratch_shapes=[
            pltpu.VMEM((BLK, number * 128), jnp.float32),
            pltpu.SemaphoreType.DMA((PARTS,)),
        ],
        **params(5, 8 * MIB),
        name="unpack",
    )(x)


PIECES = ((0, 32), (32, 16), (48, 16), (64, 16), (80, 16), (96, 16), (112, 16))


def place_kernel(*refs):
    *pieces, out, sems = refs
    copies = []
    for n, piece in enumerate(pieces):
        target = out.at[32 * (n // 2) : 32 * (n // 2) + 32, HALF * (n % 2) : HALF * (n % 2) + HALF, :]
        copies.append(pltpu.make_async_copy(piece, target, sems.at[n]))
    run_copies(copies)


def place(pieces):
    return pl.pallas_call(
        place_kernel,
        in_specs=[ANY] * 8,
        out_specs=ANY,
        out_shape=jax.ShapeDtypeStruct((4 * 32, BLK, 128), pieces[0].dtype),
        scratch_shapes=[pltpu.SemaphoreType.DMA((8,))],
        **params(1, 12 * MIB),
        name="place",
    )(*pieces)


def chip_at(at, core, lead, other):
    rx = jnp.where(core == 0, lead, other)
    ry = jnp.where(core == 0, other, lead)
    return ((at[1] + rx) % 4) * 4 + (at[2] + ry) % 4


def score_kernel(ids, own, at, q_own, q_sib, *refs):
    pieces, outs, (pv, sv) = (refs[:8], refs[8:16]), refs[16:23], refs[23:]
    core = at[0]
    spots = [
        (lead, other, chip_at(at, core, lead, other)) for lead in range(4) for other in range(4)
    ]

    @pl.loop(0, PART // STEP)
    def _(step):
        for u in range(STEP):
            there = ids[PART * core + step * STEP + u]
            for rel in range(4):

                @pl.when(there // 32 == rel)
                def _():
                    for side in range(2):
                        for h in range(2):
                            rows = slice(HALF * h, HALF * h + HALF)
                            lanes = slice(128 * side, 128 * side + 128)
                            pv[u, rows, lanes] = pieces[side][2 * rel + h][there % 32]

        for u in range(STEP):
            here = own[PART * core + step * STEP + u]
            left = jnp.concatenate([q_own[here, 0:BLK, :], q_sib[here, 0:BLK, :]], axis=1)
            tile = lax.dot_general(
                left, pv[u], (((1,), (1,)), ((), ())), preferred_element_type=jnp.float32
            )
            sv[u] = tile.reshape(BLK // 8, 8, 128)
        for u in range(STEP):
            where = pl.ds(pl.multiple_of(8 * (step * STEP + u), 8), 8)
            for lead, other, chip in spots:
                if lead == 0:
                    outs[6][other, where, :] = sv[u, chip]
                else:
                    outs[2 * lead - 2 + other // 2][other % 2, where, :] = sv[u, chip]


def partial_scores(ids, own, at, q, pieces):
    shapes = [(2, ROWS, 128)] * 6 + [(4, ROWS, 128)]
    return pl.pallas_call(
        score_kernel,
        in_specs=[SMEM] * 3 + [VMEM] * 18,
        out_specs=[VMEM] * 7,
        out_shape=[jax.ShapeDtypeStruct(s, jnp.float32) for s in shapes],
        scratch_shapes=[
            pltpu.VMEM((STEP, BLK, 2 * 128), jnp.bfloat16),
            pltpu.VMEM((STEP, BLK // 8, 8, 128), jnp.float32),
        ],
        **params(18, 20 * MIB),
        name="partial_scores",
    )(ids, own, at, *q, *pieces)


def softmax_kernel(at, x_own, x_sib, listv, q, out, *, scale):
    core = at[0]
    row = lax.broadcasted_iota(jnp.int32, (2 * ROWS, 1), 0)
    side = row // ROWS
    t = PART * (core + side - 2 * core * side) + (row & (ROWS - 1)) // 8
    r = row & 7
    lane = lax.broadcasted_iota(jnp.int32, (2 * ROWS, 128), 1)
    own = jnp.sum((listv[0:1, :] <= t).astype(jnp.int32), axis=1, keepdims=True)
    key = own * 8 + r

    x = jnp.concatenate([x_own[...], x_sib[...]], axis=0) * scale
    high = jnp.max(x, axis=1, keepdims=True)
    part = jnp.sum(jnp.exp(x - high), axis=1, keepdims=True)
    lines = jnp.where(lane == 0, high, jnp.where(lane == 1, part, key.astype(jnp.float32))).T
    high, part, keys = lines[0:1], lines[1:2], lines[2:3]

    x, t, r, lane, own, key = [v[:ROWS] for v in (x, t, r, lane, own, key)]
    same = key.astype(jnp.float32) == keys
    top = jnp.max(jnp.where(same, high, -jnp.inf), axis=1, keepdims=True)
    total = jnp.where(same, part * jnp.exp(high - top), 0.0)
    lse = top + jnp.log(jnp.sum(total, axis=1, keepdims=True))

    block = lane == own
    first = t == jnp.sum(jnp.where(block, listv[1:2, :], 0), axis=1, keepdims=True)
    marks = jnp.max(q[:, BLK:, :].astype(jnp.float32), axis=1)
    marks = jnp.concatenate([marks, jnp.zeros((128 - marks.shape[0], 128), jnp.float32)], axis=0)
    listed = jnp.dot(
        block.astype(jnp.bfloat16), marks.astype(jnp.bfloat16), preferred_element_type=jnp.float32
    )
    target = jnp.sum(jnp.where(lane == at[4] * 8 + r, listed, 0.0), axis=1, keepdims=True)
    hit = first & (lane == target.astype(jnp.int32))
    weights = jnp.exp(x - lse) - hit.astype(jnp.float32)
    out[0:ROWS, :] = weights.astype(jnp.bfloat16)

    loss = lse - jnp.sum(jnp.where(hit, x, 0.0), axis=1, keepdims=True)
    line = lax.broadcasted_iota(jnp.int32, (TAIL, 128), 0)
    tail = jnp.zeros((TAIL, 128), jnp.float32)
    for h in range(2):
        here = first & (lane + 128 * h == key)
        rest = jnp.sum(jnp.where(here, loss, 0.0), axis=0, keepdims=True)
        for n in range(3):
            term = rest.astype(jnp.bfloat16).astype(jnp.float32)
            tail = jnp.where(line == 3 * h + n, term, tail)
            rest = rest - term
    out[ROWS:, :] = tail.astype(jnp.bfloat16)


def softmax_weights(at, terms, lists, q, scale):
    return pl.pallas_call(
        functools.partial(softmax_kernel, scale=scale),
        in_specs=[SMEM] + [VMEM] * 4,
        out_specs=VMEM,
        out_shape=jax.ShapeDtypeStruct((ROWS + TAIL, 128), jnp.bfloat16),
        **params(16, 8 * MIB),
        name="softmax_weights",
    )(at, *terms, lists, q)


GATHERED = tuple((other, (0, 1, 2, 3)) for other in (0, 3, 1, 2))


def weight_spots(at, n, parts):
    side = jnp.where(at[0] == n, 0, 1)
    spots = []
    for m, (other, leads) in enumerate(GATHERED):
        for e, lead in enumerate(leads):
            spots.append((parts[len(GATHERED) * n + m], e, chip_at(at, side, lead, other)))
    return side * PART, spots


def for_pairs(spots, wv, use):
    @pl.loop(0, PART // STEP)
    def _(step):
        for v in range(STEP // 2):
            where = pl.ds(pl.multiple_of(8 * STEP * step + 16 * v, 16), 16)
            for piece, e, chip in spots:
                wv[v, chip] = piece[e, where, :]
            two = wv[v].astype(jnp.float32)
            for o in range(2):
                tile = two[:, 8 * o : 8 * o + 8, :].reshape(BLK, 128).astype(jnp.bfloat16)
                use(step * STEP + 2 * v + o, tile)


def clear(total):
    @pl.loop(0, total.shape[0] // 4)
    def _(n):
        for m in range(4):
            total[4 * n + m] = jnp.zeros((BLK, 128), jnp.float32)


def grad_p_kernel(ids, own, at, q, *refs):
    parts, outs, loss, wv, total = refs[:8], refs[8:15], *refs[15:]
    clear(total)
    mine = lax.broadcasted_iota(jnp.int32, (TAIL, 128), 0) // 3 == at[3] // 16
    for n in range(2):
        start, spots = weight_spots(at, n, parts)
        for piece, e, chip in spots:
            tail = jnp.where(mine, piece[e, ROWS:, :].astype(jnp.float32), 0.0)
            line = jnp.sum(tail, axis=0, keepdims=True)
            row = pl.ds(chip, 1)
            loss[row, :] = line if n == 0 else loss[row, :] + line

        def use(k, tile):
            total[ids[start + k]] += lax.dot_general(
                tile,
                q[own[start + k], 0:BLK, :],
                (((0,), (0,)), ((), ())),
                preferred_element_type=jnp.float32,
            )

        for_pairs(spots, wv, use)

    @pl.loop(0, 16)
    def _(n):
        for m, (first, size) in enumerate(PIECES):
            for e in range(size // 16):
                outs[m][16 * e + n] = total[first + 16 * e + n].astype(jnp.bfloat16)

    loss[...] = pltpu.roll(loss[...], (128 - 8 * (at[3] % 16)) % 128, 1)


def grad_passages(ids, own, at, q, parts):
    shapes = [jax.ShapeDtypeStruct((size, BLK, 128), jnp.bfloat16) for _, size in PIECES]
    return pl.pallas_call(
        grad_p_kernel,
        in_specs=[SMEM] * 3 + [VMEM] * 9,
        out_specs=[VMEM] * 8,
        out_shape=shapes + [jax.ShapeDtypeStruct((BLK // 8, 128), jnp.float32)],
        scratch_shapes=[
            pltpu.VMEM((STEP // 2, BLK // 8, 16, 128), jnp.bfloat16),
            pltpu.VMEM((PAIRS, BLK, 128), jnp.float32),
        ],
        **params(20, 20 * MIB),
        name="grad_passages",
    )(ids, own, at, q, *parts)


def grad_q_kernel(ids, own, at, p, *refs):
    parts, out, wv, total = refs[:8], *refs[8:]
    clear(total)
    for n in range(2):
        start, spots = weight_spots(at, n, parts)

        def use(k, tile):
            total[own[start + k]] += jnp.dot(
                tile, p[ids[start + k]], preferred_element_type=jnp.float32
            )

        for_pairs(spots, wv, use)

    @pl.loop(0, total.shape[0] // 4)
    def _(n):
        for m in range(4):
            out[4 * n + m] = total[4 * n + m].astype(jnp.bfloat16)


def grad_queries(ids, own, at, p, parts):
    nblk = p.shape[0] // 4
    return pl.pallas_call(
        grad_q_kernel,
        in_specs=[SMEM] * 3 + [VMEM] * 9,
        out_specs=VMEM,
        out_shape=jax.ShapeDtypeStruct((nblk, BLK, 128), jnp.bfloat16),
        scratch_shapes=[
            pltpu.VMEM((STEP // 2, BLK // 8, 16, 128), jnp.bfloat16),
            pltpu.VMEM((nblk, BLK, 128), jnp.float32),
        ],
        **params(14, 20 * MIB),
        name="grad_queries",
    )(ids, own, at, p, *parts)


def join_kernel(kept, *refs):
    terms, out, outv, sems = refs[:4], *refs[4:]
    half = kept.shape[0] // 2
    copies = []
    for h in range(2):
        part = slice(half * h, half * h + half)

        @pl.loop(0, half // 4)
        def _(n):
            for e in range(4):
                value = kept[half * h + 4 * n + e].astype(jnp.float32)
                for m in (2 * h, 2 * h + 1):
                    value = value + terms[m][4 * n + e].astype(jnp.float32)
                outv[half * h + 4 * n + e] = value.astype(outv.dtype)

        copies.append(pltpu.make_async_copy(outv.at[part], out.at[part], sems.at[h]))
        copies[h].start()
    for copy in copies:
        copy.wait()


def join(kept, low, high):
    return pl.pallas_call(
        join_kernel,
        in_specs=[VMEM] * 5,
        out_specs=ANY,
        out_shape=jax.ShapeDtypeStruct(kept.shape, kept.dtype),
        scratch_shapes=[pltpu.VMEM(kept.shape, kept.dtype), pltpu.SemaphoreType.DMA((2,))],
        **params(6, 8 * MIB),
        name="join",
    )(kept, *low, *high)


def along(axis, delta):
    if axis == "z":
        number = lax.axis_size("grp")
        perm = [(i, (i + delta) % number) for i in range(number)]
        return lambda v: lax.ppermute(v, "grp", perm)

    def target(d):
        x, y, core = d // 8, d // 2 % 4, d % 2
        if axis == "core":
            core = 1 - core
        elif (axis == "first") == (core == 0):
            x = (x + delta) % 4
        else:
            y = (y + delta) % 4
        return x * 8 + y * 2 + core

    perm = [(d, target(d)) for d in range(32)]
    return lambda v: lax.ppermute(v, "dev", perm)


def add(*terms):
    total = terms[0].astype(jnp.float32)
    for term in terms[1:]:
        total = total + term.astype(jnp.float32)
    return total.astype(terms[0].dtype)


def ring_terms(axis, rel1, rel2, rel3):
    up, down = along(axis, 1), along(axis, -1)
    from_below = up(rel2[0])
    from_above = down(rel2[1])
    below1 = up(rel1[1])
    above0 = down(rel3[0])
    below0 = up(add(rel1[0], from_below))
    above1 = down(add(rel3[1], from_above))
    return (below0, above0), (below1, above1)


def scatter_scores(outs):
    halves = ring_terms("first", outs[0:2], outs[2:4], outs[4:6])
    sums = [outs[6][n] + halves[n // 2][0][n % 2] + halves[n // 2][1][n % 2] for n in range(4)]
    got = [along("second", n)(sums[n]) for n in (1, 2, 3)]
    return sums[0] + got[0] + got[1] + got[2]


def gather_weights(v):
    got = {3: along("first", 1)(v), 1: along("first", -1)(v), 2: along("first", 2)(v)}
    near = jnp.stack([v, got[1], got[2], got[3]])
    up, down, flip = along("second", 1), along("second", -1), along("core", 1)
    below, above = up(near), down(near)
    side = [near, below, above, down(above)]
    return side + [flip(w) for w in side]


def per_device(queries, passages, pairs, counts, positives):
    ndev = lax.axis_size("dev")
    ngrp = lax.axis_size("grp")
    width = queries.shape[1]
    maxp = pairs.shape[1]
    me = lax.axis_index("dev")
    z = lax.axis_index("grp")
    chip, core = me // 2, me % 2
    at = jnp.stack([core, chip // 4, chip % 4, me, chip]).astype(jnp.int32)

    def exchange(v):
        return lax.all_to_all(v, "dev", 0, 0, tiled=True)

    up, down, flip = along("z", 1), along("z", -1), along("core", 1)
    halves = slice(0, HALF), slice(HALF, BLK)
    low, high = [exchange(by_features(passages, rows)) for rows in halves]
    above0, below0 = down(low), up(low)
    q_tiles = by_features(queries, slice(0, BLK), positives.reshape(1, BLK))
    q_tiles, late, *_ = lax.optimization_barrier((q_tiles, high, above0, below0))
    above1, below1 = down(late), up(late)
    last0, last1, *_ = lax.optimization_barrier((above0, below1, above1))
    far0, far1 = down(last0), up(last1)
    pieces = [low, high, above0, above1, far0, far1, below0, below1]
    others = [flip(v) for v in pieces]
    q_own = exchange(q_tiles)
    q = [q_own, flip(q_own)]

    group = counts[0]
    block = jnp.arange(ndev, dtype=jnp.int32)
    ends = jnp.sum(jnp.where(block[None, :] <= block[:, None], group[None, :], 0), axis=1)
    starts = ends - group
    t = jnp.arange(PAIRS, dtype=jnp.int32)
    own = jnp.sum((ends[None, :] <= t[:, None]).astype(jnp.int32), axis=1)
    start = jnp.sum(jnp.where(block[None, :] == own[:, None], starts[None, :], 0), axis=1)
    entry = own * maxp + t - start
    slot = jnp.arange(ndev * maxp, dtype=jnp.int32)
    ids = jnp.sum(jnp.where(slot[None, :] == entry[:, None], pairs.reshape(1, -1), 0), axis=1)
    ids = (ids + (ngrp - z) * ndev) % (ngrp * ndev)
    spare = jnp.full((128 - ndev,), 2 * PAIRS, jnp.int32)
    lists = jnp.stack([jnp.concatenate([v, spare]) for v in (ends, starts)] * 4)

    scores = scatter_scores(partial_scores(ids, own, at, q, pieces + others))
    weights = softmax_weights(at, (scores, flip(scores)), lists, q_own, width ** (-0.5))
    parts = gather_weights(weights)
    q_own, mine = lax.optimization_barrier((q_own, place(pieces)))
    *g, lines = grad_passages(ids, own, at, q_own, parts)

    low, high = ring_terms("z", g[1:3], g[3:5], g[5:7])
    q_rows = by_rows(exchange(grad_queries(ids, own, at, mine, parts)))
    p_rows = by_rows(exchange(join(g[0], low, high)))
    return lines[:, 0:8].reshape(BLK), q_rows, p_rows


def solution(mesh):
    placed = (
        P(("grp", "dev"), None),
        P(("grp", "dev"), None),
        P("grp", None),
        P("grp", None),
        P(("grp", "dev")),
    )
    return jax.shard_map(
        per_device,
        mesh=mesh,
        in_specs=placed,
        out_specs=(P(("grp", "dev")), P(("grp", "dev"), None), P(("grp", "dev"), None)),
        check_vma=False,
    )
```

```python
import functools

import jax
import jax.numpy as jnp
from jax import lax
from jax.experimental import pallas as pl
from jax.experimental.pallas import tpu as pltpu
from jax.sharding import PartitionSpec as P

BLK = 128
HALF = BLK // 2
PAIRS = 128
PART = PAIRS // 2
ROWS = 8 * PART
TAIL = 16
STEP = 8
PARTS = 8
MIB = 1024 * 1024
SMEM = pl.BlockSpec(memory_space=pltpu.SMEM)
ANY = pl.BlockSpec(memory_space=pl.ANY)
VMEM = pl.BlockSpec(memory_space=pltpu.VMEM)


def params(limit, moved, flops=0):
    cost = pl.CostEstimate(flops=flops, bytes_accessed=moved, transcendentals=0)
    limit = pltpu.CompilerParams(vmem_limit_bytes=limit * MIB)
    return dict(compiler_params=limit, cost_estimate=cost)


def run_copies(copies):
    for copy in copies:
        copy.start()
    for copy in copies:
        copy.wait()


def pack_kernel(x, *refs):
    *outs, xv, outv, marks, sems = refs
    extra = outv.shape[1] - BLK
    if extra:
        run_copies([pltpu.make_async_copy(outs[0], marks, sems.at[0])])
        outs = outs[1:]
        tile = jnp.broadcast_to(marks[...].astype(jnp.float32), (extra, 128)).astype(jnp.bfloat16)
    width = x.shape[1]
    number = outv.shape[0] // PARTS
    tall = outv.shape[1] // len(outs)
    loads, stores = [], []
    for n in range(PARTS):
        cols = slice(n * width // PARTS, (n + 1) * width // PARTS)
        loads.append(pltpu.make_async_copy(x.at[:, cols], xv.at[:, cols], sems.at[n]))
        part = slice(n * number, (n + 1) * number)
        for m, out in enumerate(outs):
            source = outv.at[part, m * tall : (m + 1) * tall, :]
            sem = sems.at[PARTS * (1 + m) + n]
            stores.append(pltpu.make_async_copy(source, out.at[part], sem))
    for copy in loads:
        copy.start()
    for n in range(PARTS):
        loads[n].wait()
        for m in range(n * number, (n + 1) * number):
            outv[m, 0:BLK, :] = xv[:, 128 * m : 128 * m + 128].astype(jnp.bfloat16)
            if extra:
                outv[m, BLK:, :] = tile
        for copy in stores[n * len(outs) : (n + 1) * len(outs)]:
            copy.start()
    for copy in stores:
        copy.wait()


def by_features(x, pos=None):
    number = x.shape[1] // 128
    tall = BLK + (0 if pos is None else 16)
    shapes = [(number, HALF, 128)] * 2 if pos is None else [(number, tall, 128)]
    given = (x,) if pos is None else (x, pos)
    return pl.pallas_call(
        pack_kernel,
        in_specs=[ANY] * len(given),
        out_specs=[ANY] * len(shapes),
        out_shape=[jax.ShapeDtypeStruct(s, jnp.bfloat16) for s in shapes],
        scratch_shapes=[
            pltpu.VMEM(x.shape, x.dtype),
            pltpu.VMEM((number, tall, 128), jnp.bfloat16),
            pltpu.VMEM((1, BLK), jnp.int32),
            pltpu.SemaphoreType.DMA((3 * PARTS,)),
        ],
        **params(56 if pos is None else 5, 5 * MIB),
        name="pack",
    )(*given)


def unpack_kernel(x, out, outv, sems):
    copies = []
    for n in range(PARTS):
        rows = slice(n * BLK // PARTS, (n + 1) * BLK // PARTS)
        for m in range(x.shape[0]):
            outv[rows, 128 * m : 128 * m + 128] = x[m, rows, :].astype(jnp.float32)
        copies.append(pltpu.make_async_copy(outv.at[rows, :], out.at[rows, :], sems.at[n]))
        copies[n].start()
    for copy in copies:
        copy.wait()


def by_rows(x):
    number = x.shape[0]
    return pl.pallas_call(
        unpack_kernel,
        in_specs=[VMEM],
        out_specs=ANY,
        out_shape=jax.ShapeDtypeStruct((BLK, number * 128), jnp.float32),
        scratch_shapes=[
            pltpu.VMEM((BLK, number * 128), jnp.float32),
            pltpu.SemaphoreType.DMA((PARTS,)),
        ],
        **params(5, 8 * MIB),
        name="unpack",
    )(x)


PIECES = ((0, 32), (32, 16), (48, 16), (64, 16), (80, 16), (96, 16), (112, 16))


def place_kernel(*refs):
    *pieces, out, sems = refs
    copies = []
    for n, piece in enumerate(pieces):
        target = out.at[32 * (n // 2) : 32 * (n // 2) + 32, HALF * (n % 2) : HALF * (n % 2) + HALF, :]
        copies.append(pltpu.make_async_copy(piece, target, sems.at[n]))
    run_copies(copies)


def place(pieces):
    return pl.pallas_call(
        place_kernel,
        in_specs=[ANY] * 8,
        out_specs=ANY,
        out_shape=jax.ShapeDtypeStruct((4 * 32, BLK, 128), pieces[0].dtype),
        scratch_shapes=[pltpu.SemaphoreType.DMA((8,))],
        **params(1, 12 * MIB),
        name="place",
    )(*pieces)


def chip_at(at, core, lead, other):
    rx = jnp.where(core == 0, lead, other)
    ry = jnp.where(core == 0, other, lead)
    return ((at[1] + rx) % 4) * 4 + (at[2] + ry) % 4


def score_kernel(ids, own, at, q_own, q_sib, *refs):
    pieces, outs, (pv, sv) = (refs[:8], refs[8:16]), refs[16:23], refs[23:]
    core = at[0]
    spots = [
        (lead, other, chip_at(at, core, lead, other)) for lead in range(4) for other in range(4)
    ]

    @pl.loop(0, PART // STEP)
    def _(step):
        for u in range(STEP):
            there = ids[PART * core + step * STEP + u]
            for rel in range(4):

                @pl.when(there // 32 == rel)
                def _():
                    for side in range(2):
                        for h in range(2):
                            rows = slice(HALF * h, HALF * h + HALF)
                            lanes = slice(128 * side, 128 * side + 128)
                            pv[u, rows, lanes] = pieces[side][2 * rel + h][there % 32]

        for u in range(STEP):
            here = own[PART * core + step * STEP + u]
            left = jnp.concatenate([q_own[here, 0:BLK, :], q_sib[here, 0:BLK, :]], axis=1)
            tile = lax.dot_general(
                left, pv[u], (((1,), (1,)), ((), ())), preferred_element_type=jnp.float32
            )
            sv[u] = tile.reshape(BLK // 8, 8, 128)
        for u in range(STEP):
            where = pl.ds(pl.multiple_of(8 * (step * STEP + u), 8), 8)
            for lead, other, chip in spots:
                if lead == 0:
                    outs[6][other, where, :] = sv[u, chip]
                else:
                    outs[2 * lead - 2 + other // 2][other % 2, where, :] = sv[u, chip]


def partial_scores(ids, own, at, q, pieces):
    shapes = [(2, ROWS, 128)] * 6 + [(4, ROWS, 128)]
    return pl.pallas_call(
        score_kernel,
        in_specs=[SMEM] * 3 + [VMEM] * 18,
        out_specs=[VMEM] * 7,
        out_shape=[jax.ShapeDtypeStruct(s, jnp.float32) for s in shapes],
        scratch_shapes=[
            pltpu.VMEM((STEP, BLK, 2 * 128), jnp.bfloat16),
            pltpu.VMEM((STEP, BLK // 8, 8, 128), jnp.float32),
        ],
        **params(18, 20 * MIB),
        name="partial_scores",
    )(ids, own, at, *q, *pieces)


def softmax_kernel(at, x_own, x_sib, listv, q, out, *, scale):
    core = at[0]
    row = lax.broadcasted_iota(jnp.int32, (2 * ROWS, 1), 0)
    side = row // ROWS
    t = PART * (core + side - 2 * core * side) + (row & (ROWS - 1)) // 8
    r = row & 7
    lane = lax.broadcasted_iota(jnp.int32, (2 * ROWS, 128), 1)
    own = jnp.sum((listv[0:1, :] <= t).astype(jnp.int32), axis=1, keepdims=True)
    key = own * 8 + r

    x = jnp.concatenate([x_own[...], x_sib[...]], axis=0) * scale
    high = jnp.max(x, axis=1, keepdims=True)
    part = jnp.sum(jnp.exp(x - high), axis=1, keepdims=True)
    lines = jnp.where(lane == 0, high, jnp.where(lane == 1, part, key.astype(jnp.float32))).T
    high, part, keys = lines[0:1], lines[1:2], lines[2:3]

    x, t, r, lane, own, key = [v[:ROWS] for v in (x, t, r, lane, own, key)]
    same = key.astype(jnp.float32) == keys
    top = jnp.max(jnp.where(same, high, -jnp.inf), axis=1, keepdims=True)
    total = jnp.where(same, part * jnp.exp(high - top), 0.0)
    lse = top + jnp.log(jnp.sum(total, axis=1, keepdims=True))

    block = lane == own
    first = t == jnp.sum(jnp.where(block, listv[1:2, :], 0), axis=1, keepdims=True)
    marks = jnp.max(q[:, BLK:, :].astype(jnp.float32), axis=1)
    marks = jnp.concatenate([marks, jnp.zeros((128 - marks.shape[0], 128), jnp.float32)], axis=0)
    listed = jnp.dot(
        block.astype(jnp.bfloat16), marks.astype(jnp.bfloat16), preferred_element_type=jnp.float32
    )
    target = jnp.sum(jnp.where(lane == at[4] * 8 + r, listed, 0.0), axis=1, keepdims=True)
    hit = first & (lane == target.astype(jnp.int32))
    weights = jnp.exp(x - lse) - hit.astype(jnp.float32)
    out[0:ROWS, :] = weights.astype(jnp.bfloat16)

    loss = lse - jnp.sum(jnp.where(hit, x, 0.0), axis=1, keepdims=True)
    line = lax.broadcasted_iota(jnp.int32, (TAIL, 128), 0)
    tail = jnp.zeros((TAIL, 128), jnp.float32)
    for h in range(2):
        here = first & (lane + 128 * h == key)
        rest = jnp.sum(jnp.where(here, loss, 0.0), axis=0, keepdims=True)
        for n in range(3):
            term = rest.astype(jnp.bfloat16).astype(jnp.float32)
            tail = jnp.where(line == 3 * h + n, term, tail)
            rest = rest - term
    out[ROWS:, :] = tail.astype(jnp.bfloat16)


def softmax_weights(at, terms, lists, q, scale):
    return pl.pallas_call(
        functools.partial(softmax_kernel, scale=scale),
        in_specs=[SMEM] + [VMEM] * 4,
        out_specs=VMEM,
        out_shape=jax.ShapeDtypeStruct((ROWS + TAIL, 128), jnp.bfloat16),
        **params(16, 8 * MIB),
        name="softmax_weights",
    )(at, *terms, lists, q)


GATHERED = tuple((other, (0, 1, 2, 3)) for other in (0, 3, 1, 2))


def weight_spots(at, n, parts):
    side = jnp.where(at[0] == n, 0, 1)
    spots = []
    for m, (other, leads) in enumerate(GATHERED):
        for e, lead in enumerate(leads):
            spots.append((parts[len(GATHERED) * n + m], e, chip_at(at, side, lead, other)))
    return side * PART, spots


def for_pairs(spots, wv, use):
    @pl.loop(0, PART // STEP)
    def _(step):
        for v in range(STEP // 2):
            where = pl.ds(pl.multiple_of(8 * STEP * step + 16 * v, 16), 16)
            for piece, e, chip in spots:
                wv[v, chip] = piece[e, where, :]
            two = wv[v].astype(jnp.float32)
            for o in range(2):
                tile = two[:, 8 * o : 8 * o + 8, :].reshape(BLK, 128).astype(jnp.bfloat16)
                use(step * STEP + 2 * v + o, tile)


def clear(total):
    @pl.loop(0, total.shape[0] // 4)
    def _(n):
        for m in range(4):
            total[4 * n + m] = jnp.zeros((BLK, 128), jnp.float32)


def grad_p_kernel(ids, own, at, q, *refs):
    parts, outs, loss, wv, total = refs[:8], refs[8:15], *refs[15:]
    clear(total)
    mine = lax.broadcasted_iota(jnp.int32, (TAIL, 128), 0) // 3 == at[3] // 16
    for n in range(2):
        start, spots = weight_spots(at, n, parts)
        for piece, e, chip in spots:
            tail = jnp.where(mine, piece[e, ROWS:, :].astype(jnp.float32), 0.0)
            line = jnp.sum(tail, axis=0, keepdims=True)
            row = pl.ds(chip, 1)
            loss[row, :] = line if n == 0 else loss[row, :] + line

        def use(k, tile):
            total[ids[start + k]] += lax.dot_general(
                tile,
                q[own[start + k], 0:BLK, :],
                (((0,), (0,)), ((), ())),
                preferred_element_type=jnp.float32,
            )

        for_pairs(spots, wv, use)

    @pl.loop(0, 16)
    def _(n):
        for m, (first, size) in enumerate(PIECES):
            for e in range(size // 16):
                outs[m][16 * e + n] = total[first + 16 * e + n].astype(jnp.bfloat16)

    loss[...] = pltpu.roll(loss[...], (128 - 8 * (at[3] % 16)) % 128, 1)


def grad_passages(ids, own, at, q, parts):
    shapes = [jax.ShapeDtypeStruct((size, BLK, 128), jnp.bfloat16) for _, size in PIECES]
    return pl.pallas_call(
        grad_p_kernel,
        in_specs=[SMEM] * 3 + [VMEM] * 9,
        out_specs=[VMEM] * 8,
        out_shape=shapes + [jax.ShapeDtypeStruct((BLK // 8, 128), jnp.float32)],
        scratch_shapes=[
            pltpu.VMEM((STEP // 2, BLK // 8, 16, 128), jnp.bfloat16),
            pltpu.VMEM((PAIRS, BLK, 128), jnp.float32),
        ],
        **params(20, 20 * MIB),
        name="grad_passages",
    )(ids, own, at, q, *parts)


def grad_q_kernel(ids, own, at, p, *refs):
    parts, out, wv, total = refs[:8], *refs[8:]
    clear(total)
    for n in range(2):
        start, spots = weight_spots(at, n, parts)

        def use(k, tile):
            total[own[start + k]] += jnp.dot(
                tile, p[ids[start + k]], preferred_element_type=jnp.float32
            )

        for_pairs(spots, wv, use)

    @pl.loop(0, total.shape[0] // 4)
    def _(n):
        for m in range(4):
            out[4 * n + m] = total[4 * n + m].astype(jnp.bfloat16)


def grad_queries(ids, own, at, p, parts):
    nblk = p.shape[0] // 4
    return pl.pallas_call(
        grad_q_kernel,
        in_specs=[SMEM] * 3 + [VMEM] * 9,
        out_specs=VMEM,
        out_shape=jax.ShapeDtypeStruct((nblk, BLK, 128), jnp.bfloat16),
        scratch_shapes=[
            pltpu.VMEM((STEP // 2, BLK // 8, 16, 128), jnp.bfloat16),
            pltpu.VMEM((nblk, BLK, 128), jnp.float32),
        ],
        **params(14, 20 * MIB),
        name="grad_queries",
    )(ids, own, at, p, *parts)


def join_kernel(kept, *refs):
    terms, out, outv, sems = refs[:4], *refs[4:]
    half = kept.shape[0] // 2
    copies = []
    for h in range(2):
        part = slice(half * h, half * h + half)

        @pl.loop(0, half // 4)
        def _(n):
            for e in range(4):
                value = kept[half * h + 4 * n + e].astype(jnp.float32)
                for m in (2 * h, 2 * h + 1):
                    value = value + terms[m][4 * n + e].astype(jnp.float32)
                outv[half * h + 4 * n + e] = value.astype(outv.dtype)

        copies.append(pltpu.make_async_copy(outv.at[part], out.at[part], sems.at[h]))
        copies[h].start()
    for copy in copies:
        copy.wait()


def join(kept, low, high):
    return pl.pallas_call(
        join_kernel,
        in_specs=[VMEM] * 5,
        out_specs=ANY,
        out_shape=jax.ShapeDtypeStruct(kept.shape, kept.dtype),
        scratch_shapes=[pltpu.VMEM(kept.shape, kept.dtype), pltpu.SemaphoreType.DMA((2,))],
        **params(6, 8 * MIB),
        name="join",
    )(kept, *low, *high)


def along(axis, delta):
    if axis == "z":
        number = lax.axis_size("grp")
        perm = [(i, (i + delta) % number) for i in range(number)]
        return lambda v: lax.ppermute(v, "grp", perm)

    def target(d):
        x, y, core = d // 8, d // 2 % 4, d % 2
        if axis == "core":
            core = 1 - core
        elif (axis == "first") == (core == 0):
            x = (x + delta) % 4
        else:
            y = (y + delta) % 4
        return x * 8 + y * 2 + core

    perm = [(d, target(d)) for d in range(32)]
    return lambda v: lax.ppermute(v, "dev", perm)


def add(*terms):
    total = terms[0].astype(jnp.float32)
    for term in terms[1:]:
        total = total + term.astype(jnp.float32)
    return total.astype(terms[0].dtype)


def ring_terms(axis, rel1, rel2, rel3):
    up, down = along(axis, 1), along(axis, -1)
    from_below = up(rel2[0])
    from_above = down(rel2[1])
    below1 = up(rel1[1])
    above0 = down(rel3[0])
    below0 = up(add(rel1[0], from_below))
    above1 = down(add(rel3[1], from_above))
    return (below0, above0), (below1, above1)


def scatter_scores(outs):
    halves = ring_terms("first", outs[0:2], outs[2:4], outs[4:6])
    sums = [outs[6][n] + halves[n // 2][0][n % 2] + halves[n // 2][1][n % 2] for n in range(4)]
    got = [along("second", n)(sums[n]) for n in (2, 3, 1)]
    return sums[0] + got[0] + got[1] + got[2]


def gather_weights(v):
    got = {2: along("first", 2)(v), 1: along("first", -1)(v), 3: along("first", 1)(v)}
    near = jnp.stack([v, got[1], got[2], got[3]])
    up, down, flip = along("second", 1), along("second", -1), along("core", 1)
    below, above = up(near), down(near)
    side = [near, below, above, down(above)]
    return side + [flip(w) for w in side]


def per_device(queries, passages, pairs, counts, positives):
    ndev = lax.axis_size("dev")
    ngrp = lax.axis_size("grp")
    width = queries.shape[1]
    maxp = pairs.shape[1]
    me = lax.axis_index("dev")
    z = lax.axis_index("grp")
    chip, core = me // 2, me % 2
    at = jnp.stack([core, chip // 4, chip % 4, me, chip]).astype(jnp.int32)

    def exchange(v):
        return lax.all_to_all(v, "dev", 0, 0, tiled=True)

    up, down, flip = along("z", 1), along("z", -1), along("core", 1)
    low, high = [exchange(v) for v in by_features(passages)]
    above0, below0 = down(low), up(low)
    q_tiles = by_features(queries, positives.reshape(1, BLK))[0]
    late, *_ = lax.optimization_barrier((high, above0, below0))
    above1, below1 = down(late), up(late)
    q_tiles, *_ = lax.optimization_barrier((q_tiles, above1, below1))
    last0, last1, *_ = lax.optimization_barrier((above0, below1, above1))
    far0, far1 = down(last0), up(last1)
    pieces = [low, high, above0, above1, far0, far1, below0, below1]
    others = [flip(v) for v in pieces]
    q_own = exchange(q_tiles)
    q = [q_own, flip(q_own)]

    group = counts[0]
    block = jnp.arange(ndev, dtype=jnp.int32)
    ends = jnp.sum(jnp.where(block[None, :] <= block[:, None], group[None, :], 0), axis=1)
    starts = ends - group
    t = jnp.arange(PAIRS, dtype=jnp.int32)
    own = jnp.sum((ends[None, :] <= t[:, None]).astype(jnp.int32), axis=1)
    start = jnp.sum(jnp.where(block[None, :] == own[:, None], starts[None, :], 0), axis=1)
    entry = own * maxp + t - start
    slot = jnp.arange(ndev * maxp, dtype=jnp.int32)
    ids = jnp.sum(jnp.where(slot[None, :] == entry[:, None], pairs.reshape(1, -1), 0), axis=1)
    ids = (ids + (ngrp - z) * ndev) % (ngrp * ndev)
    spare = jnp.full((128 - ndev,), 2 * PAIRS, jnp.int32)
    lists = jnp.stack([jnp.concatenate([v, spare]) for v in (ends, starts)] * 4)

    scores = scatter_scores(partial_scores(ids, own, at, q, pieces + others))
    weights = softmax_weights(at, (scores, flip(scores)), lists, q_own, width ** (-0.5))
    parts = gather_weights(weights)
    q_own, mine = lax.optimization_barrier((q_own, place(pieces)))
    *g, lines = grad_passages(ids, own, at, q_own, parts)

    low, high = ring_terms("z", g[1:3], g[3:5], g[5:7])
    q_rows = by_rows(exchange(grad_queries(ids, own, at, mine, parts)))
    p_rows = by_rows(exchange(join(g[0], low, high)))
    return lines[:, 0:8].reshape(BLK), q_rows, p_rows


def solution(mesh):
    placed = (
        P(("grp", "dev"), None),
        P(("grp", "dev"), None),
        P("grp", None),
        P("grp", None),
        P(("grp", "dev")),
    )
    return jax.shard_map(
        per_device,
        mesh=mesh,
        in_specs=placed,
        out_specs=(P(("grp", "dev")), P(("grp", "dev"), None), P(("grp", "dev"), None)),
        check_vma=False,
    )
```

```python
import functools

import jax
import jax.numpy as jnp
from jax import lax
from jax.experimental import pallas as pl
from jax.experimental.pallas import tpu as pltpu
from jax.sharding import PartitionSpec as P

BLK = 128
HALF = BLK // 2
PAIRS = 128
PART = PAIRS // 2
ROWS = 8 * PART
TAIL = 16
STEP = 8
PARTS = 8
MIB = 1024 * 1024
SMEM = pl.BlockSpec(memory_space=pltpu.SMEM)
ANY = pl.BlockSpec(memory_space=pl.ANY)
VMEM = pl.BlockSpec(memory_space=pltpu.VMEM)


def params(limit, moved, flops=0):
    cost = pl.CostEstimate(flops=flops, bytes_accessed=moved, transcendentals=0)
    limit = pltpu.CompilerParams(vmem_limit_bytes=limit * MIB)
    return dict(compiler_params=limit, cost_estimate=cost)


def run_copies(copies):
    for copy in copies:
        copy.start()
    for copy in copies:
        copy.wait()


def pack_kernel(x, *refs):
    *outs, xv, outv, marks, sems = refs
    extra = outv.shape[1] - BLK
    if extra:
        run_copies([pltpu.make_async_copy(outs[0], marks, sems.at[0])])
        outs = outs[1:]
        tile = jnp.broadcast_to(marks[...].astype(jnp.float32), (extra, 128)).astype(jnp.bfloat16)
    width = x.shape[1]
    number = outv.shape[0] // PARTS
    tall = outv.shape[1] // len(outs)
    loads, stores = [], []
    for n in range(PARTS):
        cols = slice(n * width // PARTS, (n + 1) * width // PARTS)
        loads.append(pltpu.make_async_copy(x.at[:, cols], xv.at[:, cols], sems.at[n]))
        part = slice(n * number, (n + 1) * number)
        for m, out in enumerate(outs):
            source = outv.at[part, m * tall : (m + 1) * tall, :]
            sem = sems.at[PARTS * (1 + m) + n]
            stores.append(pltpu.make_async_copy(source, out.at[part], sem))
    for copy in loads:
        copy.start()
    for n in range(PARTS):
        loads[n].wait()
        for m in range(n * number, (n + 1) * number):
            outv[m, 0:BLK, :] = xv[:, 128 * m : 128 * m + 128].astype(jnp.bfloat16)
            if extra:
                outv[m, BLK:, :] = tile
        for copy in stores[n * len(outs) : (n + 1) * len(outs)]:
            copy.start()
    for copy in stores:
        copy.wait()


def by_features(x, pos=None):
    number = x.shape[1] // 128
    tall = BLK + (0 if pos is None else 16)
    shapes = [(number, HALF, 128)] * 2 if pos is None else [(number, tall, 128)]
    given = (x,) if pos is None else (x, pos)
    return pl.pallas_call(
        pack_kernel,
        in_specs=[ANY] * len(given),
        out_specs=[ANY] * len(shapes),
        out_shape=[jax.ShapeDtypeStruct(s, jnp.bfloat16) for s in shapes],
        scratch_shapes=[
            pltpu.VMEM(x.shape, x.dtype),
            pltpu.VMEM((number, tall, 128), jnp.bfloat16),
            pltpu.VMEM((1, BLK), jnp.int32),
            pltpu.SemaphoreType.DMA((3 * PARTS,)),
        ],
        **params(56 if pos is None else 5, 5 * MIB),
        name="pack",
    )(*given)


def unpack_kernel(x, out, outv, sems):
    copies = []
    for n in range(PARTS):
        rows = slice(n * BLK // PARTS, (n + 1) * BLK // PARTS)
        for m in range(x.shape[0]):
            outv[rows, 128 * m : 128 * m + 128] = x[m, rows, :].astype(jnp.float32)
        copies.append(pltpu.make_async_copy(outv.at[rows, :], out.at[rows, :], sems.at[n]))
        copies[n].start()
    for copy in copies:
        copy.wait()


def by_rows(x):
    number = x.shape[0]
    return pl.pallas_call(
        unpack_kernel,
        in_specs=[VMEM],
        out_specs=ANY,
        out_shape=jax.ShapeDtypeStruct((BLK, number * 128), jnp.float32),
        scratch_shapes=[
            pltpu.VMEM((BLK, number * 128), jnp.float32),
            pltpu.SemaphoreType.DMA((PARTS,)),
        ],
        **params(5, 8 * MIB),
        name="unpack",
    )(x)


PIECES = ((0, 32), (32, 16), (48, 16), (64, 16), (80, 16), (96, 16), (112, 16))


def place_kernel(*refs):
    *pieces, out, sems = refs
    copies = []
    for n, piece in enumerate(pieces):
        target = out.at[32 * (n // 2) : 32 * (n // 2) + 32, HALF * (n % 2) : HALF * (n % 2) + HALF, :]
        copies.append(pltpu.make_async_copy(piece, target, sems.at[n]))
    run_copies(copies)


def place(pieces):
    return pl.pallas_call(
        place_kernel,
        in_specs=[ANY] * 8,
        out_specs=ANY,
        out_shape=jax.ShapeDtypeStruct((4 * 32, BLK, 128), pieces[0].dtype),
        scratch_shapes=[pltpu.SemaphoreType.DMA((8,))],
        **params(1, 12 * MIB),
        name="place",
    )(*pieces)


def chip_at(at, core, lead, other):
    rx = jnp.where(core == 0, lead, other)
    ry = jnp.where(core == 0, other, lead)
    return ((at[1] + rx) % 4) * 4 + (at[2] + ry) % 4


def score_kernel(ids, own, at, q_own, q_sib, *refs):
    pieces, outs, (pv, sv) = (refs[:8], refs[8:16]), refs[16:23], refs[23:]
    core = at[0]
    spots = [
        (lead, other, chip_at(at, core, lead, other)) for lead in range(4) for other in range(4)
    ]

    @pl.loop(0, PART // STEP)
    def _(step):
        for u in range(STEP):
            there = ids[PART * core + step * STEP + u]
            for rel in range(4):

                @pl.when(there // 32 == rel)
                def _():
                    for side in range(2):
                        for h in range(2):
                            rows = slice(HALF * h, HALF * h + HALF)
                            lanes = slice(128 * side, 128 * side + 128)
                            pv[u, rows, lanes] = pieces[side][2 * rel + h][there % 32]

        for u in range(STEP):
            here = own[PART * core + step * STEP + u]
            left = jnp.concatenate([q_own[here, 0:BLK, :], q_sib[here, 0:BLK, :]], axis=1)
            tile = lax.dot_general(
                left, pv[u], (((1,), (1,)), ((), ())), preferred_element_type=jnp.float32
            )
            sv[u] = tile.reshape(BLK // 8, 8, 128)
        for u in range(STEP):
            where = pl.ds(pl.multiple_of(8 * (step * STEP + u), 8), 8)
            for lead, other, chip in spots:
                if lead == 0:
                    outs[6][other, where, :] = sv[u, chip]
                else:
                    outs[2 * lead - 2 + other // 2][other % 2, where, :] = sv[u, chip]


def partial_scores(ids, own, at, q, pieces):
    shapes = [(2, ROWS, 128)] * 6 + [(4, ROWS, 128)]
    return pl.pallas_call(
        score_kernel,
        in_specs=[SMEM] * 3 + [VMEM] * 18,
        out_specs=[VMEM] * 7,
        out_shape=[jax.ShapeDtypeStruct(s, jnp.float32) for s in shapes],
        scratch_shapes=[
            pltpu.VMEM((STEP, BLK, 2 * 128), jnp.bfloat16),
            pltpu.VMEM((STEP, BLK // 8, 8, 128), jnp.float32),
        ],
        **params(18, 20 * MIB),
        name="partial_scores",
    )(ids, own, at, *q, *pieces)


def softmax_kernel(at, x_own, x_sib, listv, q, out, *, scale):
    core = at[0]
    row = lax.broadcasted_iota(jnp.int32, (2 * ROWS, 1), 0)
    side = row // ROWS
    t = PART * (core + side - 2 * core * side) + (row & (ROWS - 1)) // 8
    r = row & 7
    lane = lax.broadcasted_iota(jnp.int32, (2 * ROWS, 128), 1)
    own = jnp.sum((listv[0:1, :] <= t).astype(jnp.int32), axis=1, keepdims=True)
    key = own * 8 + r

    x = jnp.concatenate([x_own[...], x_sib[...]], axis=0) * scale
    high = jnp.max(x, axis=1, keepdims=True)
    part = jnp.sum(jnp.exp(x - high), axis=1, keepdims=True)
    lines = jnp.where(lane == 0, high, jnp.where(lane == 1, part, key.astype(jnp.float32))).T
    high, part, keys = lines[0:1], lines[1:2], lines[2:3]

    x, t, r, lane, own, key = [v[:ROWS] for v in (x, t, r, lane, own, key)]
    same = key.astype(jnp.float32) == keys
    top = jnp.max(jnp.where(same, high, -jnp.inf), axis=1, keepdims=True)
    total = jnp.where(same, part * jnp.exp(high - top), 0.0)
    lse = top + jnp.log(jnp.sum(total, axis=1, keepdims=True))

    block = lane == own
    first = t == jnp.sum(jnp.where(block, listv[1:2, :], 0), axis=1, keepdims=True)
    marks = jnp.max(q[:, BLK:, :].astype(jnp.float32), axis=1)
    marks = jnp.concatenate([marks, jnp.zeros((128 - marks.shape[0], 128), jnp.float32)], axis=0)
    listed = jnp.dot(
        block.astype(jnp.bfloat16), marks.astype(jnp.bfloat16), preferred_element_type=jnp.float32
    )
    target = jnp.sum(jnp.where(lane == at[4] * 8 + r, listed, 0.0), axis=1, keepdims=True)
    hit = first & (lane == target.astype(jnp.int32))
    weights = jnp.exp(x - lse) - hit.astype(jnp.float32)
    out[0:ROWS, :] = weights.astype(jnp.bfloat16)

    loss = lse - jnp.sum(jnp.where(hit, x, 0.0), axis=1, keepdims=True)
    line = lax.broadcasted_iota(jnp.int32, (TAIL, 128), 0)
    tail = jnp.zeros((TAIL, 128), jnp.float32)
    for h in range(2):
        here = first & (lane + 128 * h == key)
        rest = jnp.sum(jnp.where(here, loss, 0.0), axis=0, keepdims=True)
        for n in range(3):
            term = rest.astype(jnp.bfloat16).astype(jnp.float32)
            tail = jnp.where(line == 3 * h + n, term, tail)
            rest = rest - term
    out[ROWS:, :] = tail.astype(jnp.bfloat16)


def softmax_weights(at, terms, lists, q, scale):
    return pl.pallas_call(
        functools.partial(softmax_kernel, scale=scale),
        in_specs=[SMEM] + [VMEM] * 4,
        out_specs=VMEM,
        out_shape=jax.ShapeDtypeStruct((ROWS + TAIL, 128), jnp.bfloat16),
        **params(16, 8 * MIB),
        name="softmax_weights",
    )(at, *terms, lists, q)


GATHERED = tuple((other, (0, 1, 2, 3)) for other in (0, 3, 1, 2))


def weight_spots(at, n, parts):
    side = jnp.where(at[0] == n, 0, 1)
    spots = []
    for m, (other, leads) in enumerate(GATHERED):
        for e, lead in enumerate(leads):
            spots.append((parts[len(GATHERED) * n + m], e, chip_at(at, side, lead, other)))
    return side * PART, spots


def for_pairs(spots, wv, use):
    @pl.loop(0, PART // STEP)
    def _(step):
        for v in range(STEP // 2):
            where = pl.ds(pl.multiple_of(8 * STEP * step + 16 * v, 16), 16)
            for piece, e, chip in spots:
                wv[v, chip] = piece[e, where, :]
            two = wv[v].astype(jnp.float32)
            for o in range(2):
                tile = two[:, 8 * o : 8 * o + 8, :].reshape(BLK, 128).astype(jnp.bfloat16)
                use(step * STEP + 2 * v + o, tile)


def clear(total):
    @pl.loop(0, total.shape[0] // 4)
    def _(n):
        for m in range(4):
            total[4 * n + m] = jnp.zeros((BLK, 128), jnp.float32)


def grad_p_kernel(ids, own, at, q, *refs):
    parts, outs, loss, wv, total = refs[:8], refs[8:15], *refs[15:]
    clear(total)
    mine = lax.broadcasted_iota(jnp.int32, (TAIL, 128), 0) // 3 == at[3] // 16
    for n in range(2):
        start, spots = weight_spots(at, n, parts)
        for piece, e, chip in spots:
            tail = jnp.where(mine, piece[e, ROWS:, :].astype(jnp.float32), 0.0)
            line = jnp.sum(tail, axis=0, keepdims=True)
            row = pl.ds(chip, 1)
            loss[row, :] = line if n == 0 else loss[row, :] + line

        def use(k, tile):
            total[ids[start + k]] += lax.dot_general(
                tile,
                q[own[start + k], 0:BLK, :],
                (((0,), (0,)), ((), ())),
                preferred_element_type=jnp.float32,
            )

        for_pairs(spots, wv, use)

    @pl.loop(0, 16)
    def _(n):
        for m, (first, size) in enumerate(PIECES):
            for e in range(size // 16):
                outs[m][16 * e + n] = total[first + 16 * e + n].astype(jnp.bfloat16)

    loss[...] = pltpu.roll(loss[...], (128 - 8 * (at[3] % 16)) % 128, 1)


def grad_passages(ids, own, at, q, parts):
    shapes = [jax.ShapeDtypeStruct((size, BLK, 128), jnp.bfloat16) for _, size in PIECES]
    return pl.pallas_call(
        grad_p_kernel,
        in_specs=[SMEM] * 3 + [VMEM] * 9,
        out_specs=[VMEM] * 8,
        out_shape=shapes + [jax.ShapeDtypeStruct((BLK // 8, 128), jnp.float32)],
        scratch_shapes=[
            pltpu.VMEM((STEP // 2, BLK // 8, 16, 128), jnp.bfloat16),
            pltpu.VMEM((PAIRS, BLK, 128), jnp.float32),
        ],
        **params(20, 20 * MIB),
        name="grad_passages",
    )(ids, own, at, q, *parts)


def grad_q_kernel(ids, own, at, p, *refs):
    parts, out, wv, total = refs[:8], *refs[8:]
    clear(total)
    for n in range(2):
        start, spots = weight_spots(at, n, parts)

        def use(k, tile):
            total[own[start + k]] += jnp.dot(
                tile, p[ids[start + k]], preferred_element_type=jnp.float32
            )

        for_pairs(spots, wv, use)

    @pl.loop(0, total.shape[0] // 4)
    def _(n):
        for m in range(4):
            out[4 * n + m] = total[4 * n + m].astype(jnp.bfloat16)


def grad_queries(ids, own, at, p, parts):
    nblk = p.shape[0] // 4
    return pl.pallas_call(
        grad_q_kernel,
        in_specs=[SMEM] * 3 + [VMEM] * 9,
        out_specs=VMEM,
        out_shape=jax.ShapeDtypeStruct((nblk, BLK, 128), jnp.bfloat16),
        scratch_shapes=[
            pltpu.VMEM((STEP // 2, BLK // 8, 16, 128), jnp.bfloat16),
            pltpu.VMEM((nblk, BLK, 128), jnp.float32),
        ],
        **params(14, 20 * MIB),
        name="grad_queries",
    )(ids, own, at, p, *parts)


def join_kernel(kept, *refs):
    terms, out, outv, sems = refs[:4], *refs[4:]
    half = kept.shape[0] // 2
    copies = []
    for h in range(2):
        part = slice(half * h, half * h + half)

        @pl.loop(0, half // 4)
        def _(n):
            for e in range(4):
                value = kept[half * h + 4 * n + e].astype(jnp.float32)
                for m in (2 * h, 2 * h + 1):
                    value = value + terms[m][4 * n + e].astype(jnp.float32)
                outv[half * h + 4 * n + e] = value.astype(outv.dtype)

        copies.append(pltpu.make_async_copy(outv.at[part], out.at[part], sems.at[h]))
        copies[h].start()
    for copy in copies:
        copy.wait()


def join(kept, low, high):
    return pl.pallas_call(
        join_kernel,
        in_specs=[VMEM] * 5,
        out_specs=ANY,
        out_shape=jax.ShapeDtypeStruct(kept.shape, kept.dtype),
        scratch_shapes=[pltpu.VMEM(kept.shape, kept.dtype), pltpu.SemaphoreType.DMA((2,))],
        **params(6, 8 * MIB),
        name="join",
    )(kept, *low, *high)


def along(axis, delta):
    if axis == "z":
        number = lax.axis_size("grp")
        perm = [(i, (i + delta) % number) for i in range(number)]
        return lambda v: lax.ppermute(v, "grp", perm)

    def target(d):
        x, y, core = d // 8, d // 2 % 4, d % 2
        if axis == "core":
            core = 1 - core
        elif (axis == "first") == (core == 0):
            x = (x + delta) % 4
        else:
            y = (y + delta) % 4
        return x * 8 + y * 2 + core

    perm = [(d, target(d)) for d in range(32)]
    return lambda v: lax.ppermute(v, "dev", perm)


def add(*terms):
    total = terms[0].astype(jnp.float32)
    for term in terms[1:]:
        total = total + term.astype(jnp.float32)
    return total.astype(terms[0].dtype)


def ring_terms(axis, rel1, rel2, rel3):
    up, down = along(axis, 1), along(axis, -1)
    from_below = up(rel2[0])
    from_above = down(rel2[1])
    below1 = up(rel1[1])
    above0 = down(rel3[0])
    below0 = up(add(rel1[0], from_below))
    above1 = down(add(rel3[1], from_above))
    return (below0, above0), (below1, above1)


def scatter_scores(outs):
    halves = ring_terms("first", outs[0:2], outs[2:4], outs[4:6])
    sums = [outs[6][n] + halves[n // 2][0][n % 2] + halves[n // 2][1][n % 2] for n in range(4)]
    got = [along("second", n)(sums[n]) for n in (2, 3, 1)]
    return sums[0] + got[0] + got[1] + got[2]


def gather_weights(v):
    got = {2: along("first", 2)(v), 1: along("first", -1)(v), 3: along("first", 1)(v)}
    near = jnp.stack([v, got[1], got[2], got[3]])
    up, down, flip = along("second", 1), along("second", -1), along("core", 1)
    below, above = up(near), down(near)
    side = [near, below, above, down(above)]
    return side + [flip(w) for w in side]


def per_device(queries, passages, pairs, counts, positives):
    ndev = lax.axis_size("dev")
    ngrp = lax.axis_size("grp")
    width = queries.shape[1]
    maxp = pairs.shape[1]
    me = lax.axis_index("dev")
    z = lax.axis_index("grp")
    chip, core = me // 2, me % 2
    at = jnp.stack([core, chip // 4, chip % 4, me, chip]).astype(jnp.int32)

    def exchange(v):
        return lax.all_to_all(v, "dev", 0, 0, tiled=True)

    up, down, flip = along("z", 1), along("z", -1), along("core", 1)
    low, high = [exchange(v) for v in by_features(passages)]
    above0, below0 = down(low), up(low)
    q_tiles = by_features(queries, positives.reshape(1, BLK))[0]
    q_tiles, late, *_ = lax.optimization_barrier((q_tiles, high, above0, below0))
    above1, below1 = down(late), up(late)
    last0, last1, *_ = lax.optimization_barrier((above0, below1, above1))
    far0, far1 = down(last0), up(last1)
    pieces = [low, high, above0, above1, far0, far1, below0, below1]
    others = [flip(v) for v in pieces]
    q_own = exchange(q_tiles)
    q = [q_own, flip(q_own)]

    group = counts[0]
    block = jnp.arange(ndev, dtype=jnp.int32)
    ends = jnp.sum(jnp.where(block[None, :] <= block[:, None], group[None, :], 0), axis=1)
    starts = ends - group
    t = jnp.arange(PAIRS, dtype=jnp.int32)
    own = jnp.sum((ends[None, :] <= t[:, None]).astype(jnp.int32), axis=1)
    start = jnp.sum(jnp.where(block[None, :] == own[:, None], starts[None, :], 0), axis=1)
    entry = own * maxp + t - start
    slot = jnp.arange(ndev * maxp, dtype=jnp.int32)
    ids = jnp.sum(jnp.where(slot[None, :] == entry[:, None], pairs.reshape(1, -1), 0), axis=1)
    ids = (ids + (ngrp - z) * ndev) % (ngrp * ndev)
    spare = jnp.full((128 - ndev,), 2 * PAIRS, jnp.int32)
    lists = jnp.stack([jnp.concatenate([v, spare]) for v in (ends, starts)] * 4)

    scores = scatter_scores(partial_scores(ids, own, at, q, pieces + others))
    weights = softmax_weights(at, (scores, flip(scores)), lists, q_own, width ** (-0.5))
    parts = gather_weights(weights)
    q_own, mine = lax.optimization_barrier((q_own, place(pieces)))
    *g, lines = grad_passages(ids, own, at, q_own, parts)

    low, high = ring_terms("z", g[1:3], g[3:5], g[5:7])
    q_rows = by_rows(exchange(grad_queries(ids, own, at, mine, parts)))
    p_rows = by_rows(exchange(join(g[0], low, high)))
    return lines[:, 0:8].reshape(BLK), q_rows, p_rows


def solution(mesh):
    placed = (
        P(("grp", "dev"), None),
        P(("grp", "dev"), None),
        P("grp", None),
        P("grp", None),
        P(("grp", "dev")),
    )
    return jax.shard_map(
        per_device,
        mesh=mesh,
        in_specs=placed,
        out_specs=(P(("grp", "dev")), P(("grp", "dev"), None), P(("grp", "dev"), None)),
        check_vma=False,
    )
```

```python
import functools

import jax
import jax.numpy as jnp
from jax import lax
from jax.experimental import pallas as pl
from jax.experimental.pallas import tpu as pltpu
from jax.sharding import PartitionSpec as P

BLK = 128
HALF = BLK // 2
PAIRS = 128
PART = PAIRS // 2
ROWS = 8 * PART
TAIL = 16
STEP = 8
PARTS = 8
MIB = 1024 * 1024
SMEM = pl.BlockSpec(memory_space=pltpu.SMEM)
ANY = pl.BlockSpec(memory_space=pl.ANY)
VMEM = pl.BlockSpec(memory_space=pltpu.VMEM)


def params(limit, moved, flops=0):
    cost = pl.CostEstimate(flops=flops, bytes_accessed=moved, transcendentals=0)
    limit = pltpu.CompilerParams(vmem_limit_bytes=limit * MIB)
    return dict(compiler_params=limit, cost_estimate=cost)


def run_copies(copies):
    for copy in copies:
        copy.start()
    for copy in copies:
        copy.wait()


def pack_kernel(x, *refs):
    *outs, xv, outv, marks, sems = refs
    extra = outv.shape[1] - BLK
    if extra:
        run_copies([pltpu.make_async_copy(outs[0], marks, sems.at[0])])
        outs = outs[1:]
        tile = jnp.broadcast_to(marks[...].astype(jnp.float32), (extra, 128)).astype(jnp.bfloat16)
    width = x.shape[1]
    number = outv.shape[0] // PARTS
    tall = outv.shape[1] // len(outs)
    loads, stores = [], []
    for n in range(PARTS):
        cols = slice(n * width // PARTS, (n + 1) * width // PARTS)
        loads.append(pltpu.make_async_copy(x.at[:, cols], xv.at[:, cols], sems.at[n]))
        part = slice(n * number, (n + 1) * number)
        for m, out in enumerate(outs):
            source = outv.at[part, m * tall : (m + 1) * tall, :]
            sem = sems.at[PARTS * (1 + m) + n]
            stores.append(pltpu.make_async_copy(source, out.at[part], sem))
    for copy in loads:
        copy.start()
    for n in range(PARTS):
        loads[n].wait()
        for m in range(n * number, (n + 1) * number):
            outv[m, 0:BLK, :] = xv[:, 128 * m : 128 * m + 128].astype(jnp.bfloat16)
            if extra:
                outv[m, BLK:, :] = tile
        for copy in stores[n * len(outs) : (n + 1) * len(outs)]:
            copy.start()
    for copy in stores:
        copy.wait()


def by_features(x, pos=None):
    number = x.shape[1] // 128
    tall = BLK + (0 if pos is None else 16)
    shapes = [(number, HALF, 128)] * 2 if pos is None else [(number, tall, 128)]
    given = (x,) if pos is None else (x, pos)
    return pl.pallas_call(
        pack_kernel,
        in_specs=[ANY] * len(given),
        out_specs=[ANY] * len(shapes),
        out_shape=[jax.ShapeDtypeStruct(s, jnp.bfloat16) for s in shapes],
        scratch_shapes=[
            pltpu.VMEM(x.shape, x.dtype),
            pltpu.VMEM((number, tall, 128), jnp.bfloat16),
            pltpu.VMEM((1, BLK), jnp.int32),
            pltpu.SemaphoreType.DMA((3 * PARTS,)),
        ],
        **params(56 if pos is None else 5, 5 * MIB),
        name="pack",
    )(*given)


def unpack_kernel(x, out, outv, sems):
    copies = []
    for n in range(PARTS):
        rows = slice(n * BLK // PARTS, (n + 1) * BLK // PARTS)
        for m in range(x.shape[0]):
            outv[rows, 128 * m : 128 * m + 128] = x[m, rows, :].astype(jnp.float32)
        copies.append(pltpu.make_async_copy(outv.at[rows, :], out.at[rows, :], sems.at[n]))
        copies[n].start()
    for copy in copies:
        copy.wait()


def by_rows(x):
    number = x.shape[0]
    return pl.pallas_call(
        unpack_kernel,
        in_specs=[VMEM],
        out_specs=ANY,
        out_shape=jax.ShapeDtypeStruct((BLK, number * 128), jnp.float32),
        scratch_shapes=[
            pltpu.VMEM((BLK, number * 128), jnp.float32),
            pltpu.SemaphoreType.DMA((PARTS,)),
        ],
        **params(5, 8 * MIB),
        name="unpack",
    )(x)


PIECES = ((0, 32), (32, 16), (48, 16), (64, 16), (80, 16), (96, 16), (112, 16))


def place_kernel(*refs):
    *pieces, out, sems = refs
    copies = []
    for n, piece in enumerate(pieces):
        target = out.at[32 * (n // 2) : 32 * (n // 2) + 32, HALF * (n % 2) : HALF * (n % 2) + HALF, :]
        copies.append(pltpu.make_async_copy(piece, target, sems.at[n]))
    run_copies(copies)


def place(pieces):
    return pl.pallas_call(
        place_kernel,
        in_specs=[ANY] * 8,
        out_specs=ANY,
        out_shape=jax.ShapeDtypeStruct((4 * 32, BLK, 128), pieces[0].dtype),
        scratch_shapes=[pltpu.SemaphoreType.DMA((8,))],
        **params(1, 12 * MIB),
        name="place",
    )(*pieces)


def chip_at(at, core, lead, other):
    rx = jnp.where(core == 0, lead, other)
    ry = jnp.where(core == 0, other, lead)
    return ((at[1] + rx) % 4) * 4 + (at[2] + ry) % 4


def score_kernel(ids, own, at, q_own, q_sib, *refs):
    pieces, outs, (pv, sv) = (refs[:8], refs[8:16]), refs[16:23], refs[23:]
    core = at[0]
    spots = [
        (lead, other, chip_at(at, core, lead, other)) for lead in range(4) for other in range(4)
    ]

    @pl.loop(0, PART // STEP)
    def _(step):
        for u in range(STEP):
            there = ids[PART * core + step * STEP + u]
            for rel in range(4):

                @pl.when(there // 32 == rel)
                def _():
                    for side in range(2):
                        for h in range(2):
                            rows = slice(HALF * h, HALF * h + HALF)
                            lanes = slice(128 * side, 128 * side + 128)
                            pv[u, rows, lanes] = pieces[side][2 * rel + h][there % 32]

        for u in range(STEP):
            here = own[PART * core + step * STEP + u]
            left = jnp.concatenate([q_own[here, 0:BLK, :], q_sib[here, 0:BLK, :]], axis=1)
            tile = lax.dot_general(
                left, pv[u], (((1,), (1,)), ((), ())), preferred_element_type=jnp.float32
            )
            sv[u] = tile.reshape(BLK // 8, 8, 128)
        for u in range(STEP):
            where = pl.ds(pl.multiple_of(8 * (step * STEP + u), 8), 8)
            for lead, other, chip in spots:
                if lead == 0:
                    outs[6][other, where, :] = sv[u, chip]
                else:
                    outs[2 * lead - 2 + other // 2][other % 2, where, :] = sv[u, chip]


def partial_scores(ids, own, at, q, pieces):
    shapes = [(2, ROWS, 128)] * 6 + [(4, ROWS, 128)]
    return pl.pallas_call(
        score_kernel,
        in_specs=[SMEM] * 3 + [VMEM] * 18,
        out_specs=[VMEM] * 7,
        out_shape=[jax.ShapeDtypeStruct(s, jnp.float32) for s in shapes],
        scratch_shapes=[
            pltpu.VMEM((STEP, BLK, 2 * 128), jnp.bfloat16),
            pltpu.VMEM((STEP, BLK // 8, 8, 128), jnp.float32),
        ],
        **params(18, 20 * MIB),
        name="partial_scores",
    )(ids, own, at, *q, *pieces)


def softmax_kernel(at, x_own, x_sib, listv, q, out, *, scale):
    core = at[0]
    row = lax.broadcasted_iota(jnp.int32, (2 * ROWS, 1), 0)
    side = row // ROWS
    t = PART * (core + side - 2 * core * side) + (row & (ROWS - 1)) // 8
    r = row & 7
    lane = lax.broadcasted_iota(jnp.int32, (2 * ROWS, 128), 1)
    own = jnp.sum((listv[0:1, :] <= t).astype(jnp.int32), axis=1, keepdims=True)
    key = own * 8 + r

    x = jnp.concatenate([x_own[...], x_sib[...]], axis=0) * scale
    high = jnp.max(x, axis=1, keepdims=True)
    part = jnp.sum(jnp.exp(x - high), axis=1, keepdims=True)
    lines = jnp.where(lane == 0, high, jnp.where(lane == 1, part, key.astype(jnp.float32))).T
    high, part, keys = lines[0:1], lines[1:2], lines[2:3]

    x, t, r, lane, own, key = [v[:ROWS] for v in (x, t, r, lane, own, key)]
    same = key.astype(jnp.float32) == keys
    top = jnp.max(jnp.where(same, high, -jnp.inf), axis=1, keepdims=True)
    total = jnp.where(same, part * jnp.exp(high - top), 0.0)
    lse = top + jnp.log(jnp.sum(total, axis=1, keepdims=True))

    block = lane == own
    first = t == jnp.sum(jnp.where(block, listv[1:2, :], 0), axis=1, keepdims=True)
    marks = jnp.max(q[:, BLK:, :].astype(jnp.float32), axis=1)
    marks = jnp.concatenate([marks, jnp.zeros((128 - marks.shape[0], 128), jnp.float32)], axis=0)
    listed = jnp.dot(
        block.astype(jnp.bfloat16), marks.astype(jnp.bfloat16), preferred_element_type=jnp.float32
    )
    target = jnp.sum(jnp.where(lane == at[4] * 8 + r, listed, 0.0), axis=1, keepdims=True)
    hit = first & (lane == target.astype(jnp.int32))
    weights = jnp.exp(x - lse) - hit.astype(jnp.float32)
    out[0:ROWS, :] = weights.astype(jnp.bfloat16)

    loss = lse - jnp.sum(jnp.where(hit, x, 0.0), axis=1, keepdims=True)
    line = lax.broadcasted_iota(jnp.int32, (TAIL, 128), 0)
    tail = jnp.zeros((TAIL, 128), jnp.float32)
    for h in range(2):
        here = first & (lane + 128 * h == key)
        rest = jnp.sum(jnp.where(here, loss, 0.0), axis=0, keepdims=True)
        for n in range(3):
            term = rest.astype(jnp.bfloat16).astype(jnp.float32)
            tail = jnp.where(line == 3 * h + n, term, tail)
            rest = rest - term
    out[ROWS:, :] = tail.astype(jnp.bfloat16)


def softmax_weights(at, terms, lists, q, scale):
    return pl.pallas_call(
        functools.partial(softmax_kernel, scale=scale),
        in_specs=[SMEM] + [VMEM] * 4,
        out_specs=VMEM,
        out_shape=jax.ShapeDtypeStruct((ROWS + TAIL, 128), jnp.bfloat16),
        **params(16, 8 * MIB),
        name="softmax_weights",
    )(at, *terms, lists, q)


GATHERED = tuple((other, (0, 1, 2, 3)) for other in (0, 3, 1, 2))


def weight_spots(at, n, parts):
    side = jnp.where(at[0] == n, 0, 1)
    spots = []
    for m, (other, leads) in enumerate(GATHERED):
        for e, lead in enumerate(leads):
            spots.append((parts[len(GATHERED) * n + m], e, chip_at(at, side, lead, other)))
    return side * PART, spots


def for_pairs(spots, wv, use):
    @pl.loop(0, PART // STEP)
    def _(step):
        for v in range(STEP // 2):
            where = pl.ds(pl.multiple_of(8 * STEP * step + 16 * v, 16), 16)
            for piece, e, chip in spots:
                wv[v, chip] = piece[e, where, :]
            two = wv[v].astype(jnp.float32)
            for o in range(2):
                tile = two[:, 8 * o : 8 * o + 8, :].reshape(BLK, 128).astype(jnp.bfloat16)
                use(step * STEP + 2 * v + o, tile)


def clear(total):
    @pl.loop(0, total.shape[0] // 4)
    def _(n):
        for m in range(4):
            total[4 * n + m] = jnp.zeros((BLK, 128), jnp.float32)


def grad_p_kernel(ids, own, at, q, *refs):
    parts, outs, loss, wv, total = refs[:8], refs[8:15], *refs[15:]
    clear(total)
    mine = lax.broadcasted_iota(jnp.int32, (TAIL, 128), 0) // 3 == at[3] // 16
    for n in range(2):
        start, spots = weight_spots(at, n, parts)
        for piece, e, chip in spots:
            tail = jnp.where(mine, piece[e, ROWS:, :].astype(jnp.float32), 0.0)
            line = jnp.sum(tail, axis=0, keepdims=True)
            row = pl.ds(chip, 1)
            loss[row, :] = line if n == 0 else loss[row, :] + line

        def use(k, tile):
            total[ids[start + k]] += lax.dot_general(
                tile,
                q[own[start + k], 0:BLK, :],
                (((0,), (0,)), ((), ())),
                preferred_element_type=jnp.float32,
            )

        for_pairs(spots, wv, use)

    @pl.loop(0, 16)
    def _(n):
        for m, (first, size) in enumerate(PIECES):
            for e in range(size // 16):
                outs[m][16 * e + n] = total[first + 16 * e + n].astype(jnp.bfloat16)

    loss[...] = pltpu.roll(loss[...], (128 - 8 * (at[3] % 16)) % 128, 1)


def grad_passages(ids, own, at, q, parts):
    shapes = [jax.ShapeDtypeStruct((size, BLK, 128), jnp.bfloat16) for _, size in PIECES]
    return pl.pallas_call(
        grad_p_kernel,
        in_specs=[SMEM] * 3 + [VMEM] * 9,
        out_specs=[VMEM] * 8,
        out_shape=shapes + [jax.ShapeDtypeStruct((BLK // 8, 128), jnp.float32)],
        scratch_shapes=[
            pltpu.VMEM((STEP // 2, BLK // 8, 16, 128), jnp.bfloat16),
            pltpu.VMEM((PAIRS, BLK, 128), jnp.float32),
        ],
        **params(20, 20 * MIB),
        name="grad_passages",
    )(ids, own, at, q, *parts)


def grad_q_kernel(ids, own, at, p, *refs):
    parts, out, wv, total = refs[:8], *refs[8:]
    clear(total)
    for n in range(2):
        start, spots = weight_spots(at, n, parts)

        def use(k, tile):
            total[own[start + k]] += jnp.dot(
                tile, p[ids[start + k]], preferred_element_type=jnp.float32
            )

        for_pairs(spots, wv, use)

    @pl.loop(0, total.shape[0] // 4)
    def _(n):
        for m in range(4):
            out[4 * n + m] = total[4 * n + m].astype(jnp.bfloat16)


def grad_queries(ids, own, at, p, parts):
    nblk = p.shape[0] // 4
    return pl.pallas_call(
        grad_q_kernel,
        in_specs=[SMEM] * 3 + [VMEM] * 9,
        out_specs=VMEM,
        out_shape=jax.ShapeDtypeStruct((nblk, BLK, 128), jnp.bfloat16),
        scratch_shapes=[
            pltpu.VMEM((STEP // 2, BLK // 8, 16, 128), jnp.bfloat16),
            pltpu.VMEM((nblk, BLK, 128), jnp.float32),
        ],
        **params(14, 20 * MIB),
        name="grad_queries",
    )(ids, own, at, p, *parts)


def join_kernel(kept, *refs):
    terms, out, outv, sems = refs[:4], *refs[4:]
    half = kept.shape[0] // 2
    copies = []
    for h in range(2):
        part = slice(half * h, half * h + half)

        @pl.loop(0, half // 4)
        def _(n):
            for e in range(4):
                value = kept[half * h + 4 * n + e].astype(jnp.float32)
                for m in (2 * h, 2 * h + 1):
                    value = value + terms[m][4 * n + e].astype(jnp.float32)
                outv[half * h + 4 * n + e] = value.astype(outv.dtype)

        copies.append(pltpu.make_async_copy(outv.at[part], out.at[part], sems.at[h]))
        copies[h].start()
    for copy in copies:
        copy.wait()


def join(kept, low, high):
    return pl.pallas_call(
        join_kernel,
        in_specs=[VMEM] * 5,
        out_specs=ANY,
        out_shape=jax.ShapeDtypeStruct(kept.shape, kept.dtype),
        scratch_shapes=[pltpu.VMEM(kept.shape, kept.dtype), pltpu.SemaphoreType.DMA((2,))],
        **params(6, 8 * MIB),
        name="join",
    )(kept, *low, *high)


def along(axis, delta):
    if axis == "z":
        number = lax.axis_size("grp")
        perm = [(i, (i + delta) % number) for i in range(number)]
        return lambda v: lax.ppermute(v, "grp", perm)

    def target(d):
        x, y, core = d // 8, d // 2 % 4, d % 2
        if axis == "core":
            core = 1 - core
        elif (axis == "first") == (core == 0):
            x = (x + delta) % 4
        else:
            y = (y + delta) % 4
        return x * 8 + y * 2 + core

    perm = [(d, target(d)) for d in range(32)]
    return lambda v: lax.ppermute(v, "dev", perm)


def add(*terms):
    total = terms[0].astype(jnp.float32)
    for term in terms[1:]:
        total = total + term.astype(jnp.float32)
    return total.astype(terms[0].dtype)


def ring_terms(axis, rel1, rel2, rel3):
    up, down = along(axis, 1), along(axis, -1)
    from_below = up(rel2[0])
    from_above = down(rel2[1])
    below1 = up(rel1[1])
    above0 = down(rel3[0])
    below0 = up(add(rel1[0], from_below))
    above1 = down(add(rel3[1], from_above))
    return (below0, above0), (below1, above1)


def scatter_scores(outs):
    halves = ring_terms("first", outs[0:2], outs[2:4], outs[4:6])
    sums = [outs[6][n] + halves[n // 2][0][n % 2] + halves[n // 2][1][n % 2] for n in range(4)]
    got = [along("second", n)(sums[n]) for n in (2, 3, 1)]
    return sums[0] + got[0] + got[1] + got[2]


def gather_weights(v):
    got = {2: along("first", 2)(v), 1: along("first", -1)(v), 3: along("first", 1)(v)}
    near = jnp.stack([v, got[1], got[2], got[3]])
    up, down, flip = along("second", 1), along("second", -1), along("core", 1)
    below, above = up(near), down(near)
    side = [near, below, above, down(above)]
    return side + [flip(w) for w in side]


def per_device(queries, passages, pairs, counts, positives):
    ndev = lax.axis_size("dev")
    ngrp = lax.axis_size("grp")
    width = queries.shape[1]
    maxp = pairs.shape[1]
    me = lax.axis_index("dev")
    z = lax.axis_index("grp")
    chip, core = me // 2, me % 2
    at = jnp.stack([core, chip // 4, chip % 4, me, chip]).astype(jnp.int32)

    def exchange(v):
        return lax.all_to_all(v, "dev", 0, 0, tiled=True)

    up, down, flip = along("z", 1), along("z", -1), along("core", 1)
    low, high = [exchange(v) for v in by_features(passages)]
    below0, above0 = up(low), down(low)
    q_tiles = by_features(queries, positives.reshape(1, BLK))[0]
    q_tiles, late, *_ = lax.optimization_barrier((q_tiles, high, above0, below0))
    below1, above1 = up(late), down(late)
    last0, last1, *_ = lax.optimization_barrier((above0, below1, above1))
    far0, far1 = down(last0), up(last1)
    pieces = [low, high, above0, above1, far0, far1, below0, below1]
    others = [flip(v) for v in pieces]
    q_own = exchange(q_tiles)
    q = [q_own, flip(q_own)]

    group = counts[0]
    block = jnp.arange(ndev, dtype=jnp.int32)
    ends = jnp.sum(jnp.where(block[None, :] <= block[:, None], group[None, :], 0), axis=1)
    starts = ends - group
    t = jnp.arange(PAIRS, dtype=jnp.int32)
    own = jnp.sum((ends[None, :] <= t[:, None]).astype(jnp.int32), axis=1)
    start = jnp.sum(jnp.where(block[None, :] == own[:, None], starts[None, :], 0), axis=1)
    entry = own * maxp + t - start
    slot = jnp.arange(ndev * maxp, dtype=jnp.int32)
    ids = jnp.sum(jnp.where(slot[None, :] == entry[:, None], pairs.reshape(1, -1), 0), axis=1)
    ids = (ids + (ngrp - z) * ndev) % (ngrp * ndev)
    spare = jnp.full((128 - ndev,), 2 * PAIRS, jnp.int32)
    lists = jnp.stack([jnp.concatenate([v, spare]) for v in (ends, starts)] * 4)

    scores = scatter_scores(partial_scores(ids, own, at, q, pieces + others))
    weights = softmax_weights(at, (scores, flip(scores)), lists, q_own, width ** (-0.5))
    parts = gather_weights(weights)
    q_own, mine = lax.optimization_barrier((q_own, place(pieces)))
    *g, lines = grad_passages(ids, own, at, q_own, parts)

    low, high = ring_terms("z", g[1:3], g[3:5], g[5:7])
    q_rows = by_rows(exchange(grad_queries(ids, own, at, mine, parts)))
    p_rows = by_rows(exchange(join(g[0], low, high)))
    return lines[:, 0:8].reshape(BLK), q_rows, p_rows


def solution(mesh):
    placed = (
        P(("grp", "dev"), None),
        P(("grp", "dev"), None),
        P("grp", None),
        P("grp", None),
        P(("grp", "dev")),
    )
    return jax.shard_map(
        per_device,
        mesh=mesh,
        in_specs=placed,
        out_specs=(P(("grp", "dev")), P(("grp", "dev"), None), P(("grp", "dev"), None)),
        check_vma=False,
    )
```
